512 devices in a mesh: ep: 128 (over z, y, core), edp: 4 (over x).
Axes of the slice: x: 4, y: 8, z: 8, core: 2. Of those that a mesh axis runs over, the one named last changes fastest.
Arguments:
- tokens: bfloat16 [12288, 2048], P(('ep', 'edp')), may hold values from -6 to 6
- out_grad: bfloat16 [12288, 2048], P(('ep', 'edp')), may hold values from -6 to 6
- expert_ids: int32 [12288, 8], P(('ep', 'edp')), may hold values from 0 to 127, all different within a row; in each aligned block of 24 rows (0 to 23, 24 to 47, ...) at most 2 rows name the same one
- gate_values: float32 [12288, 8], P(('ep', 'edp')), may hold values from 0.02 to 0.3
- gate_up_weight: bfloat16 [128, 2048, 1536], P('ep', 'edp'), may hold values from -0.125 to 0.125
- down_weight: bfloat16 [128, 768, 2048], P('ep', None, 'edp'), may hold values from -0.21875 to 0.21875
Outputs:
- token_grads: bfloat16 [12288, 2048], P(('ep', 'edp'))
- down_grad: bfloat16 [128, 768, 2048], P('ep', None, 'edp')
The draws below stay inside these ranges and needn't reach their ends.
Inputs may be any that keep to these rules, and one draw needn't show every extreme that they name: `expert_ids`: A token names 8 different experts. Among the 24 tokens of one device no expert is named by more than 2 tokens, a bound that some block reaches.
All inputs are finite; a program needn't handle non-finite values. Where the reference program divides by a largest or mean magnitude, that divisor is 1e-20 or more.
Results may differ from the reference program's by a relative error of at most 0.022.
Values may be sent and summed in bfloat16 or wider, within the bound.
No kernel may reach another device: no remote copies, remote signals or barrier semaphores. Data moves between devices by JAX's collectives and lax.ppermute only.
A program may use at most 64 MiB of HBM per device.

```python
import math
import jax
import jax.numpy as jnp
import numpy as np
from jax import lax

D = 2048
H = 768
TOP = 8
TOK_DEV = 24
EXPERTS = 128
CAP = 2
TOKENS = 12288
N_EP = 128
N_EDP = 4


def shard_levels(own_key, dims, split, least, high):
    gain = 1.0
    for axis_at, shards_of in split:
        heights = jax.random.uniform(jax.random.fold_in(jax.random.fold_in(own_key, 6), axis_at), (shards_of,), jnp.float32, least / len(split), high / len(split))
        gain = gain * jnp.repeat(jnp.exp(heights), dims[axis_at] // shards_of).reshape((-1,) + (1,) * (len(dims) - 1 - axis_at))
    return gain


def assign_block(key, own, number, rows, amount, top, bound, slope):
    ranking = jax.random.permutation(key, amount)
    packed, usual = load_shares(amount, rows * top, bound, slope, True), load_shares(amount, rows * top, bound, slope, False)
    places = jnp.arange(amount)

    def named(tallies, turn):
        used = int((tallies > 0).sum())
        fixed = max(1, used // 4)
        shifted = fixed + (places - fixed + turn * (used - fixed)) % max(1, amount - fixed)
        return jnp.zeros((amount,), jnp.int32).at[ranking[jnp.where(places < fixed, places, shifted)]].set(jnp.asarray(tallies, jnp.int32))

    tallies = jnp.where(number % 4 == 0, named(packed, number // 4), named(usual, number - number // 4 - 1))
    mixed = jax.random.permutation(jax.random.fold_in(own, 3), amount)
    giver, sink = mixed[0:amount // 2 * 2:2], mixed[1:amount // 2 * 2:2]
    room = jnp.minimum(tallies[giver] - 1, bound - tallies[sink]) // 2
    room = jnp.where((giver == ranking[0]) | (sink == ranking[0]) | (tallies[sink] == 0), 0, jnp.maximum(room, 0))
    shifted = jax.random.randint(jax.random.fold_in(own, 4), (amount // 2,), 0, 1 << 20) % (room + 1)
    tallies = tallies.at[giver].add(-shifted).at[sink].add(shifted)
    items = jnp.searchsorted(jnp.cumsum(tallies), jnp.arange(rows * top), side="right").astype(jnp.int32)
    grid = items.reshape(top, rows).T
    grid = grid[jax.random.permutation(jax.random.fold_in(own, 1), rows)]
    turn = jax.random.randint(jax.random.fold_in(own, 2), (rows, 1), 0, top)
    return jnp.take_along_axis(grid, (jnp.arange(top)[None, :] + turn) % top, axis=1)


def load_shares(count, total, limit, lean, full):
    portions = [(1 << 20) // math.isqrt(rank ** lean) + 1 for rank in range(1, count + 1)]
    largest = limit if full else min(limit, max(-(-total // count), total * portions[0] // sum(portions)))
    least = 1 if total - largest >= count - 1 else 0
    given, spare = [largest] + [least] * (count - 1), total - largest - least * (count - 1)
    while spare > 0:
        candidates = [i for i in range(1, count) if given[i] < largest] or [i for i in range(1, count) if given[i] < limit]
        pool, remaining = sum([portions[i] for i in candidates]), spare
        for i in candidates:
            addition = min(limit - given[i], max(1, remaining * portions[i] // pool), spare)
            given[i] = given[i] + addition
            spare = spare - addition
    return np.array(given)


def scatter_about(rng, extent, spread, most, cuts=(), kind=jnp.bfloat16):
    drawn = spread * jax.random.normal(rng, extent, jnp.float32)
    if cuts:
        drawn = drawn * shard_levels(rng, extent, cuts, -0.22, 0.18)
    return jnp.clip(drawn, -most, most).astype(kind)


def setup_inputs(seed: int = 0) -> dict:
    streams_of = jax.random.split(jax.random.key(seed), 7)
    tokens = scatter_about(streams_of[0], (TOKENS, D), 1.0, 6.0, ((0, 512),))
    out_grad = scatter_about(streams_of[1], (TOKENS, D), 1.0, 6.0, ((0, 512),))
    expert_ids_keys = jax.random.split(jax.random.fold_in(streams_of[2], 1), TOKENS // TOK_DEV)
    expert_ids_turns = jax.random.permutation(jax.random.fold_in(streams_of[2], 3), TOKENS // TOK_DEV)
    expert_ids = jax.vmap(lambda own, number: assign_block(jax.random.fold_in(streams_of[2], 2), own, number, TOK_DEV, EXPERTS, TOP, CAP, 2))(expert_ids_keys, expert_ids_turns).reshape((TOKENS, TOP))
    gate_values = jnp.clip(0.02 + 0.28 * jax.random.uniform(streams_of[3], (TOKENS, TOP), jnp.float32) ** shard_levels(streams_of[3], (TOKENS, TOP), ((0, 512),), -0.2, 0.2), 0.02, 0.3)
    gate_up_weight = scatter_about(streams_of[4], (EXPERTS, D, 2 * H), D ** -0.5, 0.125, ((0, 128), (1, 4)))
    down_weight = scatter_about(streams_of[5], (EXPERTS, H, D), H ** -0.5, 0.21875, ((0, 128), (2, 4)))
    return {"tokens": tokens, "out_grad": out_grad, "expert_ids": expert_ids, "gate_values": gate_values, "gate_up_weight": gate_up_weight, "down_weight": down_weight}


EPSILON = 1e-6


def quantize_rows(values):
    groups = values.reshape(values.shape[:-1] + (values.shape[-1] // 128, 128))
    scales = (jnp.max(jnp.abs(groups), axis=-1) + EPSILON).astype(jnp.bfloat16)
    quant = (groups / scales.astype(jnp.float32)[..., None]).astype(jnp.bfloat16)
    return quant.reshape(values.shape), scales


def restore_rows(quant, scales):
    groups = quant.astype(jnp.float32).reshape(scales.shape + (128,))
    restored = groups * scales.astype(jnp.float32)[..., None]
    return restored.astype(jnp.bfloat16).reshape(quant.shape)


def swiglu_backward(pre_gate, pre_up, grad_hidden):
    sigmoid = jax.nn.sigmoid(pre_gate)
    activ = pre_gate * sigmoid
    grad_gate = grad_hidden * pre_up * sigmoid * (1.0 + pre_gate * (1.0 - sigmoid))
    grad_up = grad_hidden * activ
    return jnp.concatenate([grad_gate, grad_up], axis=-1).astype(jnp.bfloat16)


def reference(tokens, out_grad, expert_ids, gate_values, gate_up_weight, down_weight):
    block_count = N_EP * N_EDP
    id_flat = expert_ids.reshape(block_count, TOK_DEV * TOP)
    onehot = (id_flat[:, :, None] == jnp.arange(EXPERTS, dtype=jnp.int32)[None, None, :]).astype(jnp.int32)
    slot_rank = jnp.sum((jnp.cumsum(onehot, axis=1) - 1) * onehot, axis=2).reshape(block_count, TOK_DEV, TOP)
    id_blocks = id_flat.reshape(block_count, TOK_DEV, TOP)
    gate_blocks = gate_values.reshape(block_count, TOK_DEV, TOP)
    token_blocks = tokens.reshape(block_count, TOK_DEV, D).astype(jnp.float32)
    grad_blocks = out_grad.reshape(block_count, TOK_DEV, D).astype(jnp.float32)
    slot_index = jnp.arange(CAP, dtype=jnp.int32)
    highest = lax.Precision.HIGHEST

    def regroup(rows):
        shaped = rows.reshape(N_EP, N_EDP, CAP, D).transpose(1, 0, 2, 3)
        return shaped.reshape(N_EDP, N_EP * CAP, D).astype(jnp.float32)

    def one_expert(carry, expert):
        hits = (id_blocks == expert)[:, None, :, :] & (slot_rank[:, None, :, :] == slot_index[None, :, None, None])
        hits = hits.astype(jnp.float32)
        picks = jnp.sum(hits, axis=3)
        weighted = jnp.sum(hits * gate_blocks[:, None, :, :], axis=3)
        sent_tokens = jnp.einsum("bct,btd->bcd", picks, token_blocks, precision=highest)
        sent_grads = jnp.einsum("bct,btd->bcd", weighted, grad_blocks, precision=highest)
        rows_x = regroup(restore_rows(*quantize_rows(sent_tokens)))
        rows_g = regroup(restore_rows(*quantize_rows(sent_grads)))
        gate_up = gate_up_weight[expert].astype(jnp.float32)
        down = down_weight[expert].astype(jnp.float32)
        pre = jnp.einsum("jsd,df->jsf", rows_x, gate_up)
        pre_gate = pre[..., :H]
        pre_up = pre[..., H:]
        hidden = lax.optimization_barrier((jax.nn.silu(pre_gate) * pre_up).astype(jnp.bfloat16)).astype(jnp.float32)
        grad_hidden = jnp.einsum("jsd,hd->jsh", rows_g, down)
        partial_value = jnp.einsum("jsh,jsd->jhd", hidden, rows_g)
        partial_value = lax.optimization_barrier(partial_value.astype(jnp.bfloat16)).astype(jnp.float32)
        down_grad = jnp.sum(partial_value, axis=0).astype(jnp.bfloat16)
        grad_pre = lax.optimization_barrier(swiglu_backward(pre_gate, pre_up, grad_hidden)).astype(jnp.float32)
        back = jnp.einsum("jsf,df->jsd", grad_pre, gate_up).astype(jnp.bfloat16).astype(jnp.float32)
        back = back.reshape(N_EDP, N_EP, CAP, D).transpose(1, 0, 2, 3).reshape(block_count, CAP, D)
        carry = carry + jnp.einsum("bct,bcd->btd", picks, back, precision=highest)
        return carry, down_grad

    start = jnp.zeros((block_count, TOK_DEV, D), jnp.float32)
    total, down_grads = lax.scan(one_expert, start, jnp.arange(EXPERTS, dtype=jnp.int32))
    return total.reshape(TOKENS, D).astype(jnp.bfloat16), down_grads
```

```python
import functools

import jax
import jax.numpy as jnp
from jax import lax
from jax.experimental import pallas as pl
from jax.experimental.pallas import tpu as pltpu
from jax.sharding import PartitionSpec as P

EPSILON = 1e-06
F32, BF16 = jnp.float32, jnp.bfloat16
NT = (((1,), (1,)), ((), ()))
TN = (((0,), (0,)), ((), ()))
VMEM_LIMIT = 56 * 1024 * 1024


def whole(memory_space=pltpu.VMEM):
    return pl.BlockSpec(memory_space=memory_space)


def send_kernel(parts, toks, me_ref, ids_ref, gate_ref, tok_ref, grad_ref, send_ref, pick_ref, stack):
    block = pl.program_id(0)
    rows = send_ref.shape[0]
    lanes = parts * toks
    feat = tok_ref.shape[1] // parts

    @pl.when(block == 0)
    def _():
        for side, ref in enumerate((tok_ref, grad_ref)):
            for k in range(parts):
                first = pl.multiple_of(lax.rem(me_ref[0] + k, parts) * feat, feat)
                stack[pl.ds((side * 2 + k // 2) * toks, toks), pl.ds((k % 2) * feat, feat)] = ref[
                    :, pl.ds(first, feat)
                ].astype(F32)

    row = lax.broadcasted_iota(jnp.int32, (rows, lanes), 0) + block * rows
    lane = lax.broadcasted_iota(jnp.int32, (rows, lanes), 1)
    expert, slot, quarter = row >> 3, (row >> 2) & 1, row & 3
    named = jnp.zeros((rows, lanes), F32)
    weight = jnp.zeros((rows, lanes), F32)
    for k in range(ids_ref.shape[0]):
        hit = ids_ref[k : k + 1, :] == expert
        named = jnp.where(hit, 1.0, named)
        weight = jnp.where(hit, gate_ref[k : k + 1, :], weight)
    above = lax.broadcasted_iota(jnp.int32, (lanes, lanes), 0)
    below = lax.broadcasted_iota(jnp.int32, (lanes, lanes), 1)
    earlier = (above < below) & (above // toks == below // toks)
    rank = jnp.dot(named.astype(BF16), earlier.astype(BF16), preferred_element_type=F32)
    chosen = (named > 0.5) & (rank == slot.astype(F32)) & (lane // toks == quarter)
    pick = jnp.where(chosen, 1.0, 0.0).astype(BF16)
    pick_ref[...] = pick
    scale_row = jnp.sum(jnp.where(chosen, weight, 0.0), axis=1, keepdims=True)
    scale_row = jnp.where(quarter[:, :1] < 2, 1.0, scale_row)
    for g in range(send_ref.shape[1] // 128):
        cols = slice(g * 128, g * 128 + 128)
        value = jnp.dot(pick, stack[:, cols].astype(BF16), preferred_element_type=F32) * scale_row
        top = jnp.max(jnp.abs(value), axis=1, keepdims=True)
        scale = (top + EPSILON).astype(BF16).astype(F32)
        quant = (value / scale).astype(BF16).astype(F32)
        send_ref[:, cols] = (quant * scale).astype(BF16)


def order_matrix(rows, parts):
    out = lax.broadcasted_iota(jnp.int32, (rows, rows), 0)
    src = lax.broadcasted_iota(jnp.int32, (rows, rows), 1)
    per = rows // parts
    return ((out % per) * parts + out // per == src).astype(BF16)


def hidden_kernel(parts, recv_ref, *refs):
    weights, (pre_ref, g_ref), downs, (x_ref, hid_ref) = refs[:7], refs[7:9], refs[9:13], refs[13:]
    rows = 256
    per = rows // parts
    order = order_matrix(rows, parts)
    width = recv_ref.shape[1]
    for b in range(recv_ref.shape[0] // rows):
        got = jnp.dot(order, recv_ref[b * rows : b * rows + rows, :], preferred_element_type=F32).astype(BF16)
        at = slice(b * per, b * per + per)
        x_ref[at, :width] = got[:per]
        x_ref[at, width:] = got[per : 2 * per]
        g_ref[at, :width] = got[2 * per : 3 * per]
        g_ref[at, width:] = got[3 * per :]
    hidden_units = pre_ref.shape[1] // 2
    tile = 256
    for n in range(pre_ref.shape[1] // tile):
        cols = slice(n * tile, n * tile + tile)
        total, at = None, 0
        for w in weights:
            depth = w.shape[0]
            term = jnp.dot(x_ref[:, at : at + depth], w[:, cols], preferred_element_type=F32)
            total, at = term if total is None else total + term, at + depth
        pre_ref[:, cols] = total
    for n in range(hidden_units // tile):
        cols = slice(n * tile, n * tile + tile)
        gate = pre_ref[:, cols]
        up = pre_ref[:, hidden_units + n * tile : hidden_units + n * tile + tile]
        hid_ref[:, cols] = (gate * jax.nn.sigmoid(gate) * up).astype(BF16)
    for k, down in enumerate(downs):
        feat = down.shape[1]
        for n in range(hidden_units // tile):
            cols = slice(n * tile, n * tile + tile)
            down[cols, :] = lax.dot_general(
                hid_ref[:, cols], g_ref[:, k * feat : k * feat + feat], TN, preferred_element_type=F32
            ).astype(BF16)


def back_kernel(parts, pre_ref, g_ref, *refs):
    ups, downs, (back_ref, gp_ref) = refs[:7], refs[7:14], refs[14:]
    hidden_units = pre_ref.shape[1] // 2
    half = hidden_units // 2
    feat = g_ref.shape[1] // parts
    gs = [g_ref[:, k * feat : k * feat + feat] for k in range(parts)]
    own, right_a, right_b, far_a, far_b, left_a, left_b = downs
    for h in range(2):
        picks = (own[h * half : h * half + half, :], (right_a, right_b)[h][...], (far_a, far_b)[h][...], (left_a, left_b)[h][...])
        total = None
        for g, w in zip(gs, picks):
            term = lax.dot_general(g, w, NT, preferred_element_type=F32)
            total = term if total is None else total + term
        cols = slice(h * half, h * half + half)
        up_cols = slice(hidden_units + h * half, hidden_units + h * half + half)
        gate, up = pre_ref[:, cols], pre_ref[:, up_cols]
        sig = jax.nn.sigmoid(gate)
        gp_ref[:, cols] = (total * up * sig * (1.0 + gate * (1.0 - sig))).astype(BF16)
        gp_ref[:, up_cols] = (total * (gate * sig)).astype(BF16)
    blocks = []
    pieces = [ups[0]], [ups[1], ups[2]], [ups[3], ups[4]], [ups[5], ups[6]]
    for group in pieces:
        outs = [lax.dot_general(gp_ref[...], w[...], NT, preferred_element_type=F32).astype(BF16) for w in group]
        blocks.append(outs[0] if len(outs) == 1 else jnp.concatenate(outs, axis=1))
    rows = 256
    per = rows // parts
    order = order_matrix(rows, parts)
    for b in range(back_ref.shape[0] // rows):
        stacked = jnp.concatenate([blk[b * per : b * per + per] for blk in blocks], axis=0)
        back_ref[b * rows : b * rows + rows, :] = lax.dot_general(
            order, stacked, TN, preferred_element_type=F32
        ).astype(BF16)


def combine_kernel(parts, toks, me_ref, pick_ref, ret_ref, out_ref):
    feat = ret_ref.shape[1]
    total = lax.dot_general(pick_ref[...], ret_ref[...], TN, preferred_element_type=F32)
    for k in range(parts):
        first = pl.multiple_of(lax.rem(me_ref[0] + k, parts) * feat, feat)
        out_ref[:, pl.ds(first, feat)] = total[k * toks : k * toks + toks].astype(BF16)


def gather_pieces(w, size):
    half = w.shape[0] // 2
    top, bottom = w[:half], w[half:]
    fwd = [(i, (i + 1) % size) for i in range(size)]
    bwd = [(i, (i - 1) % size) for i in range(size)]
    left_top = lax.ppermute(top, "edp", fwd)
    right_bottom = lax.ppermute(bottom, "edp", bwd)
    left_bottom = lax.ppermute(bottom, "edp", fwd)
    right_top = lax.ppermute(top, "edp", bwd)
    far_top = lax.ppermute(left_top, "edp", fwd)
    far_bottom = lax.ppermute(right_bottom, "edp", bwd)
    return [w, right_top, right_bottom, far_top, far_bottom, left_top, left_bottom]


def per_device(tokens, out_grad, expert_ids, gate_values, gate_up_weight, down_weight):
    experts, parts = lax.axis_size("ep"), lax.axis_size("edp")
    toks, width = tokens.shape
    hidden_units = down_weight.shape[1]
    feat = width // parts
    slots = experts * 2
    params = pltpu.CompilerParams(vmem_limit_bytes=VMEM_LIMIT)
    me = lax.axis_index("edp").astype(jnp.int32).reshape(1)
    ids = jnp.tile(expert_ids.T, (1, parts))
    gates = jnp.tile(gate_values.T, (1, parts))

    ups = gather_pieces(gate_up_weight[0], parts)
    downs = gather_pieces(down_weight[0], parts)

    rows = slots * parts
    tile = 128
    sent, pick = pl.pallas_call(
        functools.partial(send_kernel, parts, toks),
        grid=(rows // tile,),
        in_specs=[whole(pltpu.SMEM)] + [whole()] * 4,
        out_specs=[
            pl.BlockSpec((tile, width // 2), lambda b: (b, 0)),
            pl.BlockSpec((tile, parts * toks), lambda b: (b, 0)),
        ],
        out_shape=[
            jax.ShapeDtypeStruct((rows, width // 2), BF16),
            jax.ShapeDtypeStruct((rows, parts * toks), BF16),
        ],
        scratch_shapes=[pltpu.VMEM((parts * toks, width // 2), F32)],
        compiler_params=params,
        name="send_rows",
    )(me, ids, gates, tokens, out_grad)
    recv = lax.all_to_all(sent, "ep", split_axis=0, concat_axis=0, tiled=True)

    pre, rows_g, *partial = pl.pallas_call(
        functools.partial(hidden_kernel, parts),
        in_specs=[whole()] * 8,
        out_specs=[whole()] * 6,
        out_shape=[
            jax.ShapeDtypeStruct((slots, 2 * hidden_units), F32),
            jax.ShapeDtypeStruct((slots, width), BF16),
        ]
        + [jax.ShapeDtypeStruct((hidden_units, feat), BF16)] * parts,
        scratch_shapes=[pltpu.VMEM((slots, width), BF16), pltpu.VMEM((slots, hidden_units), BF16)],
        compiler_params=params,
        name="hidden_rows",
    )(recv, *ups)

    sums = partial[0].astype(F32)
    for k in range(1, parts):
        perm = [(i, (i + k) % parts) for i in range(parts)]
        sums = sums + lax.ppermute(partial[k], "edp", perm).astype(F32)
    down_grad = sums.astype(BF16)[None]

    back = pl.pallas_call(
        functools.partial(back_kernel, parts),
        in_specs=[whole()] * 16,
        out_specs=whole(),
        out_shape=jax.ShapeDtypeStruct((rows, feat), BF16),
        scratch_shapes=[pltpu.VMEM((slots, 2 * hidden_units), BF16)],
        compiler_params=params,
        name="back_rows",
    )(pre, rows_g, *ups, *downs)
    returned = lax.all_to_all(back, "ep", split_axis=0, concat_axis=0, tiled=True)
    token_grads = pl.pallas_call(
        functools.partial(combine_kernel, parts, toks),
        in_specs=[whole(pltpu.SMEM), whole(), whole()],
        out_specs=whole(),
        out_shape=jax.ShapeDtypeStruct((toks, width), BF16),
        compiler_params=params,
        name="combine_rows",
    )(me, pick, returned)
    return (token_grads, down_grad)


def solution(mesh):
    return jax.shard_map(
        per_device,
        mesh=mesh,
        in_specs=(
            P(("ep", "edp"), None),
            P(("ep", "edp"), None),
            P(("ep", "edp"), None),
            P(("ep", "edp"), None),
            P("ep", "edp", None),
            P("ep", None, "edp"),
        ),
        out_specs=(P(("ep", "edp"), None), P("ep", None, "edp")),
        check_vma=False,
    )
```

```python
import functools

import jax
import jax.numpy as jnp
from jax import lax
from jax.experimental import pallas as pl
from jax.experimental.pallas import tpu as pltpu
from jax.sharding import PartitionSpec as P

EPSILON = 1e-06
F32, BF16 = jnp.float32, jnp.bfloat16
NT = (((1,), (1,)), ((), ()))
TN = (((0,), (0,)), ((), ()))
VMEM_LIMIT = 56 * 1024 * 1024


def whole(memory_space=pltpu.VMEM):
    return pl.BlockSpec(memory_space=memory_space)


def quantize(value):
    top = jnp.max(jnp.abs(value), axis=1, keepdims=True)
    scale = (top + EPSILON).astype(BF16).astype(F32)
    return ((value / scale).astype(BF16).astype(F32) * scale).astype(BF16)


def send_kernel(quarters, ids_ref, gate_ref, tok_ref, grad_ref, send_ref, pick_ref, stack):
    block = pl.program_id(0)
    rows = send_ref.shape[0]
    toks, width = tok_ref.shape
    lanes = quarters * toks
    feat = width // quarters

    @pl.when(block == 0)
    def _():
        for q in range(quarters):
            here = pl.ds(q * toks, toks)
            for g in range(feat // 128):
                cols = slice(q * feat + g * 128, q * feat + g * 128 + 128)
                stack[here, pl.ds(g * 128, 128)] = quantize(tok_ref[:, cols].astype(F32)).astype(F32)
            stack[here, pl.ds(feat, feat)] = grad_ref[:, q * feat : q * feat + feat].astype(F32)

    row = lax.broadcasted_iota(jnp.int32, (rows, lanes), 0) + block * rows
    lane = lax.broadcasted_iota(jnp.int32, (rows, lanes), 1)
    expert, slot, quarter = row >> 3, (row >> 2) & 1, row & 3
    ids = jnp.concatenate([ids_ref[...]] * quarters, axis=1)
    gates = jnp.concatenate([gate_ref[...]] * quarters, axis=1)
    named = jnp.zeros((rows, lanes), F32)
    weight = jnp.zeros((rows, lanes), F32)
    for k in range(ids_ref.shape[0]):
        hit = ids[k : k + 1, :] == expert
        named = jnp.where(hit, 1.0, named)
        weight = jnp.where(hit, gates[k : k + 1, :], weight)
    above = lax.broadcasted_iota(jnp.int32, (lanes, lanes), 0)
    below = lax.broadcasted_iota(jnp.int32, (lanes, lanes), 1)
    earlier = (above < below) & (above // toks == below // toks)
    rank = jnp.dot(named.astype(BF16), earlier.astype(BF16), preferred_element_type=F32)
    chosen = (named > 0.5) & (rank == slot.astype(F32)) & (lane // toks == quarter)
    pick = jnp.where(chosen, 1.0, 0.0).astype(BF16)
    pick_ref[...] = pick
    send_ref[:, :feat] = jnp.dot(pick, stack[:, :feat].astype(BF16), preferred_element_type=F32).astype(BF16)
    gate = jnp.sum(jnp.where(chosen, weight, 0.0), axis=1, keepdims=True)
    grads = jnp.dot(pick, stack[:, feat:].astype(BF16), preferred_element_type=F32) * gate
    for g in range(feat // 128):
        cols = slice(g * 128, g * 128 + 128)
        send_ref[:, feat + g * 128 : feat + g * 128 + 128] = quantize(grads[:, cols])


def order_matrix(rows, quarters):
    out = lax.broadcasted_iota(jnp.int32, (rows, rows), 0)
    src = lax.broadcasted_iota(jnp.int32, (rows, rows), 1)
    per = rows // quarters
    return ((out % per) * quarters + out // per == src).astype(BF16)


def hidden_kernel(quarters, recv_ref, gate_w, up_w, *refs):
    to_gate_ref, to_up_ref, g_ref, down_ref, x_ref = refs[-5:]
    rows = 256
    per = rows // quarters
    feat = recv_ref.shape[1] // 2

    @pl.when(pl.program_id(0) == 0)
    def _():
        order = order_matrix(rows, quarters)
        for b in range(recv_ref.shape[0] // rows):
            block = recv_ref[b * rows : b * rows + rows, :]
            got = jnp.dot(order, block, preferred_element_type=F32).astype(BF16)
            for q in range(quarters):
                here, cols = slice(b * per, b * per + per), slice(q * feat, q * feat + feat)
                x_ref[here, cols] = got[q * per : q * per + per, :feat]
                g_ref[here, cols] = got[q * per : q * per + per, feat:]

    x = x_ref[...]
    gate = jnp.dot(x, gate_w[...], preferred_element_type=F32)
    up = jnp.dot(x, up_w[...], preferred_element_type=F32)
    sig = jax.nn.sigmoid(gate)
    activ = gate * sig
    to_gate_ref[...] = up * sig * (1.0 + gate * (1.0 - sig))
    to_up_ref[...] = activ
    hidden = (activ * up).astype(BF16)
    down_ref[...] = lax.dot_general(hidden, g_ref[...], TN, preferred_element_type=F32).astype(BF16)


def back_kernel(quarters, me_ref, to_gate_ref, to_up_ref, g_ref, *refs):
    downs, (up_ref, back_ref, gp_ref, hold) = refs[:7], refs[7:]
    step = pl.program_id(0)
    hidden_units = to_gate_ref.shape[1]
    half = hidden_units // 2
    feat = g_ref.shape[1] // quarters

    @pl.when(step == 0)
    def _():
        gs = []
        for k in range(quarters):
            first = pl.multiple_of(lax.rem(me_ref[0] + k, quarters) * feat, feat)
            gs.append(g_ref[:, pl.ds(first, feat)])
        own, right_a, right_b, far_a, far_b, left_a, left_b = downs
        for h, others in enumerate(((right_a, far_a, left_a), (right_b, far_b, left_b))):
            total = lax.dot_general(gs[0], own[h * half : h * half + half, :], NT, preferred_element_type=F32)
            for g, w in zip(gs[1:], others):
                total = total + lax.dot_general(g, w[...], NT, preferred_element_type=F32)
            cols = slice(h * half, h * half + half)
            up_cols = slice(hidden_units + h * half, hidden_units + h * half + half)
            gp_ref[:, cols] = (total * to_gate_ref[:, cols]).astype(BF16)
            gp_ref[:, up_cols] = (total * to_up_ref[:, cols]).astype(BF16)

    hold[step] = lax.dot_general(gp_ref[...], up_ref[...], NT, preferred_element_type=F32).astype(BF16)

    @pl.when(step == quarters - 1)
    def _():
        rows = 256
        per = rows // quarters
        order = order_matrix(rows, quarters)
        for b in range(back_ref.shape[0] // rows):
            stacked = jnp.concatenate([hold[q, b * per : b * per + per, :] for q in range(quarters)], axis=0)
            back_ref[b * rows : b * rows + rows, :] = lax.dot_general(
                order, stacked, TN, preferred_element_type=F32
            ).astype(BF16)


def combine_kernel(toks, pick_ref, ret_ref, out_ref):
    feat = ret_ref.shape[1]
    total = lax.dot_general(pick_ref[...], ret_ref[...], TN, preferred_element_type=F32)
    for q in range(out_ref.shape[1] // feat):
        out_ref[:, q * feat : q * feat + feat] = total[q * toks : q * toks + toks].astype(BF16)


def gather_pieces(w, size):
    half = w.shape[0] // 2
    top, bottom = w[:half], w[half:]
    fwd = [(i, (i + 1) % size) for i in range(size)]
    bwd = [(i, (i - 1) % size) for i in range(size)]
    left_top = lax.ppermute(top, "edp", fwd)
    right_bottom = lax.ppermute(bottom, "edp", bwd)
    left_bottom = lax.ppermute(bottom, "edp", fwd)
    right_top = lax.ppermute(top, "edp", bwd)
    far_top = lax.ppermute(left_top, "edp", fwd)
    far_bottom = lax.ppermute(right_bottom, "edp", bwd)
    return [w, right_top, right_bottom, far_top, far_bottom, left_top, left_bottom]


def per_device(tokens, out_grad, expert_ids, gate_values, gate_up_weight, down_weight):
    experts, parts = lax.axis_size("ep"), lax.axis_size("edp")
    toks, width = tokens.shape
    hidden_units = down_weight.shape[1]
    quarters = 4
    feat = width // quarters
    slots = experts * 2
    rows = slots * quarters
    params = pltpu.CompilerParams(vmem_limit_bytes=VMEM_LIMIT)
    me = lax.axis_index("edp").astype(jnp.int32).reshape(1)

    gate_up = lax.all_gather(gate_up_weight[0], "edp", axis=0, tiled=True)
    downs = gather_pieces(down_weight[0], parts)

    tile = 128
    sent, pick = pl.pallas_call(
        functools.partial(send_kernel, quarters),
        grid=(rows // tile,),
        in_specs=[whole()] * 4,
        out_specs=[
            pl.BlockSpec((tile, 2 * feat), lambda b: (b, 0)),
            pl.BlockSpec((tile, quarters * toks), lambda b: (b, 0)),
        ],
        out_shape=[
            jax.ShapeDtypeStruct((rows, 2 * feat), BF16),
            jax.ShapeDtypeStruct((rows, quarters * toks), BF16),
        ],
        scratch_shapes=[pltpu.VMEM((quarters * toks, 2 * feat), F32)],
        compiler_params=params,
        name="send_rows",
    )(expert_ids.T, gate_values.T, tokens, out_grad)
    recv = lax.all_to_all(sent, "ep", split_axis=0, concat_axis=0, tiled=True)

    tile = 256
    blocks = hidden_units // tile
    to_gate, to_up, rows_g, partial = pl.pallas_call(
        functools.partial(hidden_kernel, quarters),
        grid=(blocks,),
        in_specs=[
            whole(),
            pl.BlockSpec((width, tile), lambda n: (0, n)),
            pl.BlockSpec((width, tile), lambda n: (0, n + blocks)),
        ]
        + [whole(pl.ANY)] * len(downs),
        out_specs=[
            pl.BlockSpec((slots, tile), lambda n: (0, n)),
            pl.BlockSpec((slots, tile), lambda n: (0, n)),
            whole(),
            pl.BlockSpec((tile, width), lambda n: (n, 0)),
        ],
        out_shape=[
            jax.ShapeDtypeStruct((slots, hidden_units), F32),
            jax.ShapeDtypeStruct((slots, hidden_units), F32),
            jax.ShapeDtypeStruct((slots, width), BF16),
            jax.ShapeDtypeStruct((hidden_units, width), BF16),
        ],
        scratch_shapes=[pltpu.VMEM((slots, width), BF16)],
        compiler_params=params,
        name="hidden_rows",
    )(recv, gate_up, gate_up, *downs)
    down_grad = lax.psum_scatter(partial, "edp", scatter_dimension=1, tiled=True)[None]

    back = pl.pallas_call(
        functools.partial(back_kernel, quarters),
        grid=(quarters,),
        in_specs=[whole(pltpu.SMEM)] + [whole()] * 10 + [pl.BlockSpec((feat, 2 * hidden_units), lambda k: (k, 0))],
        out_specs=whole(),
        out_shape=jax.ShapeDtypeStruct((rows, feat), BF16),
        scratch_shapes=[
            pltpu.VMEM((slots, 2 * hidden_units), BF16),
            pltpu.VMEM((quarters, slots, feat), BF16),
        ],
        compiler_params=params,
        name="back_rows",
    )(me, to_gate, to_up, rows_g, *downs, gate_up)
    returned = lax.all_to_all(back, "ep", split_axis=0, concat_axis=0, tiled=True)
    token_grads = pl.pallas_call(
        functools.partial(combine_kernel, toks),
        in_specs=[whole(), whole()],
        out_specs=whole(),
        out_shape=jax.ShapeDtypeStruct((toks, width), BF16),
        compiler_params=params,
        name="combine_rows",
    )(pick, returned)
    return (token_grads, down_grad)


def solution(mesh):
    return jax.shard_map(
        per_device,
        mesh=mesh,
        in_specs=(
            P(("ep", "edp"), None),
            P(("ep", "edp"), None),
            P(("ep", "edp"), None),
            P(("ep", "edp"), None),
            P("ep", "edp", None),
            P("ep", None, "edp"),
        ),
        out_specs=(P(("ep", "edp"), None), P("ep", None, "edp")),
        check_vma=False,
    )
```

```python
import functools

import jax
import jax.numpy as jnp
from jax import lax
from jax.experimental import pallas as pl
from jax.experimental.pallas import tpu as pltpu
from jax.sharding import PartitionSpec as P

EPSILON = 1e-06
F32, BF16 = jnp.float32, jnp.bfloat16
NT = (((1,), (1,)), ((), ()))
TN = (((0,), (0,)), ((), ()))
VMEM_LIMIT = 56 * 1024 * 1024
COST = 20 * 10**9
PASS = (0,)


def whole(memory_space=pltpu.VMEM):
    return pl.BlockSpec(memory_space=memory_space)


def quantize(value):
    top = jnp.max(jnp.abs(value), axis=1, keepdims=True)
    scale = (top + EPSILON).astype(BF16).astype(F32)
    return ((value / scale).astype(BF16).astype(F32) * scale).astype(BF16)


def send_kernel(quarters, ids_ref, gate_ref, tok_ref, grad_ref, send_ref, pick_ref, stack):
    block = pl.program_id(0)
    rows = send_ref.shape[0]
    toks, width = tok_ref.shape
    lanes = quarters * toks
    feat = width // quarters

    @pl.when(block == 0)
    def _():
        for q in range(quarters):
            here = pl.ds(q * toks, toks)
            for g in range(feat // 128):
                cols = slice(q * feat + g * 128, q * feat + g * 128 + 128)
                stack[here, pl.ds(g * 128, 128)] = quantize(tok_ref[:, cols].astype(F32)).astype(F32)
            stack[here, pl.ds(feat, feat)] = grad_ref[:, q * feat : q * feat + feat].astype(F32)

    row = lax.broadcasted_iota(jnp.int32, (rows, lanes), 0) + block * rows
    lane = lax.broadcasted_iota(jnp.int32, (rows, lanes), 1)
    expert, slot, quarter = row >> 3, (row >> 2) & 1, row & 3
    ids = jnp.concatenate([ids_ref[...]] * quarters, axis=1)
    gates = jnp.concatenate([gate_ref[...]] * quarters, axis=1)
    named = jnp.zeros((rows, lanes), F32)
    weight = jnp.zeros((rows, lanes), F32)
    for k in range(ids_ref.shape[0]):
        hit = ids[k : k + 1, :] == expert
        named = jnp.where(hit, 1.0, named)
        weight = jnp.where(hit, gates[k : k + 1, :], weight)
    above = lax.broadcasted_iota(jnp.int32, (lanes, lanes), 0)
    below = lax.broadcasted_iota(jnp.int32, (lanes, lanes), 1)
    earlier = (above < below) & (above // toks == below // toks)
    rank = jnp.dot(named.astype(BF16), earlier.astype(BF16), preferred_element_type=F32)
    chosen = (named > 0.5) & (rank == slot.astype(F32)) & (lane // toks == quarter)
    pick = jnp.where(chosen, 1.0, 0.0).astype(BF16)
    pick_ref[...] = pick
    send_ref[:, :feat] = jnp.dot(pick, stack[:, :feat].astype(BF16), preferred_element_type=F32).astype(BF16)
    gate = jnp.sum(jnp.where(chosen, weight, 0.0), axis=1, keepdims=True)
    grads = jnp.dot(pick, stack[:, feat:].astype(BF16), preferred_element_type=F32) * gate
    for g in range(feat // 128):
        cols = slice(g * 128, g * 128 + 128)
        send_ref[:, feat + g * 128 : feat + g * 128 + 128] = quantize(grads[:, cols])


def order_matrix(rows, quarters):
    out = lax.broadcasted_iota(jnp.int32, (rows, rows), 0)
    src = lax.broadcasted_iota(jnp.int32, (rows, rows), 1)
    per = rows // quarters
    return ((out % per) * quarters + out // per == src).astype(BF16)


def start_all(copies, sems, first=0):
    out = []
    for n, (src, dst) in enumerate(copies):
        copy = pltpu.make_async_copy(src, dst, sems.at[first + n])
        copy.start()
        out.append(copy)
    return out


def up_rows(own, others, cols):
    feat = own.shape[0]
    half = feat // 2
    (left_a, far_a, right_a), (right_b, far_b, left_b) = others[:3], others[3:]
    out = [(own.at[:, cols], 0, feat)]
    for k, (a, b) in enumerate(((right_a, right_b), (far_a, far_b), (left_a, left_b)), 1):
        out.append((a.at[pl.ds(0, half), cols], k * feat, half))
        out.append((b.at[pl.ds(0, half), cols], k * feat + half, half))
    return out


def hidden_kernel(quarters, me_ref, recv_ref, own, *refs):
    others, refs = refs[:6], refs[6:]
    to_gate_ref, to_up_ref, g_ref, first_a, first_b, down_ref, recv, w, x_ref, sems = refs
    rows = 256
    per = rows // quarters
    feat = recv_ref.shape[1] // 2
    hidden_units = to_gate_ref.shape[1]
    tile = 256
    (got_rows,) = start_all([(recv_ref, recv)], sems)
    waits = []
    for n in range(hidden_units // tile):
        copies = []
        for at in (n * tile, hidden_units + n * tile):
            cols = pl.ds(at, tile)
            copies += [(src, w.at[pl.ds(row, size), cols]) for src, row, size in up_rows(own, others, cols)]
        waits.append(start_all(copies, sems, 1 + n * len(copies)))
    got_rows.wait()
    order = order_matrix(rows, quarters)
    for b in range(recv_ref.shape[0] // rows):
        got = jnp.dot(order, recv[b * rows : b * rows + rows, :], preferred_element_type=F32).astype(BF16)
        here = slice(b * per, b * per + per)
        for q in range(quarters):
            at = pl.multiple_of(lax.rem(q + quarters - me_ref[0], quarters) * feat, feat)
            x_ref[here, pl.ds(at, feat)] = got[q * per : q * per + per, :feat]
            g_ref[here, pl.ds(at, feat)] = got[q * per : q * per + per, feat:]
    half = hidden_units // 2
    for n in range(hidden_units // tile):
        for copy in waits[n]:
            copy.wait()
        cols = slice(n * tile, n * tile + tile)
        gate = jnp.dot(x_ref[...], w[:, cols], preferred_element_type=F32)
        up = jnp.dot(x_ref[...], w[:, hidden_units + n * tile : hidden_units + n * tile + tile], preferred_element_type=F32)
        sig = jax.nn.sigmoid(gate)
        activ = gate * sig
        to_gate_ref[:, cols] = up * sig * (1.0 + gate * (1.0 - sig))
        to_up_ref[:, cols] = activ
        hidden = (activ * up).astype(BF16)
        part = lax.dot_general(hidden, g_ref[...], TN, preferred_element_type=F32).astype(BF16)
        for k in range(quarters):
            down_ref[k, cols, :] = part[:, k * feat : k * feat + feat]
        lo, hi = n * tile, n * tile + tile
        if lo < half:
            end = min(hi, half)
            first_a[lo:end, :] = part[: end - lo, (quarters - 1) * feat :]
        if hi > half:
            start = max(lo, half)
            first_b[start - half : hi - half, :] = part[start - lo :, feat : 2 * feat]


def back_kernel(quarters, me_ref, to_gate_ref, to_up_ref, g_ref, own_down, own, *refs):
    others, refs = refs[:6], refs[6:]
    back_ref, to_gate, to_up, g, wd, w, gp_ref, hold, sems = refs
    slots, hidden_units = to_gate.shape
    feat = own.shape[0]
    half = feat // 2
    third = hidden_units // 6
    (left_a, far_a, right_a), (right_b, far_b, left_b) = others[:3], others[3:]
    copies = [(g_ref, g), (own_down, wd.at[:, pl.ds(0, feat)])]
    for k, pair in enumerate(((right_a, right_b), (far_a, far_b), (left_a, left_b)), 1):
        for h, piece in enumerate(pair):
            for m in range(3):
                src = piece.at[pl.ds(half, third), pl.ds(m * feat, feat)]
                copies.append((src, wd.at[pl.ds((h * 3 + m) * third, third), pl.ds(k * feat, feat)]))
    copies += [(to_gate_ref, to_gate), (to_up_ref, to_up)]
    early = start_all(copies, sems)
    late = start_all(
        [(src, w.at[pl.ds(row, size), :]) for src, row, size in up_rows(own, others, slice(None))], sems, len(copies)
    )
    for copy in early:
        copy.wait()
    tile = 256
    for n in range(hidden_units // tile):
        cols = slice(n * tile, n * tile + tile)
        total = lax.dot_general(g[...], wd[cols, :], NT, preferred_element_type=F32)
        gp_ref[:, cols] = (total * to_gate[:, cols]).astype(BF16)
        gp_ref[:, hidden_units + n * tile : hidden_units + n * tile + tile] = (total * to_up[:, cols]).astype(BF16)
    for k in range(quarters):
        for copy in late[:1] if k == 0 else late[2 * k - 1 : 2 * k + 1]:
            copy.wait()
        hold[lax.rem(me_ref[0] + k, quarters)] = lax.dot_general(
            gp_ref[...], w[k * feat : k * feat + feat, :], NT, preferred_element_type=F32
        ).astype(BF16)
    rows = 256
    per = rows // quarters
    order = order_matrix(rows, quarters)
    for b in range(back_ref.shape[0] // rows):
        stacked = jnp.concatenate([hold[q, b * per : b * per + per, :] for q in range(quarters)], axis=0)
        back_ref[b * rows : b * rows + rows, :] = lax.dot_general(
            order, stacked, TN, preferred_element_type=F32
        ).astype(BF16)


def combine_kernel(toks, pick_ref, ret_ref, out_ref):
    feat = ret_ref.shape[1]
    total = lax.dot_general(pick_ref[...], ret_ref[...], TN, preferred_element_type=F32)
    for q in range(out_ref.shape[1] // feat):
        out_ref[:, q * feat : q * feat + feat] = total[q * toks : q * toks + toks].astype(BF16)


def ring(size, step):
    return [(i, (i + step) % size) for i in range(size)]


def pack_kernel(up, down, a_ref, b_ref, sems):
    half, third, feat = up.shape[0] // 2, down.shape[0] // 6, down.shape[1]
    copies = []
    for h, ref in enumerate((a_ref, b_ref)):
        copies.append((up.at[pl.ds(h * half, half), :], ref.at[pl.ds(0, half), :]))
        for m in range(3):
            copies.append(
                (down.at[pl.ds((h * 3 + m) * third, third), :], ref.at[pl.ds(half, third), pl.ds(m * feat, feat)])
            )
    for copy in start_all(copies, sems):
        copy.wait()


def halves(up, down):
    shape = jax.ShapeDtypeStruct((up.shape[0] // 2 + down.shape[0] // 6, up.shape[1]), BF16)
    return pl.pallas_call(
        pack_kernel,
        in_specs=[whole(pl.ANY)] * 2,
        out_specs=[whole(pl.ANY)] * 2,
        out_shape=[shape] * 2,
        scratch_shapes=[pltpu.SemaphoreType.DMA((8,))],
        compiler_params=pltpu.CompilerParams(vmem_limit_bytes=VMEM_LIMIT),
        name="pack_weights",
    )(up, down)


def pass_on(a, b):
    return pl.pallas_call(
        lambda *refs: None,
        in_specs=[whole(pl.ANY)] * 2,
        out_specs=[whole(pl.ANY)] * 2,
        out_shape=[jax.ShapeDtypeStruct(a.shape, a.dtype)] * 2,
        input_output_aliases={0: 0, 1: 1},
        compiler_params=pltpu.CompilerParams(vmem_limit_bytes=VMEM_LIMIT),
        cost_estimate=pl.CostEstimate(flops=COST, bytes_accessed=0, transcendentals=0),
        name="pass_on",
    )(a, b)


def gather_rings(up, down, size):
    a, b = halves(up, down)
    came_a, came_b = [], []
    for step in range(size - 1):
        a, b = lax.ppermute(a, "edp", ring(size, 1)), lax.ppermute(b, "edp", ring(size, -1))
        if step in PASS:
            a, b = pass_on(a, b)
        came_a.append(a)
        came_b.append(b)
    return came_a + came_b


def scatter_rings(first_a, first_b, partial, size):
    half = partial.shape[1] // 2
    a, b = first_a, first_b
    for step in range(size - 1):
        a, b = lax.ppermute(a, "edp", ring(size, 1)), lax.ppermute(b, "edp", ring(size, -1))
        a = (a.astype(F32) + partial[(size - 2 - step) % size, :half].astype(F32)).astype(BF16)
        b = (b.astype(F32) + partial[(step + 2) % size, half:].astype(F32)).astype(BF16)
    return jnp.concatenate([a, b], axis=0)


def per_device(tokens, out_grad, expert_ids, gate_values, gate_up_weight, down_weight):
    experts, parts = lax.axis_size("ep"), lax.axis_size("edp")
    toks, width = tokens.shape
    hidden_units = down_weight.shape[1]
    quarters = 4
    feat = width // quarters
    slots = experts * 2
    rows = slots * quarters
    params = pltpu.CompilerParams(vmem_limit_bytes=VMEM_LIMIT)
    me = lax.axis_index("edp").astype(jnp.int32).reshape(1)

    others = gather_rings(gate_up_weight[0], down_weight[0], parts)

    tile = 128
    sent, pick = pl.pallas_call(
        functools.partial(send_kernel, quarters),
        grid=(rows // tile,),
        in_specs=[whole()] * 4,
        out_specs=[
            pl.BlockSpec((tile, 2 * feat), lambda b: (b, 0)),
            pl.BlockSpec((tile, quarters * toks), lambda b: (b, 0)),
        ],
        out_shape=[
            jax.ShapeDtypeStruct((rows, 2 * feat), BF16),
            jax.ShapeDtypeStruct((rows, quarters * toks), BF16),
        ],
        scratch_shapes=[pltpu.VMEM((quarters * toks, 2 * feat), F32)],
        compiler_params=params,
        name="send_rows",
    )(expert_ids.T, gate_values.T, tokens, out_grad)
    recv = lax.all_to_all(sent, "ep", split_axis=0, concat_axis=0, tiled=True)

    half = hidden_units // 2
    to_gate, to_up, rows_g, first_a, first_b, partial = pl.pallas_call(
        functools.partial(hidden_kernel, quarters),
        in_specs=[whole(pltpu.SMEM)] + [whole(pl.ANY)] * 8,
        out_specs=[whole()] * 6,
        out_shape=[
            jax.ShapeDtypeStruct((slots, hidden_units), F32),
            jax.ShapeDtypeStruct((slots, hidden_units), F32),
            jax.ShapeDtypeStruct((slots, width), BF16),
            jax.ShapeDtypeStruct((half, feat), BF16),
            jax.ShapeDtypeStruct((half, feat), BF16),
            jax.ShapeDtypeStruct((parts, hidden_units, feat), BF16),
        ],
        scratch_shapes=[
            pltpu.VMEM((rows, 2 * feat), BF16),
            pltpu.VMEM((width, 2 * hidden_units), BF16),
            pltpu.VMEM((slots, width), BF16),
            pltpu.SemaphoreType.DMA((64,)),
        ],
        compiler_params=params,
        name="hidden_rows",
    )(me, recv, gate_up_weight[0], *others)
    down_grad = scatter_rings(first_a, first_b, partial, parts)[None]

    back = pl.pallas_call(
        functools.partial(back_kernel, quarters),
        in_specs=[whole(pltpu.SMEM)] + [whole(pl.ANY)] * 11,
        out_specs=whole(),
        out_shape=jax.ShapeDtypeStruct((rows, feat), BF16),
        scratch_shapes=[
            pltpu.VMEM((slots, hidden_units), F32),
            pltpu.VMEM((slots, hidden_units), F32),
            pltpu.VMEM((slots, width), BF16),
            pltpu.VMEM((hidden_units, width), BF16),
            pltpu.VMEM((width, 2 * hidden_units), BF16),
            pltpu.VMEM((slots, 2 * hidden_units), BF16),
            pltpu.VMEM((quarters, slots, feat), BF16),
            pltpu.SemaphoreType.DMA((32,)),
        ],
        compiler_params=params,
        name="back_rows",
    )(me, to_gate, to_up, rows_g, down_weight[0], gate_up_weight[0], *others)
    returned = lax.all_to_all(back, "ep", split_axis=0, concat_axis=0, tiled=True)
    token_grads = pl.pallas_call(
        functools.partial(combine_kernel, toks),
        in_specs=[whole(), whole()],
        out_specs=whole(),
        out_shape=jax.ShapeDtypeStruct((toks, width), BF16),
        compiler_params=params,
        name="combine_rows",
    )(pick, returned)
    return (token_grads, down_grad)


def solution(mesh):
    return jax.shard_map(
        per_device,
        mesh=mesh,
        in_specs=(
            P(("ep", "edp"), None),
            P(("ep", "edp"), None),
            P(("ep", "edp"), None),
            P(("ep", "edp"), None),
            P("ep", "edp", None),
            P("ep", None, "edp"),
        ),
        out_specs=(P(("ep", "edp"), None), P("ep", None, "edp")),
        check_vma=False,
    )
```

```python
import functools

import jax
import jax.numpy as jnp
from jax import lax
from jax.experimental import pallas as pl
from jax.experimental.pallas import tpu as pltpu
from jax.sharding import PartitionSpec as P

EPSILON = 1e-06
F32, BF16 = jnp.float32, jnp.bfloat16
NT = (((1,), (1,)), ((), ()))
TN = (((0,), (0,)), ((), ()))
VMEM_LIMIT = 56 * 1024 * 1024
COST = 20 * 10**9


def whole(memory_space=pltpu.VMEM):
    return pl.BlockSpec(memory_space=memory_space)


def rebuild(value, top):
    scale = (top + EPSILON).astype(BF16).astype(F32)
    return ((value / scale).astype(BF16).astype(F32) * scale).astype(BF16)


def send_kernel(quarters, ids_ref, gate_ref, tok_ref, grad_ref, send_ref, pick_ref, stack):
    block = pl.program_id(0)
    rows = send_ref.shape[0]
    toks, width = tok_ref.shape
    lanes = quarters * toks
    feat = width // quarters

    @pl.when(block == 0)
    def _():
        for q in range(quarters):
            here = pl.ds(q * toks, toks)
            for g in range(feat // 128):
                cols = slice(q * feat + g * 128, q * feat + g * 128 + 128)
                value = tok_ref[:, cols].astype(F32)
                top = jnp.max(jnp.abs(value), axis=1, keepdims=True)
                stack[here, pl.ds(g * 128, 128)] = rebuild(value, top).astype(F32)
            grads = grad_ref[:, q * feat : q * feat + feat].astype(F32)
            stack[here, pl.ds(feat, feat)] = grads
            for g in range(feat // 128):
                top = jnp.max(jnp.abs(grads[:, g * 128 : g * 128 + 128]), axis=1, keepdims=True)
                stack[here, pl.ds(2 * feat + g * 128, 128)] = jnp.broadcast_to(top, (toks, 128))

    row = lax.broadcasted_iota(jnp.int32, (rows, lanes), 0) + block * rows
    lane = lax.broadcasted_iota(jnp.int32, (rows, lanes), 1)
    expert, slot, quarter = row >> 3, (row >> 2) & 1, row & 3
    ids = jnp.concatenate([ids_ref[...]] * quarters, axis=1)
    gates = jnp.concatenate([gate_ref[...]] * quarters, axis=1)
    named = jnp.zeros((rows, lanes), F32)
    weight = jnp.zeros((rows, lanes), F32)
    for k in range(ids_ref.shape[0]):
        hit = ids[k : k + 1, :] == expert
        named = jnp.where(hit, 1.0, named)
        weight = jnp.where(hit, gates[k : k + 1, :], weight)
    above = lax.broadcasted_iota(jnp.int32, (lanes, lanes), 0)
    below = lax.broadcasted_iota(jnp.int32, (lanes, lanes), 1)
    earlier = (above < below) & (above // toks == below // toks)
    rank = jnp.dot(named.astype(BF16), earlier.astype(BF16), preferred_element_type=F32)
    chosen = (named > 0.5) & (rank == slot.astype(F32)) & (lane // toks == quarter)
    pick = jnp.where(chosen, 1.0, 0.0).astype(BF16)
    pick_ref[...] = pick
    send_ref[:, :feat] = jnp.dot(pick, stack[:, :feat].astype(BF16), preferred_element_type=F32).astype(BF16)
    gate = jnp.sum(jnp.where(chosen, weight, 0.0), axis=1, keepdims=True)
    grads = jnp.dot(pick, stack[:, feat : 2 * feat].astype(BF16), preferred_element_type=F32) * gate
    top = jnp.dot(pick, stack[:, 2 * feat :].astype(BF16), preferred_element_type=F32) * gate
    send_ref[:, feat:] = rebuild(grads, top)


def order_matrix(rows, quarters):
    out = lax.broadcasted_iota(jnp.int32, (rows, rows), 0)
    src = lax.broadcasted_iota(jnp.int32, (rows, rows), 1)
    per = rows // quarters
    return ((out % per) * quarters + out // per == src).astype(BF16)


def start_all(copies, sems, first=0):
    out = []
    for n, (src, dst) in enumerate(copies):
        copy = pltpu.make_async_copy(src, dst, sems.at[first + n])
        copy.start()
        out.append(copy)
    return out


def pieces(own, others, axis):
    right, far_a, far_b, left = others
    rows = own.shape[0]
    step = rows if axis == 0 else 0
    half = rows // 2
    return [
        (own, 0, rows, 0),
        (right, step, rows, 1),
        (far_a, 2 * step, half, 2),
        (far_b, 2 * step + half, half, 2),
        (left, 3 * step, rows, 3),
    ]


def hidden_kernel(quarters, me_ref, recv_ref, own, *refs):
    others, refs = refs[:4], refs[4:]
    to_gate_ref, to_up_ref, g_ref, down_own, down_right, far_top, far_bottom, down_left, recv, w, x_ref, sems = refs
    rows = 256
    per = rows // quarters
    feat = recv_ref.shape[1] // 2
    hidden_units = to_gate_ref.shape[1]
    tile = 256
    (got_rows,) = start_all([(recv_ref, recv)], sems)
    waits = []
    for n in range(hidden_units // tile):
        copies = []
        for at in (n * tile, hidden_units + n * tile):
            cols = pl.ds(at, tile)
            for src, row, size, _ in pieces(own, others, 0):
                copies.append((src.at[:, cols], w.at[pl.ds(row, size), cols]))
        waits.append(start_all(copies, sems, 1 + n * len(copies)))
    got_rows.wait()
    order = order_matrix(rows, quarters)
    for b in range(recv_ref.shape[0] // rows):
        got = jnp.dot(order, recv[b * rows : b * rows + rows, :], preferred_element_type=F32).astype(BF16)
        here = slice(b * per, b * per + per)
        for q in range(quarters):
            at = pl.multiple_of(lax.rem(q + quarters - me_ref[0], quarters) * feat, feat)
            x_ref[here, pl.ds(at, feat)] = got[q * per : q * per + per, :feat]
            g_ref[here, pl.ds(at, feat)] = got[q * per : q * per + per, feat:]
    half = hidden_units // 2
    for n in range(hidden_units // tile):
        for copy in waits[n]:
            copy.wait()
        cols = slice(n * tile, n * tile + tile)
        gate = jnp.dot(x_ref[...], w[:, cols], preferred_element_type=F32)
        up = jnp.dot(x_ref[...], w[:, hidden_units + n * tile : hidden_units + n * tile + tile], preferred_element_type=F32)
        sig = jax.nn.sigmoid(gate)
        activ = gate * sig
        to_gate_ref[:, cols] = up * sig * (1.0 + gate * (1.0 - sig))
        to_up_ref[:, cols] = activ
        hidden = (activ * up).astype(BF16)
        part = lax.dot_general(hidden, g_ref[...], TN, preferred_element_type=F32).astype(BF16)
        for k, ref in ((0, down_own), (1, down_right), (3, down_left)):
            ref[cols, :] = part[:, k * feat : k * feat + feat]
        lo, hi = n * tile, n * tile + tile
        mid = min(max(half, lo), hi)
        if lo < mid:
            far_top[lo:mid, :] = part[: mid - lo, 2 * feat : 3 * feat]
        if mid < hi:
            far_bottom[mid - half : hi - half, :] = part[mid - lo :, 2 * feat : 3 * feat]


def back_kernel(quarters, me_ref, to_gate_ref, to_up_ref, g_ref, own_down, own, *refs):
    others, other_downs, refs = refs[:4], refs[4:8], refs[8:]
    back_ref, to_gate, to_up, g, wd, w, gp_ref, hold, sems = refs
    slots, hidden_units = to_gate.shape
    feat = own.shape[0]
    copies = [(g_ref, g)]
    for src, row, size, k in pieces(own_down, other_downs, 1):
        copies.append((src, wd.at[pl.ds(row, size), pl.ds(k * feat, feat)]))
    copies += [(to_gate_ref, to_gate), (to_up_ref, to_up)]
    early = start_all(copies, sems)
    late = start_all(
        [(src, w.at[pl.ds(row, size), :]) for src, row, size, _ in pieces(own, others, 0)], sems, len(copies)
    )
    for copy in early:
        copy.wait()
    tile = 256
    for n in range(hidden_units // tile):
        cols = slice(n * tile, n * tile + tile)
        total = lax.dot_general(g[...], wd[cols, :], NT, preferred_element_type=F32)
        gp_ref[:, cols] = (total * to_gate[:, cols]).astype(BF16)
        gp_ref[:, hidden_units + n * tile : hidden_units + n * tile + tile] = (total * to_up[:, cols]).astype(BF16)
    for k in range(quarters):
        for copy in (late[:1], late[1:2], late[2:4], late[4:])[k]:
            copy.wait()
        hold[lax.rem(me_ref[0] + k, quarters)] = lax.dot_general(
            gp_ref[...], w[k * feat : k * feat + feat, :], NT, preferred_element_type=F32
        ).astype(BF16)
    rows = 256
    per = rows // quarters
    order = order_matrix(rows, quarters)
    for b in range(back_ref.shape[0] // rows):
        stacked = jnp.concatenate([hold[q, b * per : b * per + per, :] for q in range(quarters)], axis=0)
        back_ref[b * rows : b * rows + rows, :] = lax.dot_general(
            order, stacked, TN, preferred_element_type=F32
        ).astype(BF16)


def combine_kernel(toks, pick_ref, ret_ref, out_ref):
    feat = ret_ref.shape[1]
    total = lax.dot_general(pick_ref[...], ret_ref[...], TN, preferred_element_type=F32)
    for q in range(out_ref.shape[1] // feat):
        out_ref[:, q * feat : q * feat + feat] = total[q * toks : q * toks + toks].astype(BF16)


def ring(size, step):
    return [(i, (i + step) % size) for i in range(size)]


def pass_on(a, b):
    return pl.pallas_call(
        lambda *refs: None,
        in_specs=[whole(pl.ANY)] * 2,
        out_specs=[whole(pl.ANY)] * 2,
        out_shape=[jax.ShapeDtypeStruct(a.shape, a.dtype)] * 2,
        input_output_aliases={0: 0, 1: 1},
        compiler_params=pltpu.CompilerParams(vmem_limit_bytes=VMEM_LIMIT),
        cost_estimate=pl.CostEstimate(flops=COST, bytes_accessed=0, transcendentals=0),
        name="pass_on",
    )(a, b)


def gather_two_steps(up, down, size):
    fwd, bwd = ring(size, 1), ring(size, -1)
    left_up, right_up = pass_on(lax.ppermute(up, "edp", fwd), lax.ppermute(up, "edp", bwd))
    left_down, right_down = lax.ppermute(down, "edp", fwd), lax.ppermute(down, "edp", bwd)
    out = []
    for left, right in ((left_up, right_up), (left_down, right_down)):
        half = left.shape[0] // 2
        out += [right, lax.ppermute(left[:half], "edp", fwd), lax.ppermute(right[half:], "edp", bwd), left]
    return out


def add_kernel(right, left, top, bottom, right_out, left_out):
    half = top.shape[0]
    right_out[:half, :] = (right[:half, :].astype(F32) + top[...].astype(F32)).astype(BF16)
    right_out[half:, :] = right[half:, :]
    left_out[:half, :] = left[:half, :]
    left_out[half:, :] = (left[half:, :].astype(F32) + bottom[...].astype(F32)).astype(BF16)


def scatter_two_steps(blocks, size):
    fwd, bwd = ring(size, 1), ring(size, -1)
    own, right, far_top, far_bottom, left = blocks
    top, bottom = lax.ppermute(far_top, "edp", fwd), lax.ppermute(far_bottom, "edp", bwd)
    right, left = pl.pallas_call(
        add_kernel,
        in_specs=[whole()] * 4,
        out_specs=[whole()] * 2,
        out_shape=[jax.ShapeDtypeStruct(right.shape, BF16)] * 2,
        compiler_params=pltpu.CompilerParams(vmem_limit_bytes=VMEM_LIMIT),
        cost_estimate=pl.CostEstimate(flops=COST, bytes_accessed=0, transcendentals=0),
        name="add_far",
    )(right, left, top, bottom)
    from_left, from_right = lax.ppermute(right, "edp", fwd), lax.ppermute(left, "edp", bwd)
    return (own.astype(F32) + from_left.astype(F32) + from_right.astype(F32)).astype(BF16)


def per_device(tokens, out_grad, expert_ids, gate_values, gate_up_weight, down_weight):
    experts, parts = lax.axis_size("ep"), lax.axis_size("edp")
    toks, width = tokens.shape
    hidden_units = down_weight.shape[1]
    quarters = 4
    feat = width // quarters
    slots = experts * 2
    rows = slots * quarters
    params = pltpu.CompilerParams(vmem_limit_bytes=VMEM_LIMIT)
    me = lax.axis_index("edp").astype(jnp.int32).reshape(1)

    others = gather_two_steps(gate_up_weight[0], down_weight[0], parts)

    tile = 128
    sent, pick = pl.pallas_call(
        functools.partial(send_kernel, quarters),
        grid=(rows // tile,),
        in_specs=[whole()] * 4,
        out_specs=[
            pl.BlockSpec((tile, 2 * feat), lambda b: (b, 0)),
            pl.BlockSpec((tile, quarters * toks), lambda b: (b, 0)),
        ],
        out_shape=[
            jax.ShapeDtypeStruct((rows, 2 * feat), BF16),
            jax.ShapeDtypeStruct((rows, quarters * toks), BF16),
        ],
        scratch_shapes=[pltpu.VMEM((quarters * toks, 3 * feat), F32)],
        compiler_params=params,
        name="send_rows",
    )(expert_ids.T, gate_values.T, tokens, out_grad)
    recv = lax.all_to_all(sent, "ep", split_axis=0, concat_axis=0, tiled=True)

    half = hidden_units // 2
    to_gate, to_up, rows_g, *blocks = pl.pallas_call(
        functools.partial(hidden_kernel, quarters),
        in_specs=[whole(pltpu.SMEM)] + [whole(pl.ANY)] * 6,
        out_specs=[whole()] * 8,
        out_shape=[
            jax.ShapeDtypeStruct((slots, hidden_units), F32),
            jax.ShapeDtypeStruct((slots, hidden_units), F32),
            jax.ShapeDtypeStruct((slots, width), BF16),
        ]
        + [jax.ShapeDtypeStruct((size, feat), BF16) for size in (hidden_units, hidden_units, half, half, hidden_units)],
        scratch_shapes=[
            pltpu.VMEM((rows, 2 * feat), BF16),
            pltpu.VMEM((width, 2 * hidden_units), BF16),
            pltpu.VMEM((slots, width), BF16),
            pltpu.SemaphoreType.DMA((64,)),
        ],
        compiler_params=params,
        name="hidden_rows",
    )(me, recv, gate_up_weight[0], *others[:4])
    down_grad = scatter_two_steps(blocks, parts)[None]

    back = pl.pallas_call(
        functools.partial(back_kernel, quarters),
        in_specs=[whole(pltpu.SMEM)] + [whole(pl.ANY)] * 13,
        out_specs=whole(),
        out_shape=jax.ShapeDtypeStruct((rows, feat), BF16),
        scratch_shapes=[
            pltpu.VMEM((slots, hidden_units), F32),
            pltpu.VMEM((slots, hidden_units), F32),
            pltpu.VMEM((slots, width), BF16),
            pltpu.VMEM((hidden_units, width), BF16),
            pltpu.VMEM((width, 2 * hidden_units), BF16),
            pltpu.VMEM((slots, 2 * hidden_units), BF16),
            pltpu.VMEM((quarters, slots, feat), BF16),
            pltpu.SemaphoreType.DMA((32,)),
        ],
        compiler_params=params,
        name="back_rows",
    )(me, to_gate, to_up, rows_g, down_weight[0], gate_up_weight[0], *others)
    returned = lax.all_to_all(back, "ep", split_axis=0, concat_axis=0, tiled=True)
    token_grads = pl.pallas_call(
        functools.partial(combine_kernel, toks),
        in_specs=[whole(), whole()],
        out_specs=whole(),
        out_shape=jax.ShapeDtypeStruct((toks, width), BF16),
        compiler_params=params,
        name="combine_rows",
    )(pick, returned)
    return (token_grads, down_grad)


def solution(mesh):
    return jax.shard_map(
        per_device,
        mesh=mesh,
        in_specs=(
            P(("ep", "edp"), None),
            P(("ep", "edp"), None),
            P(("ep", "edp"), None),
            P(("ep", "edp"), None),
            P("ep", "edp", None),
            P("ep", None, "edp"),
        ),
        out_specs=(P(("ep", "edp"), None), P("ep", None, "edp")),
        check_vma=False,
    )
```

```python
import functools

import jax
import jax.numpy as jnp
from jax import lax
from jax.experimental import pallas as pl
from jax.experimental.pallas import tpu as pltpu
from jax.sharding import PartitionSpec as P

EPSILON = 1e-06
F32, BF16 = jnp.float32, jnp.bfloat16
NT = (((1,), (1,)), ((), ()))
TN = (((0,), (0,)), ((), ()))
VMEM_LIMIT = 16 * 1024 * 1024
SEND_LIMIT = 56 * 1024 * 1024
COST = 20 * 10**9


def whole(memory_space=pltpu.VMEM):
    return pl.BlockSpec(memory_space=memory_space)


def rebuild(value, top):
    scale = (top + EPSILON).astype(BF16).astype(F32)
    return ((value / scale).astype(BF16).astype(F32) * scale).astype(BF16)


def send_kernel(quarters, ids_ref, gate_ref, tok_ref, grad_ref, send_ref, pick_ref, stack):
    block = pl.program_id(0)
    rows = send_ref.shape[0]
    toks, width = tok_ref.shape
    lanes = quarters * toks
    feat = width // quarters

    @pl.when(block == 0)
    def _():
        for q in range(quarters):
            here = pl.ds(q * toks, toks)
            for g in range(feat // 128):
                cols = slice(q * feat + g * 128, q * feat + g * 128 + 128)
                value = tok_ref[:, cols].astype(F32)
                top = jnp.max(jnp.abs(value), axis=1, keepdims=True)
                stack[here, pl.ds(g * 128, 128)] = rebuild(value, top).astype(F32)
            grads = grad_ref[:, q * feat : q * feat + feat].astype(F32)
            stack[here, pl.ds(feat, feat)] = grads
            for g in range(feat // 128):
                top = jnp.max(jnp.abs(grads[:, g * 128 : g * 128 + 128]), axis=1, keepdims=True)
                stack[here, pl.ds(2 * feat + g * 128, 128)] = jnp.broadcast_to(top, (toks, 128))

    row = lax.broadcasted_iota(jnp.int32, (rows, lanes), 0) + block * rows
    lane = lax.broadcasted_iota(jnp.int32, (rows, lanes), 1)
    expert, slot, quarter = row >> 3, (row >> 2) & 1, row & 3
    ids = jnp.concatenate([ids_ref[...]] * quarters, axis=1)
    gates = jnp.concatenate([gate_ref[...]] * quarters, axis=1)
    named = jnp.zeros((rows, lanes), F32)
    weight = jnp.zeros((rows, lanes), F32)
    for k in range(ids_ref.shape[0]):
        hit = ids[k : k + 1, :] == expert
        named = jnp.where(hit, 1.0, named)
        weight = jnp.where(hit, gates[k : k + 1, :], weight)
    above = lax.broadcasted_iota(jnp.int32, (lanes, lanes), 0)
    below = lax.broadcasted_iota(jnp.int32, (lanes, lanes), 1)
    earlier = (above < below) & (above // toks == below // toks)
    rank = jnp.dot(named.astype(BF16), earlier.astype(BF16), preferred_element_type=F32)
    chosen = (named > 0.5) & (rank == slot.astype(F32)) & (lane // toks == quarter)
    pick = jnp.where(chosen, 1.0, 0.0).astype(BF16)
    pick_ref[...] = pick
    send_ref[:, :feat] = jnp.dot(pick, stack[:, :feat].astype(BF16), preferred_element_type=F32).astype(BF16)
    gate = jnp.sum(jnp.where(chosen, weight, 0.0), axis=1, keepdims=True)
    grads = jnp.dot(pick, stack[:, feat : 2 * feat].astype(BF16), preferred_element_type=F32) * gate
    top = jnp.dot(pick, stack[:, 2 * feat :].astype(BF16), preferred_element_type=F32) * gate
    send_ref[:, feat:] = rebuild(grads, top)


def order_matrix(rows, quarters):
    out = lax.broadcasted_iota(jnp.int32, (rows, rows), 0)
    src = lax.broadcasted_iota(jnp.int32, (rows, rows), 1)
    per = rows // quarters
    return ((out % per) * quarters + out // per == src).astype(BF16)


def hidden_kernel(quarters, me_ref, recv, own_ref, right, far_a, far_b, left, *refs):
    to_gate_ref, to_up_ref, g_ref, *downs, x_ref, own, sem = refs[2:]
    fetch = pltpu.make_async_copy(own_ref, own, sem)
    fetch.start()
    rows = 256
    per = rows // quarters
    feat = recv.shape[1] // 2
    hidden_units = to_gate_ref.shape[1]
    tile = 256
    order = order_matrix(rows, quarters)
    for b in range(recv.shape[0] // rows):
        got = jnp.dot(order, recv[b * rows : b * rows + rows, :], preferred_element_type=F32).astype(BF16)
        here = slice(b * per, b * per + per)
        for q in range(quarters):
            at = pl.multiple_of(lax.rem(q + quarters - me_ref[0], quarters) * feat, feat)
            x_ref[here, pl.ds(at, feat)] = got[q * per : q * per + per, :feat]
            g_ref[here, pl.ds(at, feat)] = got[q * per : q * per + per, feat:]

    fetch.wait()

    def pre(cols):
        total, row = None, 0
        for w in (own, right, far_a, far_b, left):
            term = jnp.dot(x_ref[:, row : row + w.shape[0]], w[:, cols], preferred_element_type=F32)
            total, row = term if total is None else total + term, row + w.shape[0]
        return total

    for n in range(hidden_units // tile):
        cols = slice(n * tile, n * tile + tile)
        gate = pre(cols)
        up = pre(slice(hidden_units + n * tile, hidden_units + n * tile + tile))
        sig = jax.nn.sigmoid(gate)
        activ = gate * sig
        to_gate_ref[:, cols] = up * sig * (1.0 + gate * (1.0 - sig))
        to_up_ref[:, cols] = activ
        hidden = (activ * up).astype(BF16)
        for k, ref in enumerate(downs):
            ref[cols, :] = lax.dot_general(
                hidden, g_ref[:, k * feat : k * feat + feat], TN, preferred_element_type=F32
            ).astype(BF16)


def back_kernel(quarters, me_ref, to_gate, to_up, g, *refs):
    (own_up_ref, *ups), (own_ref, right, far_a, far_b, left), refs = refs[:5], refs[5:10], refs[10:]
    back_ref, gp_ref, hold, own_up, own, out, sems = refs
    fetch_down = pltpu.make_async_copy(own_ref, own, sems.at[0])
    fetch_down.start()
    fetch_up = pltpu.make_async_copy(own_up_ref, own_up, sems.at[1])
    fetch_up.start()
    hidden_units = to_gate.shape[1]
    feat = g.shape[1] // quarters
    half = hidden_units // 2
    fetch_down.wait()
    for h, far in enumerate((far_a, far_b)):
        cols = slice(h * half, h * half + half)
        total = None
        for k, w in enumerate((own[cols, :], right[cols, :], far[...], left[cols, :])):
            term = lax.dot_general(g[:, k * feat : k * feat + feat], w, NT, preferred_element_type=F32)
            total = term if total is None else total + term
        gp_ref[:, cols] = (total * to_gate[:, cols]).astype(BF16)
        gp_ref[:, hidden_units + h * half : hidden_units + h * half + half] = (total * to_up[:, cols]).astype(BF16)
    fetch_up.wait()
    at = 0
    for w in (own_up, *ups):
        rows = w.shape[0]
        hold[lax.rem(me_ref[0] + at // feat, quarters), :, at % feat : at % feat + rows] = lax.dot_general(
            gp_ref[...], w[...], NT, preferred_element_type=F32
        ).astype(BF16)
        at += rows
    rows = 256
    per = rows // quarters
    order = order_matrix(rows, quarters)
    copies = []
    for b in range(back_ref.shape[0] // rows):
        here = pl.ds(b * rows, rows)
        stacked = jnp.concatenate([hold[q, b * per : b * per + per, :] for q in range(quarters)], axis=0)
        out[here, :] = lax.dot_general(order, stacked, TN, preferred_element_type=F32).astype(BF16)
        copies.append(pltpu.make_async_copy(out.at[here, :], back_ref.at[here, :], sems.at[2 + b]))
        copies[-1].start()
    for copy in copies:
        copy.wait()


def combine_kernel(toks, pick_ref, ret_ref, out_ref):
    feat = ret_ref.shape[1]
    total = lax.dot_general(pick_ref[...], ret_ref[...], TN, preferred_element_type=F32)
    for q in range(out_ref.shape[1] // feat):
        out_ref[:, q * feat : q * feat + feat] = total[q * toks : q * toks + toks].astype(BF16)


def ring(size, step):
    return [(i, (i + step) % size) for i in range(size)]


def pass_on(a, b):
    return pl.pallas_call(
        lambda *refs: None,
        in_specs=[whole(pl.ANY)] * 2,
        out_specs=[whole(pl.ANY)] * 2,
        out_shape=[jax.ShapeDtypeStruct(a.shape, a.dtype)] * 2,
        input_output_aliases={0: 0, 1: 1},
        compiler_params=pltpu.CompilerParams(vmem_limit_bytes=VMEM_LIMIT),
        cost_estimate=pl.CostEstimate(flops=COST, bytes_accessed=0, transcendentals=0),
        name="pass_on",
    )(a, b)


def gather_two_steps(up, down, size):
    fwd, bwd = ring(size, 1), ring(size, -1)
    left_up, right_up = pass_on(lax.ppermute(up, "edp", fwd), lax.ppermute(up, "edp", bwd))
    left_down, right_down = lax.ppermute(down, "edp", fwd), lax.ppermute(down, "edp", bwd)
    out = []
    for left, right in ((left_up, right_up), (left_down, right_down)):
        half = left.shape[0] // 2
        out += [right, lax.ppermute(left[:half], "edp", fwd), lax.ppermute(right[half:], "edp", bwd), left]
    return out


def add_kernel(block, came, out):
    out[...] = (block[...].astype(F32) + came[...].astype(F32)).astype(BF16)


def scatter_two_steps(blocks, size):
    own, right, far, left = blocks
    came = lax.ppermute(far, "edp", ring(size, 1))
    right = pl.pallas_call(
        add_kernel,
        in_specs=[whole()] * 2,
        out_specs=whole(),
        out_shape=jax.ShapeDtypeStruct(right.shape, BF16),
        compiler_params=pltpu.CompilerParams(vmem_limit_bytes=VMEM_LIMIT),
        cost_estimate=pl.CostEstimate(flops=COST, bytes_accessed=0, transcendentals=0),
        name="add_far",
    )(right, came)
    from_left, from_right = lax.ppermute(right, "edp", ring(size, 1)), lax.ppermute(left, "edp", ring(size, -1))
    return (own.astype(F32) + from_left.astype(F32) + from_right.astype(F32)).astype(BF16)


def per_device(tokens, out_grad, expert_ids, gate_values, gate_up_weight, down_weight):
    experts, parts = lax.axis_size("ep"), lax.axis_size("edp")
    toks, width = tokens.shape
    hidden_units = down_weight.shape[1]
    quarters = 4
    feat = width // quarters
    slots = experts * 2
    rows = slots * quarters
    params = pltpu.CompilerParams(vmem_limit_bytes=VMEM_LIMIT)
    me = lax.axis_index("edp").astype(jnp.int32).reshape(1)

    others = gather_two_steps(gate_up_weight[0], down_weight[0], parts)

    tile = 512
    sent, pick = pl.pallas_call(
        functools.partial(send_kernel, quarters),
        grid=(rows // tile,),
        in_specs=[whole()] * 4,
        out_specs=[
            pl.BlockSpec((tile, 2 * feat), lambda b: (b, 0)),
            pl.BlockSpec((tile, quarters * toks), lambda b: (b, 0)),
        ],
        out_shape=[
            jax.ShapeDtypeStruct((rows, 2 * feat), BF16),
            jax.ShapeDtypeStruct((rows, quarters * toks), BF16),
        ],
        scratch_shapes=[pltpu.VMEM((quarters * toks, 3 * feat), F32)],
        compiler_params=pltpu.CompilerParams(vmem_limit_bytes=SEND_LIMIT),
        name="send_rows",
    )(expert_ids.T, gate_values.T, tokens, out_grad)
    recv = lax.all_to_all(sent, "ep", split_axis=0, concat_axis=0, tiled=True)

    to_gate, to_up, rows_g, *blocks = pl.pallas_call(
        functools.partial(hidden_kernel, quarters),
        in_specs=[whole(pltpu.SMEM), whole(), whole(pltpu.HBM)] + [whole()] * 6,
        out_specs=[whole()] * 7,
        out_shape=[
            jax.ShapeDtypeStruct((slots, hidden_units), F32),
            jax.ShapeDtypeStruct((slots, hidden_units), F32),
            jax.ShapeDtypeStruct((slots, width), BF16),
        ]
        + [jax.ShapeDtypeStruct((hidden_units, feat), BF16)] * parts,
        scratch_shapes=[
            pltpu.VMEM((slots, width), BF16),
            pltpu.VMEM((feat, 2 * hidden_units), BF16),
            pltpu.SemaphoreType.DMA,
        ],
        compiler_params=params,
        name="hidden_rows",
    )(me, recv, gate_up_weight[0], *others[:4], *others[5:7])
    down_grad = scatter_two_steps(blocks, parts)[None]

    back = pl.pallas_call(
        functools.partial(back_kernel, quarters),
        in_specs=[whole(pltpu.SMEM)]
        + [whole()] * 3
        + [whole(pltpu.HBM)]
        + [whole()] * 4
        + [whole(pltpu.HBM)]
        + [whole()] * 4,
        out_specs=whole(pltpu.HBM),
        out_shape=jax.ShapeDtypeStruct((rows, feat), BF16),
        scratch_shapes=[
            pltpu.VMEM((slots, 2 * hidden_units), BF16),
            pltpu.VMEM((quarters, slots, feat), BF16),
            pltpu.VMEM((feat, 2 * hidden_units), BF16),
            pltpu.VMEM((hidden_units, feat), BF16),
            pltpu.VMEM((rows, feat), BF16),
            pltpu.SemaphoreType.DMA((8,)),
        ],
        compiler_params=params,
        name="back_rows",
    )(me, to_gate, to_up, rows_g, gate_up_weight[0], *others[:4], down_weight[0], *others[4:])
    returned = lax.all_to_all(back, "ep", split_axis=0, concat_axis=0, tiled=True)
    token_grads = pl.pallas_call(
        functools.partial(combine_kernel, toks),
        in_specs=[whole(), whole()],
        out_specs=whole(),
        out_shape=jax.ShapeDtypeStruct((toks, width), BF16),
        compiler_params=params,
        name="combine_rows",
    )(pick, returned)
    return (token_grads, down_grad)


def solution(mesh):
    return jax.shard_map(
        per_device,
        mesh=mesh,
        in_specs=(
            P(("ep", "edp"), None),
            P(("ep", "edp"), None),
            P(("ep", "edp"), None),
            P(("ep", "edp"), None),
            P("ep", "edp", None),
            P("ep", None, "edp"),
        ),
        out_specs=(P(("ep", "edp"), None), P("ep", None, "edp")),
        check_vma=False,
    )
```

```python
import functools

import jax
import jax.numpy as jnp
from jax import lax
from jax.experimental import pallas as pl
from jax.experimental.pallas import tpu as pltpu
from jax.sharding import PartitionSpec as P

EPSILON = 1e-06
F32, BF16 = jnp.float32, jnp.bfloat16
NT = (((1,), (1,)), ((), ()))
TN = (((0,), (0,)), ((), ()))
VMEM_LIMIT = 16 * 1024 * 1024
SEND_LIMIT = 56 * 1024 * 1024
COST = 20 * 10**9


def whole(memory_space=pltpu.VMEM):
    return pl.BlockSpec(memory_space=memory_space)


def rebuild(value, top):
    scale = (top + EPSILON).astype(BF16).astype(F32)
    return ((value / scale).astype(BF16).astype(F32) * scale).astype(BF16)


def send_kernel(quarters, ids_ref, gate_ref, tok_ref, grad_ref, send_ref, pick_ref, stack):
    block = pl.program_id(0)
    rows = send_ref.shape[0]
    toks, width = tok_ref.shape
    lanes = quarters * toks
    feat = width // quarters

    @pl.when(block == 0)
    def _():
        for q in range(quarters):
            here = pl.ds(q * toks, toks)
            for g in range(feat // 128):
                cols = slice(q * feat + g * 128, q * feat + g * 128 + 128)
                value = tok_ref[:, cols].astype(F32)
                top = jnp.max(jnp.abs(value), axis=1, keepdims=True)
                stack[here, pl.ds(g * 128, 128)] = rebuild(value, top).astype(F32)
            grads = grad_ref[:, q * feat : q * feat + feat].astype(F32)
            stack[here, pl.ds(feat, feat)] = grads
            for g in range(feat // 128):
                top = jnp.max(jnp.abs(grads[:, g * 128 : g * 128 + 128]), axis=1, keepdims=True)
                stack[here, pl.ds(2 * feat + g * 128, 128)] = jnp.broadcast_to(top, (toks, 128))

    row = lax.broadcasted_iota(jnp.int32, (rows, lanes), 0) + block * rows
    lane = lax.broadcasted_iota(jnp.int32, (rows, lanes), 1)
    expert, slot, quarter = row >> 3, (row >> 2) & 1, row & 3
    ids = jnp.concatenate([ids_ref[...]] * quarters, axis=1)
    gates = jnp.concatenate([gate_ref[...]] * quarters, axis=1)
    named = jnp.zeros((rows, lanes), F32)
    weight = jnp.zeros((rows, lanes), F32)
    for k in range(ids_ref.shape[0]):
        hit = ids[k : k + 1, :] == expert
        named = jnp.where(hit, 1.0, named)
        weight = jnp.where(hit, gates[k : k + 1, :], weight)
    above = lax.broadcasted_iota(jnp.int32, (lanes, lanes), 0)
    below = lax.broadcasted_iota(jnp.int32, (lanes, lanes), 1)
    earlier = (above < below) & (above // toks == below // toks)
    rank = jnp.dot(named.astype(BF16), earlier.astype(BF16), preferred_element_type=F32)
    chosen = (named > 0.5) & (rank == slot.astype(F32)) & (lane // toks == quarter)
    pick = jnp.where(chosen, 1.0, 0.0).astype(BF16)
    pick_ref[...] = pick
    send_ref[:, :feat] = jnp.dot(pick, stack[:, :feat].astype(BF16), preferred_element_type=F32).astype(BF16)
    gate = jnp.sum(jnp.where(chosen, weight, 0.0), axis=1, keepdims=True)
    grads = jnp.dot(pick, stack[:, feat : 2 * feat].astype(BF16), preferred_element_type=F32) * gate
    top = jnp.dot(pick, stack[:, 2 * feat :].astype(BF16), preferred_element_type=F32) * gate
    send_ref[:, feat:] = rebuild(grads, top)


def order_matrix(rows, quarters):
    out = lax.broadcasted_iota(jnp.int32, (rows, rows), 0)
    src = lax.broadcasted_iota(jnp.int32, (rows, rows), 1)
    per = rows // quarters
    return ((out % per) * quarters + out // per == src).astype(BF16)


def hidden_kernel(quarters, me_ref, recv, own_ref, right, far_a, far_b, left, *refs):
    to_gate_ref, to_up_ref, g_ref, *downs, x_ref, own, sem = refs
    fetch = pltpu.make_async_copy(own_ref, own, sem)
    fetch.start()
    rows = 256
    per = rows // quarters
    feat = recv.shape[1] // 2
    hidden_units = to_gate_ref.shape[1]
    tile = 256
    order = order_matrix(rows, quarters)
    for b in range(recv.shape[0] // rows):
        got = jnp.dot(order, recv[b * rows : b * rows + rows, :], preferred_element_type=F32).astype(BF16)
        here = slice(b * per, b * per + per)
        for q in range(quarters):
            at = pl.multiple_of(lax.rem(q + quarters - me_ref[0], quarters) * feat, feat)
            x_ref[here, pl.ds(at, feat)] = got[q * per : q * per + per, :feat]
            g_ref[here, pl.ds(at, feat)] = got[q * per : q * per + per, feat:]

    fetch.wait()

    def pre(cols):
        total, row = None, 0
        for w in (own, right, far_a, far_b, left):
            term = jnp.dot(x_ref[:, row : row + w.shape[0]], w[:, cols], preferred_element_type=F32)
            total, row = term if total is None else total + term, row + w.shape[0]
        return total

    for n in range(hidden_units // tile):
        cols = slice(n * tile, n * tile + tile)
        gate = pre(cols)
        up = pre(slice(hidden_units + n * tile, hidden_units + n * tile + tile))
        sig = jax.nn.sigmoid(gate)
        activ = gate * sig
        to_gate_ref[:, cols] = up * sig * (1.0 + gate * (1.0 - sig))
        to_up_ref[:, cols] = activ
        hidden = (activ * up).astype(BF16)
        for k, ref in enumerate(downs):
            ref[cols, :] = lax.dot_general(
                hidden, g_ref[:, k * feat : k * feat + feat], TN, preferred_element_type=F32
            ).astype(BF16)


def back_kernel(quarters, me_ref, to_gate, to_up, g, *refs):
    (own_up_ref, *ups), (own_ref, right, far_a, far_b, left), refs = refs[:5], refs[5:10], refs[10:]
    back_ref, gp_ref, hold, own_up, own, out, sems = refs
    fetch_down = pltpu.make_async_copy(own_ref, own, sems.at[0])
    fetch_down.start()
    fetch_up = pltpu.make_async_copy(own_up_ref, own_up, sems.at[1])
    fetch_up.start()
    hidden_units = to_gate.shape[1]
    feat = g.shape[1] // quarters
    half = hidden_units // 2
    fetch_down.wait()
    for h, far in enumerate((far_a, far_b)):
        cols = slice(h * half, h * half + half)
        total = None
        for k, w in enumerate((own[cols, :], right[cols, :], far[...], left[cols, :])):
            term = lax.dot_general(g[:, k * feat : k * feat + feat], w, NT, preferred_element_type=F32)
            total = term if total is None else total + term
        gp_ref[:, cols] = (total * to_gate[:, cols]).astype(BF16)
        gp_ref[:, hidden_units + h * half : hidden_units + h * half + half] = (total * to_up[:, cols]).astype(BF16)
    fetch_up.wait()
    at = 0
    for w in (own_up, *ups):
        rows = w.shape[0]
        hold[lax.rem(me_ref[0] + at // feat, quarters), :, at % feat : at % feat + rows] = lax.dot_general(
            gp_ref[...], w[...], NT, preferred_element_type=F32
        ).astype(BF16)
        at += rows
    rows = 256
    per = rows // quarters
    order = order_matrix(rows, quarters)
    copies = []
    for b in range(back_ref.shape[0] // rows):
        here = pl.ds(b * rows, rows)
        stacked = jnp.concatenate([hold[q, b * per : b * per + per, :] for q in range(quarters)], axis=0)
        out[here, :] = lax.dot_general(order, stacked, TN, preferred_element_type=F32).astype(BF16)
        copies.append(pltpu.make_async_copy(out.at[here, :], back_ref.at[here, :], sems.at[2 + b]))
        copies[-1].start()
    for copy in copies:
        copy.wait()


def combine_kernel(toks, pick_ref, ret_ref, out_ref):
    feat = ret_ref.shape[1]
    total = lax.dot_general(pick_ref[...], ret_ref[...], TN, preferred_element_type=F32)
    for q in range(out_ref.shape[1] // feat):
        out_ref[:, q * feat : q * feat + feat] = total[q * toks : q * toks + toks].astype(BF16)


def ring(size, step):
    return [(i, (i + step) % size) for i in range(size)]


def pass_on(a, b):
    return pl.pallas_call(
        lambda *refs: None,
        in_specs=[whole(pl.ANY)] * 2,
        out_specs=[whole(pl.ANY)] * 2,
        out_shape=[jax.ShapeDtypeStruct(a.shape, a.dtype)] * 2,
        input_output_aliases={0: 0, 1: 1},
        compiler_params=pltpu.CompilerParams(vmem_limit_bytes=VMEM_LIMIT),
        cost_estimate=pl.CostEstimate(flops=COST, bytes_accessed=0, transcendentals=0),
        name="pass_on",
    )(a, b)


def gather_two_steps(up, down, size):
    fwd, bwd = ring(size, 1), ring(size, -1)
    left_up, right_up = pass_on(lax.ppermute(up, "edp", fwd), lax.ppermute(up, "edp", bwd))
    left_down, right_down = lax.ppermute(down, "edp", fwd), lax.ppermute(down, "edp", bwd)
    out = []
    for left, right in ((left_up, right_up), (left_down, right_down)):
        half = left.shape[0] // 2
        out += [right, lax.ppermute(left[:half], "edp", fwd), lax.ppermute(right[half:], "edp", bwd), left]
    return out


def add_kernel(block, came, left, out, left_out):
    out[...] = (block[...].astype(F32) + came[...].astype(F32)).astype(BF16)


def scatter_two_steps(blocks, size):
    own, right, far, left = blocks
    came = lax.ppermute(far, "edp", ring(size, 1))
    right, left = pl.pallas_call(
        add_kernel,
        in_specs=[whole()] * 2 + [whole(pl.ANY)],
        out_specs=[whole(), whole(pl.ANY)],
        out_shape=[jax.ShapeDtypeStruct(right.shape, BF16)] * 2,
        input_output_aliases={2: 1},
        compiler_params=pltpu.CompilerParams(vmem_limit_bytes=VMEM_LIMIT),
        cost_estimate=pl.CostEstimate(flops=COST, bytes_accessed=0, transcendentals=0),
        name="add_far",
    )(right, came, left)
    from_left, from_right = lax.ppermute(right, "edp", ring(size, 1)), lax.ppermute(left, "edp", ring(size, -1))
    return (own.astype(F32) + from_left.astype(F32) + from_right.astype(F32)).astype(BF16)


def per_device(tokens, out_grad, expert_ids, gate_values, gate_up_weight, down_weight):
    experts, parts = lax.axis_size("ep"), lax.axis_size("edp")
    toks, width = tokens.shape
    hidden_units = down_weight.shape[1]
    quarters = 4
    feat = width // quarters
    slots = experts * 2
    rows = slots * quarters
    params = pltpu.CompilerParams(vmem_limit_bytes=VMEM_LIMIT)
    me = lax.axis_index("edp").astype(jnp.int32).reshape(1)

    others = gather_two_steps(gate_up_weight[0], down_weight[0], parts)

    tile = 512
    sent, pick = pl.pallas_call(
        functools.partial(send_kernel, quarters),
        grid=(rows // tile,),
        in_specs=[whole()] * 4,
        out_specs=[
            pl.BlockSpec((tile, 2 * feat), lambda b: (b, 0)),
            pl.BlockSpec((tile, quarters * toks), lambda b: (b, 0)),
        ],
        out_shape=[
            jax.ShapeDtypeStruct((rows, 2 * feat), BF16),
            jax.ShapeDtypeStruct((rows, quarters * toks), BF16),
        ],
        scratch_shapes=[pltpu.VMEM((quarters * toks, 3 * feat), F32)],
        compiler_params=pltpu.CompilerParams(vmem_limit_bytes=SEND_LIMIT),
        name="send_rows",
    )(expert_ids.T, gate_values.T, tokens, out_grad)
    recv = lax.all_to_all(sent, "ep", split_axis=0, concat_axis=0, tiled=True)

    to_gate, to_up, rows_g, *blocks = pl.pallas_call(
        functools.partial(hidden_kernel, quarters),
        in_specs=[whole(pltpu.SMEM), whole(), whole(pltpu.HBM)] + [whole()] * 4,
        out_specs=[whole()] * 7,
        out_shape=[
            jax.ShapeDtypeStruct((slots, hidden_units), F32),
            jax.ShapeDtypeStruct((slots, hidden_units), F32),
            jax.ShapeDtypeStruct((slots, width), BF16),
        ]
        + [jax.ShapeDtypeStruct((hidden_units, feat), BF16)] * parts,
        scratch_shapes=[
            pltpu.VMEM((slots, width), BF16),
            pltpu.VMEM((feat, 2 * hidden_units), BF16),
            pltpu.SemaphoreType.DMA,
        ],
        compiler_params=params,
        cost_estimate=pl.CostEstimate(flops=1, bytes_accessed=1, transcendentals=0),
        name="hidden_rows",
    )(me, recv, gate_up_weight[0], *others[:4])
    down_grad = scatter_two_steps(blocks, parts)[None]

    back = pl.pallas_call(
        functools.partial(back_kernel, quarters),
        in_specs=[whole(pltpu.SMEM)]
        + [whole()] * 3
        + [whole(pltpu.HBM)]
        + [whole()] * 4
        + [whole(pltpu.HBM)]
        + [whole()] * 4,
        out_specs=whole(pltpu.HBM),
        out_shape=jax.ShapeDtypeStruct((rows, feat), BF16),
        scratch_shapes=[
            pltpu.VMEM((slots, 2 * hidden_units), BF16),
            pltpu.VMEM((quarters, slots, feat), BF16),
            pltpu.VMEM((feat, 2 * hidden_units), BF16),
            pltpu.VMEM((hidden_units, feat), BF16),
            pltpu.VMEM((rows, feat), BF16),
            pltpu.SemaphoreType.DMA((8,)),
        ],
        compiler_params=params,
        cost_estimate=pl.CostEstimate(flops=COST, bytes_accessed=0, transcendentals=0),
        name="back_rows",
    )(me, to_gate, to_up, rows_g, gate_up_weight[0], *others[:4], down_weight[0], *others[4:])
    returned = lax.all_to_all(back, "ep", split_axis=0, concat_axis=0, tiled=True)
    token_grads = pl.pallas_call(
        functools.partial(combine_kernel, toks),
        in_specs=[whole(), whole()],
        out_specs=whole(),
        out_shape=jax.ShapeDtypeStruct((toks, width), BF16),
        compiler_params=params,
        name="combine_rows",
    )(pick, returned)
    return (token_grads, down_grad)


def solution(mesh):
    return jax.shard_map(
        per_device,
        mesh=mesh,
        in_specs=(
            P(("ep", "edp"), None),
            P(("ep", "edp"), None),
            P(("ep", "edp"), None),
            P(("ep", "edp"), None),
            P("ep", "edp", None),
            P("ep", None, "edp"),
        ),
        out_specs=(P(("ep", "edp"), None), P("ep", None, "edp")),
        check_vma=False,
    )
```

```python
import functools

import jax
import jax.numpy as jnp
from jax import lax
from jax.experimental import pallas as pl
from jax.experimental.pallas import tpu as pltpu
from jax.sharding import PartitionSpec as P

EPSILON = 1e-06
F32, BF16 = jnp.float32, jnp.bfloat16
NT = (((1,), (1,)), ((), ()))
TN = (((0,), (0,)), ((), ()))
VMEM_LIMIT = 16 * 1024 * 1024
EXPERT_LIMIT = 50 * 1024 * 1024
SEND_LIMIT = 56 * 1024 * 1024
COST = 20 * 10**9


def whole(memory_space=pltpu.VMEM):
    return pl.BlockSpec(memory_space=memory_space)


def rebuild(value, top):
    scale = (top + EPSILON).astype(BF16).astype(F32)
    return ((value / scale).astype(BF16).astype(F32) * scale).astype(BF16)


def send_kernel(quarters, ids_ref, gate_ref, tok_ref, grad_ref, send_ref, pick_ref, stack):
    block = pl.program_id(0)
    rows = send_ref.shape[0]
    toks, width = tok_ref.shape
    lanes = quarters * toks
    feat = width // quarters

    @pl.when(block == 0)
    def _():
        for q in range(quarters):
            here = pl.ds(q * toks, toks)
            for g in range(feat // 128):
                cols = slice(q * feat + g * 128, q * feat + g * 128 + 128)
                value = tok_ref[:, cols].astype(F32)
                top = jnp.max(jnp.abs(value), axis=1, keepdims=True)
                stack[here, pl.ds(g * 128, 128)] = rebuild(value, top).astype(F32)
            grads = grad_ref[:, q * feat : q * feat + feat].astype(F32)
            stack[here, pl.ds(feat, feat)] = grads
            for g in range(feat // 128):
                top = jnp.max(jnp.abs(grads[:, g * 128 : g * 128 + 128]), axis=1, keepdims=True)
                stack[here, pl.ds(2 * feat + g * 128, 128)] = jnp.broadcast_to(top, (toks, 128))

    row = lax.broadcasted_iota(jnp.int32, (rows, lanes), 0) + block * rows
    lane = lax.broadcasted_iota(jnp.int32, (rows, lanes), 1)
    expert, slot, quarter = row >> 3, (row >> 2) & 1, row & 3
    ids = jnp.concatenate([ids_ref[...]] * quarters, axis=1)
    gates = jnp.concatenate([gate_ref[...]] * quarters, axis=1)
    named = jnp.zeros((rows, lanes), F32)
    weight = jnp.zeros((rows, lanes), F32)
    for k in range(ids_ref.shape[0]):
        hit = ids[k : k + 1, :] == expert
        named = jnp.where(hit, 1.0, named)
        weight = jnp.where(hit, gates[k : k + 1, :], weight)
    above = lax.broadcasted_iota(jnp.int32, (lanes, lanes), 0)
    below = lax.broadcasted_iota(jnp.int32, (lanes, lanes), 1)
    earlier = (above < below) & (above // toks == below // toks)
    rank = jnp.dot(named.astype(BF16), earlier.astype(BF16), preferred_element_type=F32)
    chosen = (named > 0.5) & (rank == slot.astype(F32)) & (lane // toks == quarter)
    pick = jnp.where(chosen, 1.0, 0.0).astype(BF16)
    pick_ref[...] = pick
    send_ref[:, :feat] = jnp.dot(pick, stack[:, :feat].astype(BF16), preferred_element_type=F32).astype(BF16)
    gate = jnp.sum(jnp.where(chosen, weight, 0.0), axis=1, keepdims=True)
    grads = jnp.dot(pick, stack[:, feat : 2 * feat].astype(BF16), preferred_element_type=F32) * gate
    top = jnp.dot(pick, stack[:, 2 * feat :].astype(BF16), preferred_element_type=F32) * gate
    send_ref[:, feat:] = rebuild(grads, top)


def order_matrix(rows, quarters):
    out = lax.broadcasted_iota(jnp.int32, (rows, rows), 0)
    src = lax.broadcasted_iota(jnp.int32, (rows, rows), 1)
    per = rows // quarters
    return ((out % per) * quarters + out // per == src).astype(BF16)


def start(copies, src, dst, sems):
    copies.append(pltpu.make_async_copy(src, dst, sems.at[len(copies)]))
    copies[-1].start()
    return copies[-1]


def pieces(own, others):
    right, far_a, far_b, left = others
    rows = own.shape[0]
    half = rows // 2
    return [(own, 0, 0, rows), (right, 1, 0, rows), (far_a, 2, 0, half), (far_b, 2, half, half), (left, 3, 0, rows)]


def expert_kernel(quarters, me_ref, recv_ref, *refs):
    ups, downs, refs = pieces(refs[0], refs[1:5]), pieces(refs[5], refs[6:10]), refs[10:]
    back_ref, *blocks, recv, w, wd, x_ref, g_ref, hid_ref, to_gate, to_up, gp_ref, hold, out, sems = refs
    rows = 256
    per = rows // quarters
    feat = recv.shape[1] // 2
    hidden_units = hid_ref.shape[1]
    tile = 256
    started = []
    came, columns = [], []
    for b in range(recv.shape[0] // rows):
        here = pl.ds(b * rows, rows)
        came.append(start(started, recv_ref.at[here, :], recv.at[here, :], sems))
    for n in range(hidden_units // tile):
        some = []
        for at in (n * tile, hidden_units + n * tile):
            for ref, block, row, size in ups:
                to = w.at[pl.ds(block * feat + row, size), pl.ds(at, tile)]
                some.append(start(started, ref.at[:, pl.ds(at, tile)], to, sems))
        columns.append(some)
    down_came = [
        start(started, ref, wd.at[pl.ds(row, size), pl.ds(block * feat, feat)], sems) for ref, block, row, size in downs
    ]
    order = order_matrix(rows, quarters)
    for b in range(recv.shape[0] // rows):
        came[b].wait()
        got = jnp.dot(order, recv[b * rows : b * rows + rows, :], preferred_element_type=F32).astype(BF16)
        here = slice(b * per, b * per + per)
        for q in range(quarters):
            at = pl.multiple_of(lax.rem(q + quarters - me_ref[0], quarters) * feat, feat)
            x_ref[here, pl.ds(at, feat)] = got[q * per : q * per + per, :feat]
            g_ref[here, pl.ds(at, feat)] = got[q * per : q * per + per, feat:]

    def pre(cols):
        return jnp.dot(x_ref[...], w[:, cols], preferred_element_type=F32)

    tile = 256
    for n in range(hidden_units // tile):
        for copy in columns[n]:
            copy.wait()
        cols = slice(n * tile, n * tile + tile)
        gate = pre(cols)
        up = pre(slice(hidden_units + n * tile, hidden_units + n * tile + tile))
        sig = jax.nn.sigmoid(gate)
        activ = gate * sig
        to_gate[:, cols] = up * sig * (1.0 + gate * (1.0 - sig))
        to_up[:, cols] = activ
        hid_ref[:, cols] = (activ * up).astype(BF16)

    for copy in down_came:
        copy.wait()
    for n in range(hidden_units // tile):
        cols = slice(n * tile, n * tile + tile)
        total = lax.dot_general(g_ref[...], wd[cols, :], NT, preferred_element_type=F32)
        gp_ref[:, cols] = (total * to_gate[:, cols]).astype(BF16)
        gp_ref[:, hidden_units + n * tile : hidden_units + n * tile + tile] = (total * to_up[:, cols]).astype(BF16)
    for k in range(quarters):
        hold[lax.rem(me_ref[0] + k, quarters)] = lax.dot_general(
            gp_ref[...], w[k * feat : k * feat + feat, :], NT, preferred_element_type=F32
        ).astype(BF16)
    copies = []
    for b in range(back_ref.shape[0] // rows):
        here = pl.ds(b * rows, rows)
        stacked = jnp.concatenate([hold[q, b * per : b * per + per, :] for q in range(quarters)], axis=0)
        out[here, :] = lax.dot_general(order, stacked, TN, preferred_element_type=F32).astype(BF16)
        copies.append(start(started, out.at[here, :], back_ref.at[here, :], sems))
    for k, ref in enumerate(blocks):
        ref[...] = lax.dot_general(
            hid_ref[...], g_ref[:, k * feat : k * feat + feat], TN, preferred_element_type=F32
        ).astype(BF16)
    for copy in copies:
        copy.wait()


def combine_kernel(toks, pick_ref, ret_ref, out_ref):
    feat = ret_ref.shape[1]
    total = lax.dot_general(pick_ref[...], ret_ref[...], TN, preferred_element_type=F32)
    for q in range(out_ref.shape[1] // feat):
        out_ref[:, q * feat : q * feat + feat] = total[q * toks : q * toks + toks].astype(BF16)


def ring(size, step):
    return [(i, (i + step) % size) for i in range(size)]


def pass_on(a, b):
    return pl.pallas_call(
        lambda *refs: None,
        in_specs=[whole(pl.ANY)] * 2,
        out_specs=[whole(pl.ANY)] * 2,
        out_shape=[jax.ShapeDtypeStruct(a.shape, a.dtype)] * 2,
        input_output_aliases={0: 0, 1: 1},
        compiler_params=pltpu.CompilerParams(vmem_limit_bytes=VMEM_LIMIT),
        cost_estimate=pl.CostEstimate(flops=COST, bytes_accessed=0, transcendentals=0),
        name="pass_on",
    )(a, b)


def gather_two_steps(up, down, size):
    fwd, bwd = ring(size, 1), ring(size, -1)
    left_up, right_up = pass_on(lax.ppermute(up, "edp", fwd), lax.ppermute(up, "edp", bwd))
    left_down, right_down = lax.ppermute(down, "edp", fwd), lax.ppermute(down, "edp", bwd)
    out = []
    for left, right in ((left_up, right_up), (left_down, right_down)):
        half = left.shape[0] // 2
        out += [right, lax.ppermute(left[:half], "edp", fwd), lax.ppermute(right[half:], "edp", bwd), left]
    return out


def add_kernel(block, came, out):
    out[...] = (block[...].astype(F32) + came[...].astype(F32)).astype(BF16)


def scatter_two_steps(blocks, size):
    own, right, far, left = blocks
    came = lax.ppermute(far, "edp", ring(size, 1))
    right = pl.pallas_call(
        add_kernel,
        in_specs=[whole()] * 2,
        out_specs=whole(),
        out_shape=jax.ShapeDtypeStruct(right.shape, BF16),
        compiler_params=pltpu.CompilerParams(vmem_limit_bytes=VMEM_LIMIT),
        cost_estimate=pl.CostEstimate(flops=COST, bytes_accessed=0, transcendentals=0),
        name="add_far",
    )(right, came)
    from_left, from_right = lax.ppermute(right, "edp", ring(size, 1)), lax.ppermute(left, "edp", ring(size, -1))
    return (own.astype(F32) + from_left.astype(F32) + from_right.astype(F32)).astype(BF16)


def per_device(tokens, out_grad, expert_ids, gate_values, gate_up_weight, down_weight):
    experts, parts = lax.axis_size("ep"), lax.axis_size("edp")
    toks, width = tokens.shape
    hidden_units = down_weight.shape[1]
    quarters = 4
    feat = width // quarters
    slots = experts * 2
    rows = slots * quarters
    params = pltpu.CompilerParams(vmem_limit_bytes=VMEM_LIMIT)
    me = lax.axis_index("edp").astype(jnp.int32).reshape(1)

    others = gather_two_steps(gate_up_weight[0], down_weight[0], parts)

    tile = 512
    sent, pick = pl.pallas_call(
        functools.partial(send_kernel, quarters),
        grid=(rows // tile,),
        in_specs=[whole()] * 4,
        out_specs=[
            pl.BlockSpec((tile, 2 * feat), lambda b: (b, 0)),
            pl.BlockSpec((tile, quarters * toks), lambda b: (b, 0)),
        ],
        out_shape=[
            jax.ShapeDtypeStruct((rows, 2 * feat), BF16),
            jax.ShapeDtypeStruct((rows, quarters * toks), BF16),
        ],
        scratch_shapes=[pltpu.VMEM((quarters * toks, 3 * feat), F32)],
        compiler_params=pltpu.CompilerParams(vmem_limit_bytes=SEND_LIMIT),
        name="send_rows",
    )(expert_ids.T, gate_values.T, tokens, out_grad)
    recv = lax.all_to_all(sent, "ep", split_axis=0, concat_axis=0, tiled=True)

    back, *blocks = pl.pallas_call(
        functools.partial(expert_kernel, quarters),
        in_specs=[whole(pltpu.SMEM)] + [whole(pl.ANY)] * 11,
        out_specs=[whole(pl.ANY)] + [whole()] * parts,
        out_shape=[jax.ShapeDtypeStruct((rows, feat), BF16)]
        + [jax.ShapeDtypeStruct((hidden_units, feat), BF16)] * parts,
        scratch_shapes=[
            pltpu.VMEM((rows, 2 * feat), BF16),
            pltpu.VMEM((width, 2 * hidden_units), BF16),
            pltpu.VMEM((hidden_units, width), BF16),
            pltpu.VMEM((slots, width), BF16),
            pltpu.VMEM((slots, width), BF16),
            pltpu.VMEM((slots, hidden_units), BF16),
            pltpu.VMEM((slots, hidden_units), F32),
            pltpu.VMEM((slots, hidden_units), F32),
            pltpu.VMEM((slots, 2 * hidden_units), BF16),
            pltpu.VMEM((quarters, slots, feat), BF16),
            pltpu.VMEM((rows, feat), BF16),
            pltpu.SemaphoreType.DMA((64,)),
        ],
        compiler_params=pltpu.CompilerParams(vmem_limit_bytes=EXPERT_LIMIT),
        name="expert_rows",
    )(me, recv, gate_up_weight[0], *others[:4], down_weight[0], *others[4:])
    down_grad = scatter_two_steps(blocks, parts)[None]
    returned = lax.all_to_all(back, "ep", split_axis=0, concat_axis=0, tiled=True)
    token_grads = pl.pallas_call(
        functools.partial(combine_kernel, toks),
        in_specs=[whole(), whole()],
        out_specs=whole(),
        out_shape=jax.ShapeDtypeStruct((toks, width), BF16),
        compiler_params=params,
        name="combine_rows",
    )(pick, returned)
    return (token_grads, down_grad)


def solution(mesh):
    return jax.shard_map(
        per_device,
        mesh=mesh,
        in_specs=(
            P(("ep", "edp"), None),
            P(("ep", "edp"), None),
            P(("ep", "edp"), None),
            P(("ep", "edp"), None),
            P("ep", "edp", None),
            P("ep", None, "edp"),
        ),
        out_specs=(P(("ep", "edp"), None), P("ep", None, "edp")),
        check_vma=False,
    )
```

```python
import functools

import jax
import jax.numpy as jnp
from jax import lax
from jax.experimental import pallas as pl
from jax.experimental.pallas import tpu as pltpu
from jax.sharding import PartitionSpec as P

EPSILON = 1e-06
F32, BF16 = jnp.float32, jnp.bfloat16
NT = (((1,), (1,)), ((), ()))
TN = (((0,), (0,)), ((), ()))
VMEM_LIMIT = 16 * 1024 * 1024
BACK_LIMIT = 16 * 1024 * 1024
HIDDEN_LIMIT = 44 * 1024 * 1024
SEND_LIMIT = 56 * 1024 * 1024
COST = 20 * 10**9
ADD_COST = 8 * 10**9


def whole(memory_space=pltpu.VMEM):
    return pl.BlockSpec(memory_space=memory_space)


def rebuild(value, top):
    scale = (top + EPSILON).astype(BF16).astype(F32)
    return ((value / scale).astype(BF16).astype(F32) * scale).astype(BF16)


def send_kernel(quarters, ids_ref, gate_ref, tok_ref, grad_ref, send_ref, pick_ref, stack):
    block = pl.program_id(0)
    rows = send_ref.shape[0]
    toks, width = tok_ref.shape
    lanes = quarters * toks
    feat = width // quarters

    @pl.when(block == 0)
    def _():
        for q in range(quarters):
            here = pl.ds(q * toks, toks)
            for g in range(feat // 128):
                cols = slice(q * feat + g * 128, q * feat + g * 128 + 128)
                value = tok_ref[:, cols].astype(F32)
                top = jnp.max(jnp.abs(value), axis=1, keepdims=True)
                stack[here, pl.ds(g * 128, 128)] = rebuild(value, top).astype(F32)
            grads = grad_ref[:, q * feat : q * feat + feat].astype(F32)
            stack[here, pl.ds(feat, feat)] = grads
            for g in range(feat // 128):
                top = jnp.max(jnp.abs(grads[:, g * 128 : g * 128 + 128]), axis=1, keepdims=True)
                stack[here, pl.ds(2 * feat + g * 128, 128)] = jnp.broadcast_to(top, (toks, 128))

    row = lax.broadcasted_iota(jnp.int32, (rows, lanes), 0) + block * rows
    lane = lax.broadcasted_iota(jnp.int32, (rows, lanes), 1)
    expert, slot, quarter = row >> 3, (row >> 2) & 1, row & 3
    ids = jnp.concatenate([ids_ref[...]] * quarters, axis=1)
    gates = jnp.concatenate([gate_ref[...]] * quarters, axis=1)
    named = jnp.zeros((rows, lanes), F32)
    weight = jnp.zeros((rows, lanes), F32)
    for k in range(ids_ref.shape[0]):
        hit = ids[k : k + 1, :] == expert
        named = jnp.where(hit, 1.0, named)
        weight = jnp.where(hit, gates[k : k + 1, :], weight)
    above = lax.broadcasted_iota(jnp.int32, (lanes, lanes), 0)
    below = lax.broadcasted_iota(jnp.int32, (lanes, lanes), 1)
    earlier = (above < below) & (above // toks == below // toks)
    rank = jnp.dot(named.astype(BF16), earlier.astype(BF16), preferred_element_type=F32)
    chosen = (named > 0.5) & (rank == slot.astype(F32)) & (lane // toks == quarter)
    pick = jnp.where(chosen, 1.0, 0.0).astype(BF16)
    pick_ref[...] = pick
    send_ref[:, :feat] = jnp.dot(pick, stack[:, :feat].astype(BF16), preferred_element_type=F32).astype(BF16)
    gate = jnp.sum(jnp.where(chosen, weight, 0.0), axis=1, keepdims=True)
    grads = jnp.dot(pick, stack[:, feat : 2 * feat].astype(BF16), preferred_element_type=F32) * gate
    top = jnp.dot(pick, stack[:, 2 * feat :].astype(BF16), preferred_element_type=F32) * gate
    send_ref[:, feat:] = rebuild(grads, top)


def order_matrix(rows, quarters):
    out = lax.broadcasted_iota(jnp.int32, (rows, rows), 0)
    src = lax.broadcasted_iota(jnp.int32, (rows, rows), 1)
    per = rows // quarters
    return ((out % per) * quarters + out // per == src).astype(BF16)


def start(copies, src, dst, sems):
    copies.append(pltpu.make_async_copy(src, dst, sems.at[len(copies)]))
    copies[-1].start()
    return copies[-1]


def pieces(own, others):
    right, far_a, far_b, left = others
    rows = own.shape[0]
    half = rows // 2
    return [(own, 0, 0, rows), (right, 1, 0, rows), (far_a, 2, 0, half), (far_b, 2, half, half), (left, 3, 0, rows)]


def hidden_kernel(quarters, me_ref, recv_ref, *refs):
    ups, refs = pieces(refs[0], refs[1:5]), refs[5:]
    to_gate, to_up, g_ref, *blocks, recv, w, x_ref, hid_ref, sems = refs
    rows = 256
    per = rows // quarters
    feat = recv.shape[1] // 2
    hidden_units = hid_ref.shape[1]
    tile = 256
    started = []
    came, columns = [], []
    for b in range(recv.shape[0] // rows):
        here = pl.ds(b * rows, rows)
        came.append(start(started, recv_ref.at[here, :], recv.at[here, :], sems))
    for n in range(hidden_units // tile):
        some = []
        for at in (n * tile, hidden_units + n * tile):
            for ref, block, row, size in ups:
                to = w.at[pl.ds(block * feat + row, size), pl.ds(at, tile)]
                some.append(start(started, ref.at[:, pl.ds(at, tile)], to, sems))
        columns.append(some)
    order = order_matrix(rows, quarters)
    for b in range(recv.shape[0] // rows):
        came[b].wait()
        got = jnp.dot(order, recv[b * rows : b * rows + rows, :], preferred_element_type=F32).astype(BF16)
        here = slice(b * per, b * per + per)
        for q in range(quarters):
            at = pl.multiple_of(lax.rem(q + quarters - me_ref[0], quarters) * feat, feat)
            x_ref[here, pl.ds(at, feat)] = got[q * per : q * per + per, :feat]
            g_ref[here, pl.ds(at, feat)] = got[q * per : q * per + per, feat:]
    for n in range(hidden_units // tile):
        for copy in columns[n]:
            copy.wait()
        cols = slice(n * tile, n * tile + tile)
        up_cols = slice(hidden_units + n * tile, hidden_units + n * tile + tile)
        gate = jnp.dot(x_ref[...], w[:, cols], preferred_element_type=F32)
        up = jnp.dot(x_ref[...], w[:, up_cols], preferred_element_type=F32)
        sig = jax.nn.sigmoid(gate)
        activ = gate * sig
        to_gate[:, cols] = up * sig * (1.0 + gate * (1.0 - sig))
        to_up[:, cols] = activ
        hid_ref[:, cols] = (activ * up).astype(BF16)
    for k, ref in enumerate(blocks):
        ref[...] = lax.dot_general(
            hid_ref[...], g_ref[:, k * feat : k * feat + feat], TN, preferred_element_type=F32
        ).astype(BF16)


def back_kernel(quarters, me_ref, to_gate, to_up, g, *refs):
    ups, (own_ref, right, far_a, far_b, left), (back_ref, gp_ref, hold, out, own, sems) = refs[:5], refs[5:10], refs[10:]
    started = []
    fetch = start(started, own_ref, own, sems)
    hidden_units = to_gate.shape[1]
    feat = out.shape[1]
    half = hidden_units // 2

    def product(h, k, w):
        return lax.dot_general(g[:, k * feat : k * feat + feat], w, NT, preferred_element_type=F32)

    sums = []
    for h, far in enumerate((far_a, far_b)):
        cols = slice(h * half, h * half + half)
        sums.append(product(h, 1, right[cols, :]) + product(h, 2, far[...]) + product(h, 3, left[cols, :]))
    fetch.wait()
    for h, total in enumerate(sums):
        cols = slice(h * half, h * half + half)
        total = total + product(h, 0, own[cols, :])
        gp_ref[:, cols] = (total * to_gate[:, cols]).astype(BF16)
        gp_ref[:, hidden_units + h * half : hidden_units + h * half + half] = (total * to_up[:, cols]).astype(BF16)
    at = 0
    for w in ups:
        size = w.shape[0]
        hold[lax.rem(me_ref[0] + at // feat, quarters), :, at % feat : at % feat + size] = lax.dot_general(
            gp_ref[...], w[...], NT, preferred_element_type=F32
        ).astype(BF16)
        at += size
    rows = 256
    per = rows // quarters
    order = order_matrix(rows, quarters)
    copies = []
    for b in range(back_ref.shape[0] // rows):
        here = pl.ds(b * rows, rows)
        stacked = jnp.concatenate([hold[q, b * per : b * per + per, :] for q in range(quarters)], axis=0)
        out[here, :] = lax.dot_general(order, stacked, TN, preferred_element_type=F32).astype(BF16)
        copies.append(start(started, out.at[here, :], back_ref.at[here, :], sems))
    for copy in copies:
        copy.wait()


def combine_kernel(toks, pick_ref, ret_ref, out_ref):
    feat = ret_ref.shape[1]
    total = lax.dot_general(pick_ref[...], ret_ref[...], TN, preferred_element_type=F32)
    for q in range(out_ref.shape[1] // feat):
        out_ref[:, q * feat : q * feat + feat] = total[q * toks : q * toks + toks].astype(BF16)


def ring(size, step):
    return [(i, (i + step) % size) for i in range(size)]


def pass_on(a, b):
    return pl.pallas_call(
        lambda *refs: None,
        in_specs=[whole(pl.ANY)] * 2,
        out_specs=[whole(pl.ANY)] * 2,
        out_shape=[jax.ShapeDtypeStruct(a.shape, a.dtype)] * 2,
        input_output_aliases={0: 0, 1: 1},
        compiler_params=pltpu.CompilerParams(vmem_limit_bytes=VMEM_LIMIT),
        cost_estimate=pl.CostEstimate(flops=COST, bytes_accessed=0, transcendentals=0),
        name="pass_on",
    )(a, b)


def gather_two_steps(up, down, size):
    fwd, bwd = ring(size, 1), ring(size, -1)
    left_up, right_up = pass_on(lax.ppermute(up, "edp", fwd), lax.ppermute(up, "edp", bwd))
    left_down, right_down = lax.ppermute(down, "edp", fwd), lax.ppermute(down, "edp", bwd)
    out = []
    for left, right in ((left_up, right_up), (left_down, right_down)):
        half = left.shape[0] // 2
        out += [right, lax.ppermute(left[:half], "edp", fwd), lax.ppermute(right[half:], "edp", bwd), left]
    return out


def add_kernel(block, came, out):
    out[...] = (block[...].astype(F32) + came[...].astype(F32)).astype(BF16)


def scatter_two_steps(blocks, size):
    own, right, far, left = blocks
    came = lax.ppermute(far, "edp", ring(size, 1))
    right = pl.pallas_call(
        add_kernel,
        in_specs=[whole()] * 2,
        out_specs=whole(),
        out_shape=jax.ShapeDtypeStruct(right.shape, BF16),
        compiler_params=pltpu.CompilerParams(vmem_limit_bytes=VMEM_LIMIT),
        cost_estimate=pl.CostEstimate(flops=ADD_COST, bytes_accessed=0, transcendentals=0),
        name="add_far",
    )(right, came)
    from_left, from_right = lax.ppermute(right, "edp", ring(size, 1)), lax.ppermute(left, "edp", ring(size, -1))
    return (own.astype(F32) + from_left.astype(F32) + from_right.astype(F32)).astype(BF16)


def per_device(tokens, out_grad, expert_ids, gate_values, gate_up_weight, down_weight):
    experts, parts = lax.axis_size("ep"), lax.axis_size("edp")
    toks, width = tokens.shape
    hidden_units = down_weight.shape[1]
    quarters = 4
    feat = width // quarters
    slots = experts * 2
    rows = slots * quarters
    params = pltpu.CompilerParams(vmem_limit_bytes=VMEM_LIMIT)
    me = lax.axis_index("edp").astype(jnp.int32).reshape(1)

    others = gather_two_steps(gate_up_weight[0], down_weight[0], parts)

    tile = 512
    sent, pick = pl.pallas_call(
        functools.partial(send_kernel, quarters),
        grid=(rows // tile,),
        in_specs=[whole()] * 4,
        out_specs=[
            pl.BlockSpec((tile, 2 * feat), lambda b: (b, 0)),
            pl.BlockSpec((tile, quarters * toks), lambda b: (b, 0)),
        ],
        out_shape=[
            jax.ShapeDtypeStruct((rows, 2 * feat), BF16),
            jax.ShapeDtypeStruct((rows, quarters * toks), BF16),
        ],
        scratch_shapes=[pltpu.VMEM((quarters * toks, 3 * feat), F32)],
        compiler_params=pltpu.CompilerParams(vmem_limit_bytes=SEND_LIMIT),
        name="send_rows",
    )(expert_ids.T, gate_values.T, tokens, out_grad)
    recv = lax.all_to_all(sent, "ep", split_axis=0, concat_axis=0, tiled=True)

    large = pltpu.CompilerParams(vmem_limit_bytes=HIDDEN_LIMIT)
    to_gate, to_up, rows_g, *blocks = pl.pallas_call(
        functools.partial(hidden_kernel, quarters),
        in_specs=[whole(pltpu.SMEM)] + [whole(pl.ANY)] * 6,
        out_specs=[whole()] * (3 + parts),
        out_shape=[jax.ShapeDtypeStruct((slots, hidden_units), F32)] * 2
        + [jax.ShapeDtypeStruct((slots, width), BF16)]
        + [jax.ShapeDtypeStruct((hidden_units, feat), BF16)] * parts,
        scratch_shapes=[
            pltpu.VMEM((rows, 2 * feat), BF16),
            pltpu.VMEM((width, 2 * hidden_units), BF16),
            pltpu.VMEM((slots, width), BF16),
            pltpu.VMEM((slots, hidden_units), BF16),
            pltpu.SemaphoreType.DMA((48,)),
        ],
        compiler_params=large,
        name="hidden_rows",
    )(me, recv, gate_up_weight[0], *others[:4])
    down_grad = scatter_two_steps(blocks, parts)[None]

    back = pl.pallas_call(
        functools.partial(back_kernel, quarters),
        in_specs=[whole(pltpu.SMEM)] + [whole()] * 8 + [whole(pl.ANY)] + [whole()] * 4,
        out_specs=whole(pl.ANY),
        out_shape=jax.ShapeDtypeStruct((rows, feat), BF16),
        scratch_shapes=[
            pltpu.VMEM((slots, 2 * hidden_units), BF16),
            pltpu.VMEM((quarters, slots, feat), BF16),
            pltpu.VMEM((rows, feat), BF16),
            pltpu.VMEM((hidden_units, feat), BF16),
            pltpu.SemaphoreType.DMA((8,)),
        ],
        compiler_params=pltpu.CompilerParams(vmem_limit_bytes=BACK_LIMIT),
        cost_estimate=pl.CostEstimate(flops=COST, bytes_accessed=0, transcendentals=0),
        name="back_rows",
    )(me, to_gate, to_up, rows_g, gate_up_weight[0], *others[:4], down_weight[0], *others[4:])
    returned = lax.all_to_all(back, "ep", split_axis=0, concat_axis=0, tiled=True)
    token_grads = pl.pallas_call(
        functools.partial(combine_kernel, toks),
        in_specs=[whole(), whole()],
        out_specs=whole(),
        out_shape=jax.ShapeDtypeStruct((toks, width), BF16),
        compiler_params=params,
        name="combine_rows",
    )(pick, returned)
    return (token_grads, down_grad)


def solution(mesh):
    return jax.shard_map(
        per_device,
        mesh=mesh,
        in_specs=(
            P(("ep", "edp"), None),
            P(("ep", "edp"), None),
            P(("ep", "edp"), None),
            P(("ep", "edp"), None),
            P("ep", "edp", None),
            P("ep", None, "edp"),
        ),
        out_specs=(P(("ep", "edp"), None), P("ep", None, "edp")),
        check_vma=False,
    )
```

```python
import functools

import jax
import jax.numpy as jnp
from jax import lax
from jax.experimental import pallas as pl
from jax.experimental.pallas import tpu as pltpu
from jax.sharding import PartitionSpec as P

EPSILON = 1e-06
F32, BF16 = jnp.float32, jnp.bfloat16
NT = (((1,), (1,)), ((), ()))
TN = (((0,), (0,)), ((), ()))
VMEM_LIMIT = 16 * 1024 * 1024
BACK_LIMIT = 16 * 1024 * 1024
HIDDEN_LIMIT = 40 * 1024 * 1024
SEND_LIMIT = 56 * 1024 * 1024
COST = 20 * 10**9
ADD_COST = 8 * 10**9


def whole(memory_space=pltpu.VMEM):
    return pl.BlockSpec(memory_space=memory_space)


def rebuild(value, top):
    scale = (top + EPSILON).astype(BF16).astype(F32)
    return ((value / scale).astype(BF16).astype(F32) * scale).astype(BF16)


def send_kernel(quarters, ids_ref, gate_ref, tok_ref, grad_ref, send_ref, pick_ref, stack):
    block = pl.program_id(0)
    rows = send_ref.shape[0]
    toks, width = tok_ref.shape
    lanes = quarters * toks
    feat = width // quarters

    @pl.when(block == 0)
    def _():
        for q in range(quarters):
            here = pl.ds(q * toks, toks)
            for g in range(feat // 128):
                cols = slice(q * feat + g * 128, q * feat + g * 128 + 128)
                value = tok_ref[:, cols].astype(F32)
                top = jnp.max(jnp.abs(value), axis=1, keepdims=True)
                stack[here, pl.ds(g * 128, 128)] = rebuild(value, top).astype(F32)
            grads = grad_ref[:, q * feat : q * feat + feat].astype(F32)
            stack[here, pl.ds(feat, feat)] = grads
            for g in range(feat // 128):
                top = jnp.max(jnp.abs(grads[:, g * 128 : g * 128 + 128]), axis=1, keepdims=True)
                stack[here, pl.ds(2 * feat + g * 128, 128)] = jnp.broadcast_to(top, (toks, 128))

    row = lax.broadcasted_iota(jnp.int32, (rows, lanes), 0) + block * rows
    lane = lax.broadcasted_iota(jnp.int32, (rows, lanes), 1)
    expert, slot, quarter = row >> 3, (row >> 2) & 1, row & 3
    ids = jnp.concatenate([ids_ref[...]] * quarters, axis=1)
    gates = jnp.concatenate([gate_ref[...]] * quarters, axis=1)
    named = jnp.zeros((rows, lanes), F32)
    weight = jnp.zeros((rows, lanes), F32)
    for k in range(ids_ref.shape[0]):
        hit = ids[k : k + 1, :] == expert
        named = jnp.where(hit, 1.0, named)
        weight = jnp.where(hit, gates[k : k + 1, :], weight)
    above = lax.broadcasted_iota(jnp.int32, (lanes, lanes), 0)
    below = lax.broadcasted_iota(jnp.int32, (lanes, lanes), 1)
    earlier = (above < below) & (above // toks == below // toks)
    rank = jnp.dot(named.astype(BF16), earlier.astype(BF16), preferred_element_type=F32)
    chosen = (named > 0.5) & (rank == slot.astype(F32)) & (lane // toks == quarter)
    pick = jnp.where(chosen, 1.0, 0.0).astype(BF16)
    pick_ref[...] = pick
    send_ref[:, :feat] = jnp.dot(pick, stack[:, :feat].astype(BF16), preferred_element_type=F32).astype(BF16)
    gate = jnp.sum(jnp.where(chosen, weight, 0.0), axis=1, keepdims=True)
    grads = jnp.dot(pick, stack[:, feat : 2 * feat].astype(BF16), preferred_element_type=F32) * gate
    top = jnp.dot(pick, stack[:, 2 * feat :].astype(BF16), preferred_element_type=F32) * gate
    send_ref[:, feat:] = rebuild(grads, top)


def order_matrix(rows, quarters):
    out = lax.broadcasted_iota(jnp.int32, (rows, rows), 0)
    src = lax.broadcasted_iota(jnp.int32, (rows, rows), 1)
    per = rows // quarters
    return ((out % per) * quarters + out // per == src).astype(BF16)


def start(copies, src, dst, sems):
    copies.append(pltpu.make_async_copy(src, dst, sems.at[len(copies)]))
    copies[-1].start()
    return copies[-1]


def pieces(own, others):
    right, far_a, far_b, left = others
    rows = own.shape[0]
    half = rows // 2
    return [(own, 0, 0, rows), (right, 1, 0, rows), (far_a, 2, 0, half), (far_b, 2, half, half), (left, 3, 0, rows)]


def hidden_kernel(quarters, me_ref, recv_ref, *refs):
    ups, refs = pieces(refs[0], refs[1:5]), refs[5:]
    to_gate, to_up, g_ref, *blocks, recv, w, x_ref, hid_ref, sems = refs
    rows = 256
    per = rows // quarters
    feat = recv.shape[1] // 2
    hidden_units = hid_ref.shape[1]
    tile = 256
    started = []
    came, columns = [], []
    for b in range(recv.shape[0] // rows):
        here = pl.ds(b * rows, rows)
        came.append(start(started, recv_ref.at[here, :], recv.at[here, :], sems))
    for n in range(hidden_units // tile):
        some = []
        for at in (n * tile, hidden_units + n * tile):
            for ref, block, row, size in ups:
                to = w.at[pl.ds(block * feat + row, size), pl.ds(at, tile)]
                some.append(start(started, ref.at[:, pl.ds(at, tile)], to, sems))
        columns.append(some)
    order = order_matrix(rows, quarters)
    for b in range(recv.shape[0] // rows):
        came[b].wait()
        got = jnp.dot(order, recv[b * rows : b * rows + rows, :], preferred_element_type=F32).astype(BF16)
        here = slice(b * per, b * per + per)
        for q in range(quarters):
            at = pl.multiple_of(lax.rem(q + quarters - me_ref[0], quarters) * feat, feat)
            x_ref[here, pl.ds(at, feat)] = got[q * per : q * per + per, :feat]
            g_ref[here, pl.ds(at, feat)] = got[q * per : q * per + per, feat:]
    for n in range(hidden_units // tile):
        for copy in columns[n]:
            copy.wait()
        cols = slice(n * tile, n * tile + tile)
        up_cols = slice(hidden_units + n * tile, hidden_units + n * tile + tile)
        gate = jnp.dot(x_ref[...], w[:, cols], preferred_element_type=F32)
        up = jnp.dot(x_ref[...], w[:, up_cols], preferred_element_type=F32)
        sig = jax.nn.sigmoid(gate)
        activ = gate * sig
        to_gate[:, cols] = up * sig * (1.0 + gate * (1.0 - sig))
        to_up[:, cols] = activ
        hid_ref[:, cols] = (activ * up).astype(BF16)
    for k, ref in enumerate(blocks):
        ref[...] = lax.dot_general(
            hid_ref[...], g_ref[:, k * feat : k * feat + feat], TN, preferred_element_type=F32
        ).astype(BF16)


def back_kernel(quarters, me_ref, to_gate, to_up, g, *refs):
    ups, (own_ref, right, far_a, far_b, left), (back_ref, gp_ref, hold, out, own, sems) = refs[:5], refs[5:10], refs[10:]
    started = []
    fetch = start(started, own_ref, own, sems)
    hidden_units = to_gate.shape[1]
    feat = out.shape[1]
    half = hidden_units // 2

    def product(h, k, w):
        return lax.dot_general(g[:, k * feat : k * feat + feat], w, NT, preferred_element_type=F32)

    sums = []
    for h, far in enumerate((far_a, far_b)):
        cols = slice(h * half, h * half + half)
        sums.append(product(h, 1, right[cols, :]) + product(h, 2, far[...]) + product(h, 3, left[cols, :]))
    fetch.wait()
    for h, total in enumerate(sums):
        cols = slice(h * half, h * half + half)
        total = total + product(h, 0, own[cols, :])
        gp_ref[:, cols] = (total * to_gate[:, cols]).astype(BF16)
        gp_ref[:, hidden_units + h * half : hidden_units + h * half + half] = (total * to_up[:, cols]).astype(BF16)
    at = 0
    for w in ups:
        size = w.shape[0]
        hold[lax.rem(me_ref[0] + at // feat, quarters), :, at % feat : at % feat + size] = lax.dot_general(
            gp_ref[...], w[...], NT, preferred_element_type=F32
        ).astype(BF16)
        at += size
    rows = 256
    per = rows // quarters
    order = order_matrix(rows, quarters)
    copies = []
    for b in range(back_ref.shape[0] // rows):
        here = pl.ds(b * rows, rows)
        stacked = jnp.concatenate([hold[q, b * per : b * per + per, :] for q in range(quarters)], axis=0)
        out[here, :] = lax.dot_general(order, stacked, TN, preferred_element_type=F32).astype(BF16)
        copies.append(start(started, out.at[here, :], back_ref.at[here, :], sems))
    for copy in copies:
        copy.wait()


def combine_kernel(toks, pick_ref, ret_ref, out_ref):
    feat = ret_ref.shape[1]
    total = lax.dot_general(pick_ref[...], ret_ref[...], TN, preferred_element_type=F32)
    for q in range(out_ref.shape[1] // feat):
        out_ref[:, q * feat : q * feat + feat] = total[q * toks : q * toks + toks].astype(BF16)


def ring(size, step):
    return [(i, (i + step) % size) for i in range(size)]


def hand_on_kernel(left, right, left_out, right_out, top, bottom, sems):
    half = top.shape[0]
    copies = []
    start(copies, left.at[pl.ds(0, half), :], top, sems)
    start(copies, right.at[pl.ds(half, half), :], bottom, sems)
    for copy in copies:
        copy.wait()


def hand_on(left, right):
    half = jax.ShapeDtypeStruct((left.shape[0] // 2, left.shape[1]), left.dtype)
    return pl.pallas_call(
        hand_on_kernel,
        in_specs=[whole(pl.ANY)] * 2,
        out_specs=[whole(pl.ANY)] * 2 + [whole()] * 2,
        out_shape=[jax.ShapeDtypeStruct(left.shape, left.dtype)] * 2 + [half] * 2,
        input_output_aliases={0: 0, 1: 1},
        scratch_shapes=[pltpu.SemaphoreType.DMA((2,))],
        compiler_params=pltpu.CompilerParams(vmem_limit_bytes=VMEM_LIMIT),
        cost_estimate=pl.CostEstimate(flops=COST, bytes_accessed=0, transcendentals=0),
        name="hand_on",
    )(left, right)


def gather_two_steps(up, down, size):
    fwd, bwd = ring(size, 1), ring(size, -1)
    left_up, right_up, up_top, up_bottom = hand_on(lax.ppermute(up, "edp", fwd), lax.ppermute(up, "edp", bwd))
    left_down, right_down = lax.ppermute(down, "edp", fwd), lax.ppermute(down, "edp", bwd)
    half = down.shape[0] // 2
    far_up = [lax.ppermute(up_top, "edp", fwd), lax.ppermute(up_bottom, "edp", bwd)]
    far_down = [lax.ppermute(left_down[:half], "edp", fwd), lax.ppermute(right_down[half:], "edp", bwd)]
    return [right_up, *far_up, left_up], [right_down, *far_down, left_down]


def add_kernel(block, came, out):
    out[...] = (block[...].astype(F32) + came[...].astype(F32)).astype(BF16)


def scatter_two_steps(blocks, size):
    own, right, far, left = blocks
    came = lax.ppermute(far, "edp", ring(size, 1))
    right = pl.pallas_call(
        add_kernel,
        in_specs=[whole()] * 2,
        out_specs=whole(),
        out_shape=jax.ShapeDtypeStruct(right.shape, BF16),
        compiler_params=pltpu.CompilerParams(vmem_limit_bytes=VMEM_LIMIT),
        cost_estimate=pl.CostEstimate(flops=ADD_COST, bytes_accessed=0, transcendentals=0),
        name="add_far",
    )(right, came)
    from_left, from_right = lax.ppermute(right, "edp", ring(size, 1)), lax.ppermute(left, "edp", ring(size, -1))
    return (own.astype(F32) + from_left.astype(F32) + from_right.astype(F32)).astype(BF16)


def per_device(tokens, out_grad, expert_ids, gate_values, gate_up_weight, down_weight):
    experts, parts = lax.axis_size("ep"), lax.axis_size("edp")
    toks, width = tokens.shape
    hidden_units = down_weight.shape[1]
    quarters = 4
    feat = width // quarters
    slots = experts * 2
    rows = slots * quarters
    params = pltpu.CompilerParams(vmem_limit_bytes=VMEM_LIMIT)
    me = lax.axis_index("edp").astype(jnp.int32).reshape(1)

    ups, downs = gather_two_steps(gate_up_weight[0], down_weight[0], parts)

    tile = 512
    sent, pick = pl.pallas_call(
        functools.partial(send_kernel, quarters),
        grid=(rows // tile,),
        in_specs=[whole()] * 4,
        out_specs=[
            pl.BlockSpec((tile, 2 * feat), lambda b: (b, 0)),
            pl.BlockSpec((tile, quarters * toks), lambda b: (b, 0)),
        ],
        out_shape=[
            jax.ShapeDtypeStruct((rows, 2 * feat), BF16),
            jax.ShapeDtypeStruct((rows, quarters * toks), BF16),
        ],
        scratch_shapes=[pltpu.VMEM((quarters * toks, 3 * feat), F32)],
        compiler_params=pltpu.CompilerParams(vmem_limit_bytes=SEND_LIMIT),
        name="send_rows",
    )(expert_ids.T, gate_values.T, tokens, out_grad)
    recv = lax.all_to_all(sent, "ep", split_axis=0, concat_axis=0, tiled=True)

    large = pltpu.CompilerParams(vmem_limit_bytes=HIDDEN_LIMIT)
    to_gate, to_up, rows_g, *blocks = pl.pallas_call(
        functools.partial(hidden_kernel, quarters),
        in_specs=[whole(pltpu.SMEM)] + [whole(pl.ANY)] * 6,
        out_specs=[whole()] * (3 + parts),
        out_shape=[jax.ShapeDtypeStruct((slots, hidden_units), F32)] * 2
        + [jax.ShapeDtypeStruct((slots, width), BF16)]
        + [jax.ShapeDtypeStruct((hidden_units, feat), BF16)] * parts,
        scratch_shapes=[
            pltpu.VMEM((rows, 2 * feat), BF16),
            pltpu.VMEM((width, 2 * hidden_units), BF16),
            pltpu.VMEM((slots, width), BF16),
            pltpu.VMEM((slots, hidden_units), BF16),
            pltpu.SemaphoreType.DMA((48,)),
        ],
        compiler_params=large,
        name="hidden_rows",
    )(me, recv, gate_up_weight[0], *ups)
    down_grad = scatter_two_steps(blocks, parts)[None]

    back = pl.pallas_call(
        functools.partial(back_kernel, quarters),
        in_specs=[whole(pltpu.SMEM)] + [whole()] * 8 + [whole(pl.ANY)] + [whole()] * 4,
        out_specs=whole(pl.ANY),
        out_shape=jax.ShapeDtypeStruct((rows, feat), BF16),
        scratch_shapes=[
            pltpu.VMEM((slots, 2 * hidden_units), BF16),
            pltpu.VMEM((quarters, slots, feat), BF16),
            pltpu.VMEM((rows, feat), BF16),
            pltpu.VMEM((hidden_units, feat), BF16),
            pltpu.SemaphoreType.DMA((8,)),
        ],
        compiler_params=pltpu.CompilerParams(vmem_limit_bytes=BACK_LIMIT),
        cost_estimate=pl.CostEstimate(flops=COST, bytes_accessed=0, transcendentals=0),
        name="back_rows",
    )(me, to_gate, to_up, rows_g, gate_up_weight[0], *ups, down_weight[0], *downs)
    returned = lax.all_to_all(back, "ep", split_axis=0, concat_axis=0, tiled=True)
    token_grads = pl.pallas_call(
        functools.partial(combine_kernel, toks),
        in_specs=[whole(), whole()],
        out_specs=whole(),
        out_shape=jax.ShapeDtypeStruct((toks, width), BF16),
        compiler_params=params,
        name="combine_rows",
    )(pick, returned)
    return (token_grads, down_grad)


def solution(mesh):
    return jax.shard_map(
        per_device,
        mesh=mesh,
        in_specs=(
            P(("ep", "edp"), None),
            P(("ep", "edp"), None),
            P(("ep", "edp"), None),
            P(("ep", "edp"), None),
            P("ep", "edp", None),
            P("ep", None, "edp"),
        ),
        out_specs=(P(("ep", "edp"), None), P("ep", None, "edp")),
        check_vma=False,
    )
```

```python
import functools

import jax
import jax.numpy as jnp
from jax import lax
from jax.experimental import pallas as pl
from jax.experimental.pallas import tpu as pltpu
from jax.sharding import PartitionSpec as P

EPSILON = 1e-06
F32, BF16 = jnp.float32, jnp.bfloat16
NT = (((1,), (1,)), ((), ()))
TN = (((0,), (0,)), ((), ()))
VMEM_LIMIT = 16 * 1024 * 1024
BACK_LIMIT = 16 * 1024 * 1024
UNPACK_COST = 7 * 10**9
HIDDEN_LIMIT = 32 * 1024 * 1024
SEND_LIMIT = 56 * 1024 * 1024
COST = 30 * 10**9
ADD_COST = 8 * 10**9


def whole(memory_space=pltpu.VMEM):
    return pl.BlockSpec(memory_space=memory_space)


def rebuild(value, top):
    scale = (top + EPSILON).astype(BF16).astype(F32)
    return ((value / scale).astype(BF16).astype(F32) * scale).astype(BF16)


def send_kernel(quarters, ids_ref, gate_ref, tok_ref, grad_ref, send_ref, pick_ref, stack):
    block = pl.program_id(0)
    rows = send_ref.shape[0]
    toks, width = tok_ref.shape
    lanes = quarters * toks
    feat = width // quarters

    @pl.when(block == 0)
    def _():
        for q in range(quarters):
            here = pl.ds(q * toks, toks)
            for g in range(feat // 128):
                cols = slice(q * feat + g * 128, q * feat + g * 128 + 128)
                value = tok_ref[:, cols].astype(F32)
                top = jnp.max(jnp.abs(value), axis=1, keepdims=True)
                stack[here, pl.ds(g * 128, 128)] = rebuild(value, top).astype(F32)
            grads = grad_ref[:, q * feat : q * feat + feat].astype(F32)
            stack[here, pl.ds(feat, feat)] = grads
            for g in range(feat // 128):
                top = jnp.max(jnp.abs(grads[:, g * 128 : g * 128 + 128]), axis=1, keepdims=True)
                stack[here, pl.ds(2 * feat + g * 128, 128)] = jnp.broadcast_to(top, (toks, 128))

    row = lax.broadcasted_iota(jnp.int32, (rows, lanes), 0) + block * rows
    lane = lax.broadcasted_iota(jnp.int32, (rows, lanes), 1)
    expert, slot, quarter = row >> 3, (row >> 2) & 1, row & 3
    ids = jnp.concatenate([ids_ref[...]] * quarters, axis=1)
    gates = jnp.concatenate([gate_ref[...]] * quarters, axis=1)
    named = jnp.zeros((rows, lanes), F32)
    weight = jnp.zeros((rows, lanes), F32)
    for k in range(ids_ref.shape[0]):
        hit = ids[k : k + 1, :] == expert
        named = jnp.where(hit, 1.0, named)
        weight = jnp.where(hit, gates[k : k + 1, :], weight)
    above = lax.broadcasted_iota(jnp.int32, (lanes, lanes), 0)
    below = lax.broadcasted_iota(jnp.int32, (lanes, lanes), 1)
    earlier = (above < below) & (above // toks == below // toks)
    rank = jnp.dot(named.astype(BF16), earlier.astype(BF16), preferred_element_type=F32)
    chosen = (named > 0.5) & (rank == slot.astype(F32)) & (lane // toks == quarter)
    pick = jnp.where(chosen, 1.0, 0.0).astype(BF16)
    pick_ref[...] = pick
    send_ref[:, :feat] = jnp.dot(pick, stack[:, :feat].astype(BF16), preferred_element_type=F32).astype(BF16)
    gate = jnp.sum(jnp.where(chosen, weight, 0.0), axis=1, keepdims=True)
    grads = jnp.dot(pick, stack[:, feat : 2 * feat].astype(BF16), preferred_element_type=F32) * gate
    top = jnp.dot(pick, stack[:, 2 * feat :].astype(BF16), preferred_element_type=F32) * gate
    send_ref[:, feat:] = rebuild(grads, top)


def order_matrix(rows, quarters):
    out = lax.broadcasted_iota(jnp.int32, (rows, rows), 0)
    src = lax.broadcasted_iota(jnp.int32, (rows, rows), 1)
    per = rows // quarters
    return ((out % per) * quarters + out // per == src).astype(BF16)


def start(copies, src, dst, sems):
    copies.append(pltpu.make_async_copy(src, dst, sems.at[len(copies)]))
    copies[-1].start()
    return copies[-1]


def unpack_kernel(quarters, me_ref, recv_ref, x_ref, g_ref, recv, sems):
    rows = 256
    per = rows // quarters
    feat = recv.shape[1] // 2
    started = []
    for b in range(recv.shape[0] // rows):
        here = pl.ds(b * rows, rows)
        start(started, recv_ref.at[here, :], recv.at[here, :], sems)
    order = order_matrix(rows, quarters)
    for b, copy in enumerate(started):
        copy.wait()
        got = jnp.dot(order, recv[b * rows : b * rows + rows, :], preferred_element_type=F32).astype(BF16)
        here = slice(b * per, b * per + per)
        for q in range(quarters):
            at = pl.multiple_of(lax.rem(q + quarters - me_ref[0], quarters) * feat, feat)
            x_ref[here, pl.ds(at, feat)] = got[q * per : q * per + per, :feat]
            g_ref[here, pl.ds(at, feat)] = got[q * per : q * per + per, feat:]


def hidden_kernel(x_ref, g_ref, own_up, right, far_a, far_b, left, own_down_ref, *refs):
    to_gate, to_up, *blocks, own_down, hid_ref, sem = refs
    own_came = pltpu.make_async_copy(own_down_ref, own_down, sem)
    own_came.start()
    feat = g_ref.shape[1] // len(blocks)
    hidden_units = hid_ref.shape[1]
    tile = 256

    def pre(cols):
        total, row = None, 0
        for w in (own_up, right, far_a, far_b, left):
            term = jnp.dot(x_ref[:, row : row + w.shape[0]], w[:, cols], preferred_element_type=F32)
            total, row = term if total is None else total + term, row + w.shape[0]
        return total

    for n in range(hidden_units // tile):
        cols = slice(n * tile, n * tile + tile)
        gate = pre(cols)
        up = pre(slice(hidden_units + n * tile, hidden_units + n * tile + tile))
        sig = jax.nn.sigmoid(gate)
        activ = gate * sig
        to_gate[:, cols] = up * sig * (1.0 + gate * (1.0 - sig))
        to_up[:, cols] = activ
        hid_ref[:, cols] = (activ * up).astype(BF16)
    for k, ref in enumerate(blocks):
        ref[...] = lax.dot_general(
            hid_ref[...], g_ref[:, k * feat : k * feat + feat], TN, preferred_element_type=F32
        ).astype(BF16)
    own_came.wait()


def back_kernel(quarters, me_ref, to_gate, to_up, g, *refs):
    ups, (own, right, far_a, far_b, left), (back_ref, gp_ref, hold, out, sems) = refs[:5], refs[5:10], refs[10:]
    started = []
    hidden_units = to_gate.shape[1]
    feat = out.shape[1]
    half = hidden_units // 2

    def product(h, k, w):
        return lax.dot_general(g[:, k * feat : k * feat + feat], w, NT, preferred_element_type=F32)

    for h, far in enumerate((far_a, far_b)):
        cols = slice(h * half, h * half + half)
        total = product(h, 0, own[cols, :]) + product(h, 1, right[cols, :])
        total = total + product(h, 2, far[...]) + product(h, 3, left[cols, :])
        gp_ref[:, cols] = (total * to_gate[:, cols]).astype(BF16)
        gp_ref[:, hidden_units + h * half : hidden_units + h * half + half] = (total * to_up[:, cols]).astype(BF16)
    at = 0
    for w in ups:
        size = w.shape[0]
        hold[lax.rem(me_ref[0] + at // feat, quarters), :, at % feat : at % feat + size] = lax.dot_general(
            gp_ref[...], w[...], NT, preferred_element_type=F32
        ).astype(BF16)
        at += size
    rows = 256
    per = rows // quarters
    order = order_matrix(rows, quarters)
    copies = []
    for b in range(back_ref.shape[0] // rows):
        here = pl.ds(b * rows, rows)
        stacked = jnp.concatenate([hold[q, b * per : b * per + per, :] for q in range(quarters)], axis=0)
        out[here, :] = lax.dot_general(order, stacked, TN, preferred_element_type=F32).astype(BF16)
        copies.append(start(started, out.at[here, :], back_ref.at[here, :], sems))
    for copy in copies:
        copy.wait()


def combine_kernel(toks, pick_ref, ret_ref, out_ref):
    feat = ret_ref.shape[1]
    total = lax.dot_general(pick_ref[...], ret_ref[...], TN, preferred_element_type=F32)
    for q in range(out_ref.shape[1] // feat):
        out_ref[:, q * feat : q * feat + feat] = total[q * toks : q * toks + toks].astype(BF16)


def ring(size, step):
    return [(i, (i + step) % size) for i in range(size)]


def hand_on_kernel(left, right, left_out, right_out, top, bottom, sems):
    half = top.shape[0]
    copies = []
    start(copies, left.at[pl.ds(0, half), :], top, sems)
    start(copies, right.at[pl.ds(half, half), :], bottom, sems)
    for copy in copies:
        copy.wait()


def hand_on(left, right):
    half = jax.ShapeDtypeStruct((left.shape[0] // 2, left.shape[1]), left.dtype)
    return pl.pallas_call(
        hand_on_kernel,
        in_specs=[whole(pl.ANY)] * 2,
        out_specs=[whole(pl.ANY)] * 2 + [whole()] * 2,
        out_shape=[jax.ShapeDtypeStruct(left.shape, left.dtype)] * 2 + [half] * 2,
        input_output_aliases={0: 0, 1: 1},
        scratch_shapes=[pltpu.SemaphoreType.DMA((2,))],
        compiler_params=pltpu.CompilerParams(vmem_limit_bytes=VMEM_LIMIT),
        cost_estimate=pl.CostEstimate(flops=COST, bytes_accessed=0, transcendentals=0),
        name="hand_on",
    )(left, right)


def gather_two_steps(up, down, size):
    fwd, bwd = ring(size, 1), ring(size, -1)
    left_up, right_up, up_top, up_bottom = hand_on(lax.ppermute(up, "edp", fwd), lax.ppermute(up, "edp", bwd))
    left_down, right_down = lax.ppermute(down, "edp", fwd), lax.ppermute(down, "edp", bwd)
    half = down.shape[0] // 2
    far_up = [lax.ppermute(up_top, "edp", fwd), lax.ppermute(up_bottom, "edp", bwd)]
    far_down = [lax.ppermute(left_down[:half], "edp", fwd), lax.ppermute(right_down[half:], "edp", bwd)]
    return [right_up, *far_up, left_up], [right_down, *far_down, left_down]


def add_kernel(block, came, out):
    out[...] = (block[...].astype(F32) + came[...].astype(F32)).astype(BF16)


def scatter_two_steps(blocks, size):
    own, right, far, left = blocks
    came = lax.ppermute(far, "edp", ring(size, 1))
    right = pl.pallas_call(
        add_kernel,
        in_specs=[whole()] * 2,
        out_specs=whole(),
        out_shape=jax.ShapeDtypeStruct(right.shape, BF16),
        compiler_params=pltpu.CompilerParams(vmem_limit_bytes=VMEM_LIMIT),
        cost_estimate=pl.CostEstimate(flops=ADD_COST, bytes_accessed=0, transcendentals=0),
        name="add_far",
    )(right, came)
    from_left, from_right = lax.ppermute(right, "edp", ring(size, 1)), lax.ppermute(left, "edp", ring(size, -1))
    return (own.astype(F32) + from_left.astype(F32) + from_right.astype(F32)).astype(BF16)


def per_device(tokens, out_grad, expert_ids, gate_values, gate_up_weight, down_weight):
    experts, parts = lax.axis_size("ep"), lax.axis_size("edp")
    toks, width = tokens.shape
    hidden_units = down_weight.shape[1]
    quarters = 4
    feat = width // quarters
    slots = experts * 2
    rows = slots * quarters
    params = pltpu.CompilerParams(vmem_limit_bytes=VMEM_LIMIT)
    me = lax.axis_index("edp").astype(jnp.int32).reshape(1)

    ups, downs = gather_two_steps(gate_up_weight[0], down_weight[0], parts)

    tile = 512
    sent, pick = pl.pallas_call(
        functools.partial(send_kernel, quarters),
        grid=(rows // tile,),
        in_specs=[whole()] * 4,
        out_specs=[
            pl.BlockSpec((tile, 2 * feat), lambda b: (b, 0)),
            pl.BlockSpec((tile, quarters * toks), lambda b: (b, 0)),
        ],
        out_shape=[
            jax.ShapeDtypeStruct((rows, 2 * feat), BF16),
            jax.ShapeDtypeStruct((rows, quarters * toks), BF16),
        ],
        scratch_shapes=[pltpu.VMEM((quarters * toks, 3 * feat), F32)],
        compiler_params=pltpu.CompilerParams(vmem_limit_bytes=SEND_LIMIT),
        name="send_rows",
    )(expert_ids.T, gate_values.T, tokens, out_grad)
    recv = lax.all_to_all(sent, "ep", split_axis=0, concat_axis=0, tiled=True)

    rows_x, rows_g = pl.pallas_call(
        functools.partial(unpack_kernel, quarters),
        in_specs=[whole(pltpu.SMEM), whole(pl.ANY)],
        out_specs=[whole()] * 2,
        out_shape=[jax.ShapeDtypeStruct((slots, width), BF16)] * 2,
        scratch_shapes=[pltpu.VMEM((rows, 2 * feat), BF16), pltpu.SemaphoreType.DMA((4,))],
        compiler_params=params,
        cost_estimate=pl.CostEstimate(flops=UNPACK_COST, bytes_accessed=0, transcendentals=0),
        name="unpack_rows",
    )(me, recv)
    to_gate, to_up, *blocks, own_down = pl.pallas_call(
        hidden_kernel,
        in_specs=[whole()] * 7 + [whole(pl.ANY)],
        out_specs=[whole()] * (3 + parts),
        out_shape=[jax.ShapeDtypeStruct((slots, hidden_units), F32)] * 2
        + [jax.ShapeDtypeStruct((hidden_units, feat), BF16)] * (parts + 1),
        scratch_shapes=[pltpu.VMEM((slots, hidden_units), BF16), pltpu.SemaphoreType.DMA],
        compiler_params=pltpu.CompilerParams(vmem_limit_bytes=HIDDEN_LIMIT),
        name="hidden_rows",
    )(rows_x, rows_g, gate_up_weight[0], *ups, down_weight[0])
    down_grad = scatter_two_steps(blocks, parts)[None]

    back = pl.pallas_call(
        functools.partial(back_kernel, quarters),
        in_specs=[whole(pltpu.SMEM)] + [whole()] * 13,
        out_specs=whole(pl.ANY),
        out_shape=jax.ShapeDtypeStruct((rows, feat), BF16),
        scratch_shapes=[
            pltpu.VMEM((slots, 2 * hidden_units), BF16),
            pltpu.VMEM((quarters, slots, feat), BF16),
            pltpu.VMEM((rows, feat), BF16),
            pltpu.SemaphoreType.DMA((4,)),
        ],
        compiler_params=pltpu.CompilerParams(vmem_limit_bytes=BACK_LIMIT),
        cost_estimate=pl.CostEstimate(flops=COST, bytes_accessed=0, transcendentals=0),
        name="back_rows",
    )(me, to_gate, to_up, rows_g, gate_up_weight[0], *ups, own_down, *downs)
    returned = lax.all_to_all(back, "ep", split_axis=0, concat_axis=0, tiled=True)
    token_grads = pl.pallas_call(
        functools.partial(combine_kernel, toks),
        in_specs=[whole(), whole()],
        out_specs=whole(),
        out_shape=jax.ShapeDtypeStruct((toks, width), BF16),
        compiler_params=params,
        name="combine_rows",
    )(pick, returned)
    return (token_grads, down_grad)


def solution(mesh):
    return jax.shard_map(
        per_device,
        mesh=mesh,
        in_specs=(
            P(("ep", "edp"), None),
            P(("ep", "edp"), None),
            P(("ep", "edp"), None),
            P(("ep", "edp"), None),
            P("ep", "edp", None),
            P("ep", None, "edp"),
        ),
        out_specs=(P(("ep", "edp"), None), P("ep", None, "edp")),
        check_vma=False,
    )
```

```python
import functools

import jax
import jax.numpy as jnp
from jax import lax
from jax.experimental import pallas as pl
from jax.experimental.pallas import tpu as pltpu
from jax.sharding import PartitionSpec as P

EPSILON = 1e-06
F32, BF16 = jnp.float32, jnp.bfloat16
NT = (((1,), (1,)), ((), ()))
TN = (((0,), (0,)), ((), ()))
VMEM_LIMIT = 16 * 1024 * 1024
BACK_LIMIT = 24 * 1024 * 1024
UNPACK_COST = 7 * 10**9
HIDDEN_LIMIT = 32 * 1024 * 1024
SEND_LIMIT = 56 * 1024 * 1024
COST = 30 * 10**9
ADD_COST = 8 * 10**9


def whole(memory_space=pltpu.VMEM):
    return pl.BlockSpec(memory_space=memory_space)


def rebuild(value, top):
    scale = (top + EPSILON).astype(BF16).astype(F32)
    return ((value / scale).astype(BF16).astype(F32) * scale).astype(BF16)


def send_kernel(quarters, ids_ref, gate_ref, tok_ref, grad_ref, send_ref, pick_ref, stack):
    block = pl.program_id(0)
    rows = send_ref.shape[0]
    toks, width = tok_ref.shape
    lanes = quarters * toks
    feat = width // quarters

    @pl.when(block == 0)
    def _():
        for q in range(quarters):
            here = pl.ds(q * toks, toks)
            for g in range(feat // 128):
                cols = slice(q * feat + g * 128, q * feat + g * 128 + 128)
                value = tok_ref[:, cols].astype(F32)
                top = jnp.max(jnp.abs(value), axis=1, keepdims=True)
                stack[here, pl.ds(g * 128, 128)] = rebuild(value, top).astype(F32)
            grads = grad_ref[:, q * feat : q * feat + feat].astype(F32)
            stack[here, pl.ds(feat, feat)] = grads
            for g in range(feat // 128):
                top = jnp.max(jnp.abs(grads[:, g * 128 : g * 128 + 128]), axis=1, keepdims=True)
                stack[here, pl.ds(2 * feat + g * 128, 128)] = jnp.broadcast_to(top, (toks, 128))

    row = lax.broadcasted_iota(jnp.int32, (rows, lanes), 0) + block * rows
    lane = lax.broadcasted_iota(jnp.int32, (rows, lanes), 1)
    expert, slot, quarter = row >> 3, (row >> 2) & 1, row & 3
    ids = jnp.concatenate([ids_ref[...]] * quarters, axis=1)
    gates = jnp.concatenate([gate_ref[...]] * quarters, axis=1)
    named = jnp.zeros((rows, lanes), F32)
    weight = jnp.zeros((rows, lanes), F32)
    for k in range(ids_ref.shape[0]):
        hit = ids[k : k + 1, :] == expert
        named = jnp.where(hit, 1.0, named)
        weight = jnp.where(hit, gates[k : k + 1, :], weight)
    above = lax.broadcasted_iota(jnp.int32, (lanes, lanes), 0)
    below = lax.broadcasted_iota(jnp.int32, (lanes, lanes), 1)
    earlier = (above < below) & (above // toks == below // toks)
    rank = jnp.dot(named.astype(BF16), earlier.astype(BF16), preferred_element_type=F32)
    chosen = (named > 0.5) & (rank == slot.astype(F32)) & (lane // toks == quarter)
    pick = jnp.where(chosen, 1.0, 0.0).astype(BF16)
    pick_ref[...] = pick
    send_ref[:, :feat] = jnp.dot(pick, stack[:, :feat].astype(BF16), preferred_element_type=F32).astype(BF16)
    gate = jnp.sum(jnp.where(chosen, weight, 0.0), axis=1, keepdims=True)
    grads = jnp.dot(pick, stack[:, feat : 2 * feat].astype(BF16), preferred_element_type=F32) * gate
    top = jnp.dot(pick, stack[:, 2 * feat :].astype(BF16), preferred_element_type=F32) * gate
    send_ref[:, feat:] = rebuild(grads, top)


def order_matrix(rows, quarters):
    out = lax.broadcasted_iota(jnp.int32, (rows, rows), 0)
    src = lax.broadcasted_iota(jnp.int32, (rows, rows), 1)
    per = rows // quarters
    return ((out % per) * quarters + out // per == src).astype(BF16)


def start(copies, src, dst, sems):
    copies.append(pltpu.make_async_copy(src, dst, sems.at[len(copies)]))
    copies[-1].start()
    return copies[-1]


def unpack_kernel(quarters, me_ref, recv_ref, x_ref, g_ref, recv, sems):
    rows = 256
    per = rows // quarters
    feat = recv.shape[1] // 2
    started = []
    for b in range(recv.shape[0] // rows):
        here = pl.ds(b * rows, rows)
        start(started, recv_ref.at[here, :], recv.at[here, :], sems)
    order = order_matrix(rows, quarters)
    for b, copy in enumerate(started):
        copy.wait()
        got = jnp.dot(order, recv[b * rows : b * rows + rows, :], preferred_element_type=F32).astype(BF16)
        here = slice(b * per, b * per + per)
        for q in range(quarters):
            at = pl.multiple_of(lax.rem(q + quarters - me_ref[0], quarters) * feat, feat)
            x_ref[here, pl.ds(at, feat)] = got[q * per : q * per + per, :feat]
            g_ref[here, pl.ds(at, feat)] = got[q * per : q * per + per, feat:]


def fetch(refs, holds, sems):
    copies = [pltpu.make_async_copy(ref, hold, sems.at[i]) for i, (ref, hold) in enumerate(zip(refs, holds))]
    for copy in copies:
        copy.start()
    waited = set()

    def get(i):
        if i not in waited:
            waited.add(i)
            copies[i].wait()
        return holds[i]

    return get


def hidden_kernel(x_ref, g_ref, own_up, *refs):
    to_gate, to_up, *blocks, own_down = refs[5:12]
    hid_ref, *holds, sems = refs[12:]
    get = fetch(refs[:5], [*holds, own_down], sems)
    feat = g_ref.shape[1] // len(blocks)
    hidden_units = hid_ref.shape[1]
    tile = 256

    def pre(cols):
        row = own_up.shape[0]
        total = jnp.dot(x_ref[:, :row], own_up[:, cols], preferred_element_type=F32)
        for i in range(len(holds)):
            w = get(i)
            total = total + jnp.dot(x_ref[:, row : row + w.shape[0]], w[:, cols], preferred_element_type=F32)
            row += w.shape[0]
        return total

    for n in range(hidden_units // tile):
        cols = slice(n * tile, n * tile + tile)
        gate = pre(cols)
        up = pre(slice(hidden_units + n * tile, hidden_units + n * tile + tile))
        sig = jax.nn.sigmoid(gate)
        activ = gate * sig
        to_gate[:, cols] = up * sig * (1.0 + gate * (1.0 - sig))
        to_up[:, cols] = activ
        hid_ref[:, cols] = (activ * up).astype(BF16)
    for k, ref in enumerate(blocks):
        ref[...] = lax.dot_general(
            hid_ref[...], g_ref[:, k * feat : k * feat + feat], TN, preferred_element_type=F32
        ).astype(BF16)
    get(len(holds))


def back_kernel(quarters, me_ref, to_gate, to_up, g, *refs):
    own_up, own, others, (back_ref, gp_ref, hold, out, *holds, sems, got_sems) = refs[0], refs[1], refs[2:10], refs[10:]
    get = fetch(others, holds, got_sems)
    started = []
    hidden_units = to_gate.shape[1]
    feat = out.shape[1]
    half = hidden_units // 2

    def product(h, k, w):
        return lax.dot_general(g[:, k * feat : k * feat + feat], w, NT, preferred_element_type=F32)

    sums = [product(h, 0, own[h * half : h * half + half, :]) for h in range(2)]
    for h in range(2):
        cols = slice(h * half, h * half + half)
        total = sums[h] + product(h, 1, get(0)[cols, :])
        total = total + product(h, 2, get(1 + h)[...]) + product(h, 3, get(3)[cols, :])
        gp_ref[:, cols] = (total * to_gate[:, cols]).astype(BF16)
        gp_ref[:, hidden_units + h * half : hidden_units + h * half + half] = (total * to_up[:, cols]).astype(BF16)
    at = 0
    for i in range(5):
        w = get(3 + i) if i else own_up
        size = w.shape[0]
        hold[lax.rem(me_ref[0] + at // feat, quarters), :, at % feat : at % feat + size] = lax.dot_general(
            gp_ref[...], w[...], NT, preferred_element_type=F32
        ).astype(BF16)
        at += size
    rows = 256
    per = rows // quarters
    order = order_matrix(rows, quarters)
    copies = []
    for b in range(back_ref.shape[0] // rows):
        here = pl.ds(b * rows, rows)
        stacked = jnp.concatenate([hold[q, b * per : b * per + per, :] for q in range(quarters)], axis=0)
        out[here, :] = lax.dot_general(order, stacked, TN, preferred_element_type=F32).astype(BF16)
        copies.append(start(started, out.at[here, :], back_ref.at[here, :], sems))
    for copy in copies:
        copy.wait()


def combine_kernel(toks, pick_ref, ret_ref, out_ref):
    feat = ret_ref.shape[1]
    total = lax.dot_general(pick_ref[...], ret_ref[...], TN, preferred_element_type=F32)
    for q in range(out_ref.shape[1] // feat):
        out_ref[:, q * feat : q * feat + feat] = total[q * toks : q * toks + toks].astype(BF16)


def ring(size, step):
    return [(i, (i + step) % size) for i in range(size)]


def hand_on_kernel(left, right, left_out, right_out, top, bottom, sems):
    half = top.shape[0]
    copies = []
    start(copies, left.at[pl.ds(0, half), :], top, sems)
    start(copies, right.at[pl.ds(half, half), :], bottom, sems)
    for copy in copies:
        copy.wait()


def hand_on(left, right):
    half = jax.ShapeDtypeStruct((left.shape[0] // 2, left.shape[1]), left.dtype)
    return pl.pallas_call(
        hand_on_kernel,
        in_specs=[whole(pl.ANY)] * 2,
        out_specs=[whole(pl.ANY)] * 2 + [whole()] * 2,
        out_shape=[jax.ShapeDtypeStruct(left.shape, left.dtype)] * 2 + [half] * 2,
        input_output_aliases={0: 0, 1: 1},
        scratch_shapes=[pltpu.SemaphoreType.DMA((2,))],
        compiler_params=pltpu.CompilerParams(vmem_limit_bytes=VMEM_LIMIT),
        cost_estimate=pl.CostEstimate(flops=COST, bytes_accessed=0, transcendentals=0),
        name="hand_on",
    )(left, right)


def gather_two_steps(up, down, size):
    fwd, bwd = ring(size, 1), ring(size, -1)
    left_up, right_up, up_top, up_bottom = hand_on(lax.ppermute(up, "edp", fwd), lax.ppermute(up, "edp", bwd))
    left_down, right_down = lax.ppermute(down, "edp", fwd), lax.ppermute(down, "edp", bwd)
    half = down.shape[0] // 2
    far_up = [lax.ppermute(up_top, "edp", fwd), lax.ppermute(up_bottom, "edp", bwd)]
    far_down = [lax.ppermute(left_down[:half], "edp", fwd), lax.ppermute(right_down[half:], "edp", bwd)]
    return [right_up, *far_up, left_up], [right_down, *far_down, left_down]


def add_kernel(block, came, out):
    out[...] = (block[...].astype(F32) + came[...].astype(F32)).astype(BF16)


def scatter_two_steps(blocks, size):
    own, right, far, left = blocks
    came = lax.ppermute(far, "edp", ring(size, 1))
    right = pl.pallas_call(
        add_kernel,
        in_specs=[whole()] * 2,
        out_specs=whole(),
        out_shape=jax.ShapeDtypeStruct(right.shape, BF16),
        compiler_params=pltpu.CompilerParams(vmem_limit_bytes=VMEM_LIMIT),
        cost_estimate=pl.CostEstimate(flops=ADD_COST, bytes_accessed=0, transcendentals=0),
        name="add_far",
    )(right, came)
    from_left, from_right = lax.ppermute(right, "edp", ring(size, 1)), lax.ppermute(left, "edp", ring(size, -1))
    return (own.astype(F32) + from_left.astype(F32) + from_right.astype(F32)).astype(BF16)


def per_device(tokens, out_grad, expert_ids, gate_values, gate_up_weight, down_weight):
    experts, parts = lax.axis_size("ep"), lax.axis_size("edp")
    toks, width = tokens.shape
    hidden_units = down_weight.shape[1]
    quarters = 4
    feat = width // quarters
    slots = experts * 2
    rows = slots * quarters
    params = pltpu.CompilerParams(vmem_limit_bytes=VMEM_LIMIT)
    me = lax.axis_index("edp").astype(jnp.int32).reshape(1)

    ups, downs = gather_two_steps(gate_up_weight[0], down_weight[0], parts)

    tile = 512
    sent, pick = pl.pallas_call(
        functools.partial(send_kernel, quarters),
        grid=(rows // tile,),
        in_specs=[whole()] * 4,
        out_specs=[
            pl.BlockSpec((tile, 2 * feat), lambda b: (b, 0)),
            pl.BlockSpec((tile, quarters * toks), lambda b: (b, 0)),
        ],
        out_shape=[
            jax.ShapeDtypeStruct((rows, 2 * feat), BF16),
            jax.ShapeDtypeStruct((rows, quarters * toks), BF16),
        ],
        scratch_shapes=[pltpu.VMEM((quarters * toks, 3 * feat), F32)],
        compiler_params=pltpu.CompilerParams(vmem_limit_bytes=SEND_LIMIT),
        name="send_rows",
    )(expert_ids.T, gate_values.T, tokens, out_grad)
    recv = lax.all_to_all(sent, "ep", split_axis=0, concat_axis=0, tiled=True)

    rows_x, rows_g = pl.pallas_call(
        functools.partial(unpack_kernel, quarters),
        in_specs=[whole(pltpu.SMEM), whole(pl.ANY)],
        out_specs=[whole()] * 2,
        out_shape=[jax.ShapeDtypeStruct((slots, width), BF16)] * 2,
        scratch_shapes=[pltpu.VMEM((rows, 2 * feat), BF16), pltpu.SemaphoreType.DMA((4,))],
        compiler_params=params,
        cost_estimate=pl.CostEstimate(flops=UNPACK_COST, bytes_accessed=0, transcendentals=0),
        name="unpack_rows",
    )(me, recv)
    to_gate, to_up, *blocks, own_down = pl.pallas_call(
        hidden_kernel,
        in_specs=[whole()] * 3 + [whole(pl.ANY)] * 5,
        out_specs=[whole()] * (3 + parts),
        out_shape=[jax.ShapeDtypeStruct((slots, hidden_units), F32)] * 2
        + [jax.ShapeDtypeStruct((hidden_units, feat), BF16)] * (parts + 1),
        scratch_shapes=[pltpu.VMEM((slots, hidden_units), BF16)]
        + [pltpu.VMEM(x.shape, BF16) for x in ups]
        + [pltpu.SemaphoreType.DMA((5,))],
        compiler_params=pltpu.CompilerParams(vmem_limit_bytes=HIDDEN_LIMIT),
        name="hidden_rows",
    )(rows_x, rows_g, gate_up_weight[0], *ups, down_weight[0])
    down_grad = scatter_two_steps(blocks, parts)[None]

    back = pl.pallas_call(
        functools.partial(back_kernel, quarters),
        in_specs=[whole(pltpu.SMEM)] + [whole()] * 5 + [whole(pl.ANY)] * 8,
        out_specs=whole(pl.ANY),
        out_shape=jax.ShapeDtypeStruct((rows, feat), BF16),
        scratch_shapes=[
            pltpu.VMEM((slots, 2 * hidden_units), BF16),
            pltpu.VMEM((quarters, slots, feat), BF16),
            pltpu.VMEM((rows, feat), BF16),
        ]
        + [pltpu.VMEM(x.shape, BF16) for x in (*downs, *ups)]
        + [pltpu.SemaphoreType.DMA((4,)), pltpu.SemaphoreType.DMA((8,))],
        compiler_params=pltpu.CompilerParams(vmem_limit_bytes=BACK_LIMIT),
        cost_estimate=pl.CostEstimate(flops=COST, bytes_accessed=0, transcendentals=0),
        name="back_rows",
    )(me, to_gate, to_up, rows_g, gate_up_weight[0], own_down, *downs, *ups)
    returned = lax.all_to_all(back, "ep", split_axis=0, concat_axis=0, tiled=True)
    token_grads = pl.pallas_call(
        functools.partial(combine_kernel, toks),
        in_specs=[whole(), whole()],
        out_specs=whole(),
        out_shape=jax.ShapeDtypeStruct((toks, width), BF16),
        compiler_params=params,
        name="combine_rows",
    )(pick, returned)
    return (token_grads, down_grad)


def solution(mesh):
    return jax.shard_map(
        per_device,
        mesh=mesh,
        in_specs=(
            P(("ep", "edp"), None),
            P(("ep", "edp"), None),
            P(("ep", "edp"), None),
            P(("ep", "edp"), None),
            P("ep", "edp", None),
            P("ep", None, "edp"),
        ),
        out_specs=(P(("ep", "edp"), None), P("ep", None, "edp")),
        check_vma=False,
    )
```

```python
import functools

import jax
import jax.numpy as jnp
from jax import lax
from jax.experimental import pallas as pl
from jax.experimental.pallas import tpu as pltpu
from jax.sharding import PartitionSpec as P

EPSILON = 1e-06
F32, BF16 = jnp.float32, jnp.bfloat16
NT = (((1,), (1,)), ((), ()))
TN = (((0,), (0,)), ((), ()))
VMEM_LIMIT = 16 * 1024 * 1024
BACK_LIMIT = 24 * 1024 * 1024
UNPACK_COST = 7 * 10**9
HIDDEN_LIMIT = 32 * 1024 * 1024
SEND_LIMIT = 56 * 1024 * 1024
COST = 30 * 10**9
ADD_COST = 8 * 10**9


def whole(memory_space=pltpu.VMEM):
    return pl.BlockSpec(memory_space=memory_space)


def rebuild(value, top):
    scale = (top + EPSILON).astype(BF16).astype(F32)
    return ((value / scale).astype(BF16).astype(F32) * scale).astype(BF16)


def send_kernel(quarters, ids_ref, gate_ref, tok_ref, grad_ref, send_ref, pick_ref, stack):
    block = pl.program_id(0)
    rows = send_ref.shape[0]
    toks, width = tok_ref.shape
    lanes = quarters * toks
    feat = width // quarters

    @pl.when(block == 0)
    def _():
        for q in range(quarters):
            here = pl.ds(q * toks, toks)
            for g in range(feat // 128):
                cols = slice(q * feat + g * 128, q * feat + g * 128 + 128)
                value = tok_ref[:, cols].astype(F32)
                top = jnp.max(jnp.abs(value), axis=1, keepdims=True)
                stack[here, pl.ds(g * 128, 128)] = rebuild(value, top).astype(F32)
            grads = grad_ref[:, q * feat : q * feat + feat].astype(F32)
            stack[here, pl.ds(feat, feat)] = grads
            for g in range(feat // 128):
                top = jnp.max(jnp.abs(grads[:, g * 128 : g * 128 + 128]), axis=1, keepdims=True)
                stack[here, pl.ds(2 * feat + g * 128, 128)] = jnp.broadcast_to(top, (toks, 128))

    row = lax.broadcasted_iota(jnp.int32, (rows, lanes), 0) + block * rows
    lane = lax.broadcasted_iota(jnp.int32, (rows, lanes), 1)
    expert, slot, quarter = row >> 3, (row >> 2) & 1, row & 3
    ids = jnp.concatenate([ids_ref[...]] * quarters, axis=1)
    gates = jnp.concatenate([gate_ref[...]] * quarters, axis=1)
    named = jnp.zeros((rows, lanes), F32)
    weight = jnp.zeros((rows, lanes), F32)
    for k in range(ids_ref.shape[0]):
        hit = ids[k : k + 1, :] == expert
        named = jnp.where(hit, 1.0, named)
        weight = jnp.where(hit, gates[k : k + 1, :], weight)
    above = lax.broadcasted_iota(jnp.int32, (lanes, lanes), 0)
    below = lax.broadcasted_iota(jnp.int32, (lanes, lanes), 1)
    earlier = (above < below) & (above // toks == below // toks)
    rank = jnp.dot(named.astype(BF16), earlier.astype(BF16), preferred_element_type=F32)
    chosen = (named > 0.5) & (rank == slot.astype(F32)) & (lane // toks == quarter)
    pick = jnp.where(chosen, 1.0, 0.0).astype(BF16)
    pick_ref[...] = pick
    send_ref[:, :feat] = jnp.dot(pick, stack[:, :feat].astype(BF16), preferred_element_type=F32).astype(BF16)
    gate = jnp.sum(jnp.where(chosen, weight, 0.0), axis=1, keepdims=True)
    grads = jnp.dot(pick, stack[:, feat : 2 * feat].astype(BF16), preferred_element_type=F32) * gate
    top = jnp.dot(pick, stack[:, 2 * feat :].astype(BF16), preferred_element_type=F32) * gate
    send_ref[:, feat:] = rebuild(grads, top)


def order_matrix(rows, quarters):
    out = lax.broadcasted_iota(jnp.int32, (rows, rows), 0)
    src = lax.broadcasted_iota(jnp.int32, (rows, rows), 1)
    per = rows // quarters
    return ((out % per) * quarters + out // per == src).astype(BF16)


def start(copies, src, dst, sems):
    copies.append(pltpu.make_async_copy(src, dst, sems.at[len(copies)]))
    copies[-1].start()
    return copies[-1]


def unpack_kernel(quarters, me_ref, recv_ref, x_ref, g_ref, recv, sems):
    rows = 256
    per = rows // quarters
    feat = recv.shape[1] // 2
    started = []
    for b in range(recv.shape[0] // rows):
        here = pl.ds(b * rows, rows)
        start(started, recv_ref.at[here, :], recv.at[here, :], sems)
    order = order_matrix(rows, quarters)
    for b, copy in enumerate(started):
        copy.wait()
        got = jnp.dot(order, recv[b * rows : b * rows + rows, :], preferred_element_type=F32).astype(BF16)
        here = slice(b * per, b * per + per)
        for q in range(quarters):
            at = pl.multiple_of(lax.rem(q + quarters - me_ref[0], quarters) * feat, feat)
            x_ref[here, pl.ds(at, feat)] = got[q * per : q * per + per, :feat]
            g_ref[here, pl.ds(at, feat)] = got[q * per : q * per + per, feat:]


def fetch(refs, holds, sems):
    copies = [pltpu.make_async_copy(ref, hold, sems.at[i]) for i, (ref, hold) in enumerate(zip(refs, holds))]
    for copy in copies:
        copy.start()
    waited = set()

    def get(i):
        if i not in waited:
            waited.add(i)
            copies[i].wait()
        return holds[i]

    return get


def hidden_kernel(x_ref, g_ref, own_up, *refs):
    given, outs, (pre, hid_ref, sems) = refs[:7], refs[7:20], refs[20:]
    to_gate, to_up, blocks, holds = outs[0], outs[1], outs[2:6], outs[6:]
    get = fetch(given, holds, sems)
    feat = g_ref.shape[1] // len(blocks)
    hidden_units = hid_ref.shape[1]
    tile = 256
    row = 0
    for i in range(5):
        w = get(i - 1) if i else own_up
        rows = slice(row, row + w.shape[0])
        row += w.shape[0]
        for n in range(w.shape[1] // tile):
            cols = slice(n * tile, n * tile + tile)
            term = jnp.dot(x_ref[:, rows], w[:, cols], preferred_element_type=F32)
            pre[:, cols] = pre[:, cols] + term if i else term
    for n in range(hidden_units // tile):
        cols = slice(n * tile, n * tile + tile)
        gate = pre[:, cols]
        up = pre[:, hidden_units + n * tile : hidden_units + n * tile + tile]
        sig = jax.nn.sigmoid(gate)
        activ = gate * sig
        to_gate[:, cols] = up * sig * (1.0 + gate * (1.0 - sig))
        to_up[:, cols] = activ
        hid_ref[:, cols] = (activ * up).astype(BF16)
    for k, ref in enumerate(blocks):
        ref[...] = lax.dot_general(
            hid_ref[...], g_ref[:, k * feat : k * feat + feat], TN, preferred_element_type=F32
        ).astype(BF16)
    for i in range(4, len(holds)):
        get(i)


def back_kernel(quarters, me_ref, to_gate, to_up, g, *refs):
    ups, own, right, left, (far_a, far_b), refs = refs[:5], refs[5], refs[6], refs[7], refs[8:10], refs[10:]
    back_ref, gp_ref, hold, out, *holds, sems, far_sems = refs
    get = fetch((far_a, far_b), holds, far_sems)
    started = []
    hidden_units = to_gate.shape[1]
    feat = out.shape[1]
    half = hidden_units // 2

    def product(h, k, w):
        return lax.dot_general(g[:, k * feat : k * feat + feat], w, NT, preferred_element_type=F32)

    sums = []
    for h in range(2):
        cols = slice(h * half, h * half + half)
        sums.append(product(h, 0, own[cols, :]) + product(h, 1, right[cols, :]) + product(h, 3, left[cols, :]))
    for h in range(2):
        cols = slice(h * half, h * half + half)
        total = sums[h] + product(h, 2, get(h)[...])
        gp_ref[:, cols] = (total * to_gate[:, cols]).astype(BF16)
        gp_ref[:, hidden_units + h * half : hidden_units + h * half + half] = (total * to_up[:, cols]).astype(BF16)
    at = 0
    for w in ups:
        size = w.shape[0]
        hold[lax.rem(me_ref[0] + at // feat, quarters), :, at % feat : at % feat + size] = lax.dot_general(
            gp_ref[...], w[...], NT, preferred_element_type=F32
        ).astype(BF16)
        at += size
    rows = 256
    per = rows // quarters
    order = order_matrix(rows, quarters)
    copies = []
    for b in range(back_ref.shape[0] // rows):
        here = pl.ds(b * rows, rows)
        stacked = jnp.concatenate([hold[q, b * per : b * per + per, :] for q in range(quarters)], axis=0)
        out[here, :] = lax.dot_general(order, stacked, TN, preferred_element_type=F32).astype(BF16)
        copies.append(start(started, out.at[here, :], back_ref.at[here, :], sems))
    for copy in copies:
        copy.wait()


def combine_kernel(toks, pick_ref, ret_ref, out_ref):
    feat = ret_ref.shape[1]
    total = lax.dot_general(pick_ref[...], ret_ref[...], TN, preferred_element_type=F32)
    for q in range(out_ref.shape[1] // feat):
        out_ref[:, q * feat : q * feat + feat] = total[q * toks : q * toks + toks].astype(BF16)


def ring(size, step):
    return [(i, (i + step) % size) for i in range(size)]


def hand_on_kernel(left, right, left_out, right_out, top, bottom, sems):
    half = top.shape[0]
    copies = []
    start(copies, left.at[pl.ds(0, half), :], top, sems)
    start(copies, right.at[pl.ds(half, half), :], bottom, sems)
    for copy in copies:
        copy.wait()


def hand_on(left, right):
    half = jax.ShapeDtypeStruct((left.shape[0] // 2, left.shape[1]), left.dtype)
    return pl.pallas_call(
        hand_on_kernel,
        in_specs=[whole(pl.ANY)] * 2,
        out_specs=[whole(pl.ANY)] * 2 + [whole()] * 2,
        out_shape=[jax.ShapeDtypeStruct(left.shape, left.dtype)] * 2 + [half] * 2,
        input_output_aliases={0: 0, 1: 1},
        scratch_shapes=[pltpu.SemaphoreType.DMA((2,))],
        compiler_params=pltpu.CompilerParams(vmem_limit_bytes=VMEM_LIMIT),
        cost_estimate=pl.CostEstimate(flops=COST, bytes_accessed=0, transcendentals=0),
        name="hand_on",
    )(left, right)


def gather_two_steps(up, down, size):
    fwd, bwd = ring(size, 1), ring(size, -1)
    left_up, right_up, up_top, up_bottom = hand_on(lax.ppermute(up, "edp", fwd), lax.ppermute(up, "edp", bwd))
    left_down, right_down = lax.ppermute(down, "edp", fwd), lax.ppermute(down, "edp", bwd)
    half = down.shape[0] // 2
    far_up = [lax.ppermute(up_top, "edp", fwd), lax.ppermute(up_bottom, "edp", bwd)]
    far_down = [lax.ppermute(left_down[:half], "edp", fwd), lax.ppermute(right_down[half:], "edp", bwd)]
    return [right_up, *far_up, left_up], [right_down, *far_down, left_down]


def add_kernel(block, came, out):
    out[...] = (block[...].astype(F32) + came[...].astype(F32)).astype(BF16)


def scatter_two_steps(blocks, size):
    own, right, far, left = blocks
    came = lax.ppermute(far, "edp", ring(size, 1))
    right = pl.pallas_call(
        add_kernel,
        in_specs=[whole()] * 2,
        out_specs=whole(),
        out_shape=jax.ShapeDtypeStruct(right.shape, BF16),
        compiler_params=pltpu.CompilerParams(vmem_limit_bytes=VMEM_LIMIT),
        cost_estimate=pl.CostEstimate(flops=ADD_COST, bytes_accessed=0, transcendentals=0),
        name="add_far",
    )(right, came)
    from_left, from_right = lax.ppermute(right, "edp", ring(size, 1)), lax.ppermute(left, "edp", ring(size, -1))
    return (own.astype(F32) + from_left.astype(F32) + from_right.astype(F32)).astype(BF16)


def per_device(tokens, out_grad, expert_ids, gate_values, gate_up_weight, down_weight):
    experts, parts = lax.axis_size("ep"), lax.axis_size("edp")
    toks, width = tokens.shape
    hidden_units = down_weight.shape[1]
    quarters = 4
    feat = width // quarters
    slots = experts * 2
    rows = slots * quarters
    params = pltpu.CompilerParams(vmem_limit_bytes=VMEM_LIMIT)
    me = lax.axis_index("edp").astype(jnp.int32).reshape(1)

    ups, downs = gather_two_steps(gate_up_weight[0], down_weight[0], parts)

    tile = 512
    sent, pick = pl.pallas_call(
        functools.partial(send_kernel, quarters),
        grid=(rows // tile,),
        in_specs=[whole()] * 4,
        out_specs=[
            pl.BlockSpec((tile, 2 * feat), lambda b: (b, 0)),
            pl.BlockSpec((tile, quarters * toks), lambda b: (b, 0)),
        ],
        out_shape=[
            jax.ShapeDtypeStruct((rows, 2 * feat), BF16),
            jax.ShapeDtypeStruct((rows, quarters * toks), BF16),
        ],
        scratch_shapes=[pltpu.VMEM((quarters * toks, 3 * feat), F32)],
        compiler_params=pltpu.CompilerParams(vmem_limit_bytes=SEND_LIMIT),
        name="send_rows",
    )(expert_ids.T, gate_values.T, tokens, out_grad)
    recv = lax.all_to_all(sent, "ep", split_axis=0, concat_axis=0, tiled=True)

    rows_x, rows_g = pl.pallas_call(
        functools.partial(unpack_kernel, quarters),
        in_specs=[whole(pltpu.SMEM), whole(pl.ANY)],
        out_specs=[whole()] * 2,
        out_shape=[jax.ShapeDtypeStruct((slots, width), BF16)] * 2,
        scratch_shapes=[pltpu.VMEM((rows, 2 * feat), BF16), pltpu.SemaphoreType.DMA((4,))],
        compiler_params=params,
        cost_estimate=pl.CostEstimate(flops=UNPACK_COST, bytes_accessed=0, transcendentals=0),
        name="unpack_rows",
    )(me, recv)
    near_downs = (down_weight[0], downs[0], downs[3])
    to_gate, to_up, *rest = pl.pallas_call(
        hidden_kernel,
        in_specs=[whole()] * 3 + [whole(pl.ANY)] * 7,
        out_specs=[whole()] * 13,
        out_shape=[jax.ShapeDtypeStruct((slots, hidden_units), F32)] * 2
        + [jax.ShapeDtypeStruct((hidden_units, feat), BF16)] * parts
        + [jax.ShapeDtypeStruct(x.shape, BF16) for x in (*ups, *near_downs)],
        scratch_shapes=[
            pltpu.VMEM((slots, 2 * hidden_units), F32),
            pltpu.VMEM((slots, hidden_units), BF16),
            pltpu.SemaphoreType.DMA((7,)),
        ],
        compiler_params=pltpu.CompilerParams(vmem_limit_bytes=HIDDEN_LIMIT),
        name="hidden_rows",
    )(rows_x, rows_g, gate_up_weight[0], *ups, *near_downs)
    blocks, held = rest[:parts], rest[parts:]
    down_grad = scatter_two_steps(blocks, parts)[None]

    back = pl.pallas_call(
        functools.partial(back_kernel, quarters),
        in_specs=[whole(pltpu.SMEM)] + [whole()] * 11 + [whole(pl.ANY)] * 2,
        out_specs=whole(pl.ANY),
        out_shape=jax.ShapeDtypeStruct((rows, feat), BF16),
        scratch_shapes=[
            pltpu.VMEM((slots, 2 * hidden_units), BF16),
            pltpu.VMEM((quarters, slots, feat), BF16),
            pltpu.VMEM((rows, feat), BF16),
        ]
        + [pltpu.VMEM(x.shape, BF16) for x in downs[1:3]]
        + [pltpu.SemaphoreType.DMA((4,)), pltpu.SemaphoreType.DMA((2,))],
        compiler_params=pltpu.CompilerParams(vmem_limit_bytes=BACK_LIMIT),
        cost_estimate=pl.CostEstimate(flops=COST, bytes_accessed=0, transcendentals=0),
        name="back_rows",
    )(me, to_gate, to_up, rows_g, gate_up_weight[0], *held, *downs[1:3])
    returned = lax.all_to_all(back, "ep", split_axis=0, concat_axis=0, tiled=True)
    token_grads = pl.pallas_call(
        functools.partial(combine_kernel, toks),
        in_specs=[whole(), whole()],
        out_specs=whole(),
        out_shape=jax.ShapeDtypeStruct((toks, width), BF16),
        compiler_params=params,
        name="combine_rows",
    )(pick, returned)
    return (token_grads, down_grad)


def solution(mesh):
    return jax.shard_map(
        per_device,
        mesh=mesh,
        in_specs=(
            P(("ep", "edp"), None),
            P(("ep", "edp"), None),
            P(("ep", "edp"), None),
            P(("ep", "edp"), None),
            P("ep", "edp", None),
            P("ep", None, "edp"),
        ),
        out_specs=(P(("ep", "edp"), None), P("ep", None, "edp")),
        check_vma=False,
    )
```

```python
import functools

import jax
import jax.numpy as jnp
from jax import lax
from jax.experimental import pallas as pl
from jax.experimental.pallas import tpu as pltpu
from jax.sharding import PartitionSpec as P

EPSILON = 1e-06
F32, BF16 = jnp.float32, jnp.bfloat16
NT = (((1,), (1,)), ((), ()))
TN = (((0,), (0,)), ((), ()))
VMEM_LIMIT = 16 * 1024 * 1024
BACK_LIMIT = 24 * 1024 * 1024
UNPACK_COST = 7 * 10**9
HIDDEN_LIMIT = 32 * 1024 * 1024
SEND_LIMIT = 56 * 1024 * 1024
COST = 30 * 10**9
LEFT_COST = 1 * 10**9
RIGHT_COST = 30 * 10**9
ADD_COST = 8 * 10**9


def whole(memory_space=pltpu.VMEM):
    return pl.BlockSpec(memory_space=memory_space)


def rebuild(value, top):
    scale = (top + EPSILON).astype(BF16).astype(F32)
    return ((value / scale).astype(BF16).astype(F32) * scale).astype(BF16)


def send_kernel(quarters, ids_ref, gate_ref, tok_ref, grad_ref, send_ref, pick_ref, stack):
    block = pl.program_id(0)
    rows = send_ref.shape[0]
    toks, width = tok_ref.shape
    lanes = quarters * toks
    feat = width // quarters

    @pl.when(block == 0)
    def _():
        for q in range(quarters):
            here = pl.ds(q * toks, toks)
            for g in range(feat // 128):
                cols = slice(q * feat + g * 128, q * feat + g * 128 + 128)
                value = tok_ref[:, cols].astype(F32)
                top = jnp.max(jnp.abs(value), axis=1, keepdims=True)
                stack[here, pl.ds(g * 128, 128)] = rebuild(value, top).astype(F32)
            grads = grad_ref[:, q * feat : q * feat + feat].astype(F32)
            stack[here, pl.ds(feat, feat)] = grads
            for g in range(feat // 128):
                top = jnp.max(jnp.abs(grads[:, g * 128 : g * 128 + 128]), axis=1, keepdims=True)
                stack[here, pl.ds(2 * feat + g * 128, 128)] = jnp.broadcast_to(top, (toks, 128))

    row = lax.broadcasted_iota(jnp.int32, (rows, lanes), 0) + block * rows
    lane = lax.broadcasted_iota(jnp.int32, (rows, lanes), 1)
    expert, slot, quarter = row >> 3, (row >> 2) & 1, row & 3
    ids = jnp.concatenate([ids_ref[...]] * quarters, axis=1)
    gates = jnp.concatenate([gate_ref[...]] * quarters, axis=1)
    named = jnp.zeros((rows, lanes), F32)
    weight = jnp.zeros((rows, lanes), F32)
    for k in range(ids_ref.shape[0]):
        hit = ids[k : k + 1, :] == expert
        named = jnp.where(hit, 1.0, named)
        weight = jnp.where(hit, gates[k : k + 1, :], weight)
    above = lax.broadcasted_iota(jnp.int32, (lanes, lanes), 0)
    below = lax.broadcasted_iota(jnp.int32, (lanes, lanes), 1)
    earlier = (above < below) & (above // toks == below // toks)
    rank = jnp.dot(named.astype(BF16), earlier.astype(BF16), preferred_element_type=F32)
    chosen = (named > 0.5) & (rank == slot.astype(F32)) & (lane // toks == quarter)
    pick = jnp.where(chosen, 1.0, 0.0).astype(BF16)
    pick_ref[...] = pick
    send_ref[:, :feat] = jnp.dot(pick, stack[:, :feat].astype(BF16), preferred_element_type=F32).astype(BF16)
    gate = jnp.sum(jnp.where(chosen, weight, 0.0), axis=1, keepdims=True)
    grads = jnp.dot(pick, stack[:, feat : 2 * feat].astype(BF16), preferred_element_type=F32) * gate
    top = jnp.dot(pick, stack[:, 2 * feat :].astype(BF16), preferred_element_type=F32) * gate
    send_ref[:, feat:] = rebuild(grads, top)


def order_matrix(rows, quarters):
    out = lax.broadcasted_iota(jnp.int32, (rows, rows), 0)
    src = lax.broadcasted_iota(jnp.int32, (rows, rows), 1)
    per = rows // quarters
    return ((out % per) * quarters + out // per == src).astype(BF16)


def start(copies, src, dst, sems):
    copies.append(pltpu.make_async_copy(src, dst, sems.at[len(copies)]))
    copies[-1].start()
    return copies[-1]


def unpack_kernel(quarters, me_ref, recv_ref, x_ref, g_ref, recv, sems):
    rows = 256
    per = rows // quarters
    feat = recv.shape[1] // 2
    started = []
    for b in range(recv.shape[0] // rows):
        here = pl.ds(b * rows, rows)
        start(started, recv_ref.at[here, :], recv.at[here, :], sems)
    order = order_matrix(rows, quarters)
    for b, copy in enumerate(started):
        copy.wait()
        got = jnp.dot(order, recv[b * rows : b * rows + rows, :], preferred_element_type=F32).astype(BF16)
        here = slice(b * per, b * per + per)
        for q in range(quarters):
            at = pl.multiple_of(lax.rem(q + quarters - me_ref[0], quarters) * feat, feat)
            x_ref[here, pl.ds(at, feat)] = got[q * per : q * per + per, :feat]
            g_ref[here, pl.ds(at, feat)] = got[q * per : q * per + per, feat:]


def fetch(refs, holds, sems):
    copies = [pltpu.make_async_copy(ref, hold, sems.at[i]) for i, (ref, hold) in enumerate(zip(refs, holds))]
    for copy in copies:
        copy.start()
    waited = set()

    def get(i):
        if i not in waited:
            waited.add(i)
            copies[i].wait()
        return holds[i]

    return get


def hidden_kernel(x_ref, g_ref, own_up, *refs):
    given, outs, (pre, hid_ref, sems) = refs[:7], refs[7:20], refs[20:]
    to_gate, to_up, blocks, holds = outs[0], outs[1], outs[2:6], outs[6:]
    get = fetch(given, holds, sems)
    feat = g_ref.shape[1] // len(blocks)
    hidden_units = hid_ref.shape[1]
    tile = 256
    row = 0
    for i in range(5):
        w = get(i - 1) if i else own_up
        rows = slice(row, row + w.shape[0])
        row += w.shape[0]
        for n in range(w.shape[1] // tile):
            cols = slice(n * tile, n * tile + tile)
            term = jnp.dot(x_ref[:, rows], w[:, cols], preferred_element_type=F32)
            pre[:, cols] = pre[:, cols] + term if i else term
    for n in range(hidden_units // tile):
        cols = slice(n * tile, n * tile + tile)
        gate = pre[:, cols]
        up = pre[:, hidden_units + n * tile : hidden_units + n * tile + tile]
        sig = jax.nn.sigmoid(gate)
        activ = gate * sig
        to_gate[:, cols] = up * sig * (1.0 + gate * (1.0 - sig))
        to_up[:, cols] = activ
        hid_ref[:, cols] = (activ * up).astype(BF16)
    for k, ref in enumerate(blocks):
        ref[...] = lax.dot_general(
            hid_ref[...], g_ref[:, k * feat : k * feat + feat], TN, preferred_element_type=F32
        ).astype(BF16)
    for i in range(4, len(holds)):
        get(i)


def back_kernel(quarters, me_ref, to_gate, to_up, g, *refs):
    ups, own, right, left, (far_a, far_b), refs = refs[:5], refs[5], refs[6], refs[7], refs[8:10], refs[10:]
    back_ref, gp_ref, hold, out, *holds, sems, far_sems = refs
    get = fetch((far_a, far_b), holds, far_sems)
    started = []
    hidden_units = to_gate.shape[1]
    feat = out.shape[1]
    half = hidden_units // 2

    def product(h, k, w):
        return lax.dot_general(g[:, k * feat : k * feat + feat], w, NT, preferred_element_type=F32)

    sums = []
    for h in range(2):
        cols = slice(h * half, h * half + half)
        sums.append(product(h, 0, own[cols, :]) + product(h, 1, right[cols, :]) + product(h, 3, left[cols, :]))
    for h in range(2):
        cols = slice(h * half, h * half + half)
        total = sums[h] + product(h, 2, get(h)[...])
        gp_ref[:, cols] = (total * to_gate[:, cols]).astype(BF16)
        gp_ref[:, hidden_units + h * half : hidden_units + h * half + half] = (total * to_up[:, cols]).astype(BF16)
    at = 0
    for w in ups:
        size = w.shape[0]
        hold[lax.rem(me_ref[0] + at // feat, quarters), :, at % feat : at % feat + size] = lax.dot_general(
            gp_ref[...], w[...], NT, preferred_element_type=F32
        ).astype(BF16)
        at += size
    rows = 256
    per = rows // quarters
    order = order_matrix(rows, quarters)
    copies = []
    for b in range(back_ref.shape[0] // rows):
        here = pl.ds(b * rows, rows)
        stacked = jnp.concatenate([hold[q, b * per : b * per + per, :] for q in range(quarters)], axis=0)
        out[here, :] = lax.dot_general(order, stacked, TN, preferred_element_type=F32).astype(BF16)
        copies.append(start(started, out.at[here, :], back_ref.at[here, :], sems))
    for copy in copies:
        copy.wait()


def combine_kernel(toks, pick_ref, ret_ref, out_ref):
    feat = ret_ref.shape[1]
    total = lax.dot_general(pick_ref[...], ret_ref[...], TN, preferred_element_type=F32)
    for q in range(out_ref.shape[1] // feat):
        out_ref[:, q * feat : q * feat + feat] = total[q * toks : q * toks + toks].astype(BF16)


def ring(size, step):
    return [(i, (i + step) % size) for i in range(size)]


def hand_on_kernel(first, block, block_out, going, sem):
    copy = pltpu.make_async_copy(block.at[pl.ds(first, going.shape[0]), :], going, sem)
    copy.start()
    copy.wait()


def hand_on(block, first, cost):
    half = jax.ShapeDtypeStruct((block.shape[0] // 2, block.shape[1]), block.dtype)
    return pl.pallas_call(
        functools.partial(hand_on_kernel, first),
        in_specs=[whole(pl.ANY)],
        out_specs=[whole(pl.ANY), whole()],
        out_shape=[jax.ShapeDtypeStruct(block.shape, block.dtype), half],
        input_output_aliases={0: 0},
        scratch_shapes=[pltpu.SemaphoreType.DMA],
        compiler_params=pltpu.CompilerParams(vmem_limit_bytes=VMEM_LIMIT),
        cost_estimate=pl.CostEstimate(flops=cost, bytes_accessed=0, transcendentals=0),
        name="hand_on",
    )(block)


def gather_two_steps(up, down, size):
    fwd, bwd = ring(size, 1), ring(size, -1)
    left_up, up_top = hand_on(lax.ppermute(up, "edp", fwd), 0, LEFT_COST)
    right_up, up_bottom = hand_on(lax.ppermute(up, "edp", bwd), up.shape[0] // 2, RIGHT_COST)
    left_down, right_down = lax.ppermute(down, "edp", fwd), lax.ppermute(down, "edp", bwd)
    half = down.shape[0] // 2
    far_up = [lax.ppermute(up_top, "edp", fwd), lax.ppermute(up_bottom, "edp", bwd)]
    far_down = [lax.ppermute(left_down[:half], "edp", fwd), lax.ppermute(right_down[half:], "edp", bwd)]
    return [right_up, *far_up, left_up], [right_down, *far_down, left_down]


def add_kernel(block, came, out):
    out[...] = (block[...].astype(F32) + came[...].astype(F32)).astype(BF16)


def scatter_two_steps(blocks, size):
    own, right, far, left = blocks
    came = lax.ppermute(far, "edp", ring(size, 1))
    right = pl.pallas_call(
        add_kernel,
        in_specs=[whole()] * 2,
        out_specs=whole(),
        out_shape=jax.ShapeDtypeStruct(right.shape, BF16),
        compiler_params=pltpu.CompilerParams(vmem_limit_bytes=VMEM_LIMIT),
        cost_estimate=pl.CostEstimate(flops=ADD_COST, bytes_accessed=0, transcendentals=0),
        name="add_far",
    )(right, came)
    from_left, from_right = lax.ppermute(right, "edp", ring(size, 1)), lax.ppermute(left, "edp", ring(size, -1))
    return (own.astype(F32) + from_left.astype(F32) + from_right.astype(F32)).astype(BF16)


def per_device(tokens, out_grad, expert_ids, gate_values, gate_up_weight, down_weight):
    experts, parts = lax.axis_size("ep"), lax.axis_size("edp")
    toks, width = tokens.shape
    hidden_units = down_weight.shape[1]
    quarters = 4
    feat = width // quarters
    slots = experts * 2
    rows = slots * quarters
    params = pltpu.CompilerParams(vmem_limit_bytes=VMEM_LIMIT)
    me = lax.axis_index("edp").astype(jnp.int32).reshape(1)

    ups, downs = gather_two_steps(gate_up_weight[0], down_weight[0], parts)

    tile = 512
    sent, pick = pl.pallas_call(
        functools.partial(send_kernel, quarters),
        grid=(rows // tile,),
        in_specs=[whole()] * 4,
        out_specs=[
            pl.BlockSpec((tile, 2 * feat), lambda b: (b, 0)),
            pl.BlockSpec((tile, quarters * toks), lambda b: (b, 0)),
        ],
        out_shape=[
            jax.ShapeDtypeStruct((rows, 2 * feat), BF16),
            jax.ShapeDtypeStruct((rows, quarters * toks), BF16),
        ],
        scratch_shapes=[pltpu.VMEM((quarters * toks, 3 * feat), F32)],
        compiler_params=pltpu.CompilerParams(vmem_limit_bytes=SEND_LIMIT),
        name="send_rows",
    )(expert_ids.T, gate_values.T, tokens, out_grad)
    recv = lax.all_to_all(sent, "ep", split_axis=0, concat_axis=0, tiled=True)

    rows_x, rows_g = pl.pallas_call(
        functools.partial(unpack_kernel, quarters),
        in_specs=[whole(pltpu.SMEM), whole(pl.ANY)],
        out_specs=[whole()] * 2,
        out_shape=[jax.ShapeDtypeStruct((slots, width), BF16)] * 2,
        scratch_shapes=[pltpu.VMEM((rows, 2 * feat), BF16), pltpu.SemaphoreType.DMA((4,))],
        compiler_params=params,
        cost_estimate=pl.CostEstimate(flops=UNPACK_COST, bytes_accessed=0, transcendentals=0),
        name="unpack_rows",
    )(me, recv)
    near_downs = (down_weight[0], downs[0], downs[3])
    to_gate, to_up, *rest = pl.pallas_call(
        hidden_kernel,
        in_specs=[whole()] * 3 + [whole(pl.ANY)] * 7,
        out_specs=[whole()] * 13,
        out_shape=[jax.ShapeDtypeStruct((slots, hidden_units), F32)] * 2
        + [jax.ShapeDtypeStruct((hidden_units, feat), BF16)] * parts
        + [jax.ShapeDtypeStruct(x.shape, BF16) for x in (*ups, *near_downs)],
        scratch_shapes=[
            pltpu.VMEM((slots, 2 * hidden_units), F32),
            pltpu.VMEM((slots, hidden_units), BF16),
            pltpu.SemaphoreType.DMA((7,)),
        ],
        compiler_params=pltpu.CompilerParams(vmem_limit_bytes=HIDDEN_LIMIT),
        name="hidden_rows",
    )(rows_x, rows_g, gate_up_weight[0], *ups, *near_downs)
    blocks, held = rest[:parts], rest[parts:]
    down_grad = scatter_two_steps(blocks, parts)[None]

    back = pl.pallas_call(
        functools.partial(back_kernel, quarters),
        in_specs=[whole(pltpu.SMEM)] + [whole()] * 11 + [whole(pl.ANY)] * 2,
        out_specs=whole(pl.ANY),
        out_shape=jax.ShapeDtypeStruct((rows, feat), BF16),
        scratch_shapes=[
            pltpu.VMEM((slots, 2 * hidden_units), BF16),
            pltpu.VMEM((quarters, slots, feat), BF16),
            pltpu.VMEM((rows, feat), BF16),
        ]
        + [pltpu.VMEM(x.shape, BF16) for x in downs[1:3]]
        + [pltpu.SemaphoreType.DMA((4,)), pltpu.SemaphoreType.DMA((2,))],
        compiler_params=pltpu.CompilerParams(vmem_limit_bytes=BACK_LIMIT),
        cost_estimate=pl.CostEstimate(flops=COST, bytes_accessed=0, transcendentals=0),
        name="back_rows",
    )(me, to_gate, to_up, rows_g, gate_up_weight[0], *held, *downs[1:3])
    returned = lax.all_to_all(back, "ep", split_axis=0, concat_axis=0, tiled=True)
    token_grads = pl.pallas_call(
        functools.partial(combine_kernel, toks),
        in_specs=[whole(), whole()],
        out_specs=whole(),
        out_shape=jax.ShapeDtypeStruct((toks, width), BF16),
        compiler_params=params,
        name="combine_rows",
    )(pick, returned)
    return (token_grads, down_grad)


def solution(mesh):
    return jax.shard_map(
        per_device,
        mesh=mesh,
        in_specs=(
            P(("ep", "edp"), None),
            P(("ep", "edp"), None),
            P(("ep", "edp"), None),
            P(("ep", "edp"), None),
            P("ep", "edp", None),
            P("ep", None, "edp"),
        ),
        out_specs=(P(("ep", "edp"), None), P("ep", None, "edp")),
        check_vma=False,
    )
```
